32 devices in a mesh: dp: 16 (over z, y, x), expert: 2 (over core).
Axes of the slice: x: 2, y: 2, z: 4, core: 2. Of those that a mesh axis runs over, the one named last changes fastest.
Arguments:
- inputs: bfloat16 [32768, 512], P(('dp', 'expert')), may hold values from -6 to 6
- cotangent: bfloat16 [32768, 512], P(('dp', 'expert')), may hold values from -6 to 6
- lengths: int32 [16, 2, 4], P('dp'), may hold values from 0 to 1024, as said below
- routes: int32 [16, 2, 1024, 2], P('dp'), may hold values from 0 to 7, all different within a row; in each aligned block of 1024 rows (0 to 1023, 1024 to 2047, ..., all dimensions but the last counted through in order) at most 512 rows name the same one
- first_gain: bfloat16 [512], replicated, may hold values from 0.5 to 1.5
- first_bias: bfloat16 [512], replicated, may hold values from -1.1953125 to 1.1953125
- router_weight: bfloat16 [512, 8], replicated, may hold values from -0.25 to 0.25
- key_weight: bfloat16 [512, 64], replicated, may hold values from -0.25 to 0.25
- value_weight: bfloat16 [512, 64], replicated, may hold values from -0.25 to 0.25
- query_weight: bfloat16 [8, 512, 64], P('expert'), may hold values from -0.25 to 0.25
- output_weight: bfloat16 [8, 64, 512], P('expert'), may hold values from -3 to 3
- second_gain: bfloat16 [512], replicated, may hold values from 0.5 to 1.5
- second_bias: bfloat16 [512], replicated, may hold values from -1.1953125 to 1.1953125
- hidden_weight: bfloat16 [512, 2048], replicated, may hold values from -0.25 to 0.25
- hidden_bias: bfloat16 [2048], replicated, may hold values from -1.1953125 to 1.1953125
- return_weight: bfloat16 [2048, 512], replicated, may hold values from -0.25 to 0.25
- return_bias: bfloat16 [512], replicated, may hold values from -1.1953125 to 1.1953125
Outputs:
- layer_out: float32 [32768, 512], P(('dp', 'expert'))
- input_grad: float32 [32768, 512], P(('dp', 'expert'))
- first_gain_grad: float32 [512], replicated
- first_bias_grad: float32 [512], replicated
- router_grad: float32 [512, 8], replicated
- key_grad: float32 [512, 64], replicated
- value_grad: float32 [512, 64], replicated
- query_grad: float32 [8, 512, 64], P('expert')
- output_grad: float32 [8, 64, 512], P('expert')
- second_gain_grad: float32 [512], replicated
- second_bias_grad: float32 [512], replicated
- hidden_grad: float32 [512, 2048], replicated
- hidden_bias_grad: float32 [2048], replicated
- return_grad: float32 [2048, 512], replicated
- return_bias_grad: float32 [512], replicated
The draws below stay inside these ranges and needn't reach their ends.
Inputs may be any that keep to these rules, and one draw needn't show every extreme that they name: Slots with length 0 are unused; a device's lengths sum to at most 1024 and the rest of its rows are padding; devices hold different numbers of sentences; in every draw some device holds a single sentence of 1024 rows. Each token names two different experts; the rows of one device name no expert more than 512 times, and in every draw some device names some expert exactly 512 times. routes[i, j] belongs to the device at index i of dp and j of expert.
All inputs are finite; a program needn't handle non-finite values.
Results may differ from the reference program's by a relative error of at most 0.012.
Values may be sent and summed in bfloat16 or wider, within the bound.
No kernel may reach another device: no remote copies, remote signals or barrier semaphores. Data moves between devices by JAX's collectives and lax.ppermute only.
A program may use at most 192 MiB of HBM per device.

```python
import math
import jax
import jax.numpy as jnp
import numpy as np
from jax import lax

D = 512
FF = 2048
HD = 64
EXPERTS = 8
TOP = 2
SLOTS = 4
TOK_DEV = 1024
CAP = 512
TOKENS = 32768
N_DP = 16
N_EXPERT = 2


def draw_lengths(key, part):
    key = jax.random.fold_in(key, 7)
    key_pad, key_cut, key_num, key_full = jax.random.split(key, 4)
    device_count = N_DP * N_EXPERT
    padding = jax.random.randint(key_pad, (device_count, 1), 0, TOK_DEV // 4 + 1)
    filled = TOK_DEV - padding
    sentences = jax.random.randint(key_num, (device_count, 1), 1, SLOTS + 1)
    borders = jax.random.randint(key_cut, (device_count, SLOTS - 1), 0, TOK_DEV + 1)
    borders = jnp.sort(jnp.minimum(borders, filled), axis=1)
    column = jnp.arange(SLOTS - 1)[None, :]
    borders = jnp.where(column < sentences - 1, borders, filled)
    bounds = jnp.concatenate([jnp.zeros((device_count, 1), jnp.int32), borders.astype(jnp.int32), filled.astype(jnp.int32)], axis=1)
    pieces = bounds[:, 1:] - bounds[:, :-1]
    chosen = jax.random.randint(key_full, (), 0, device_count)
    single = jnp.zeros((SLOTS,), jnp.int32).at[0].set(TOK_DEV)
    pieces = jnp.where((jnp.arange(device_count) == chosen)[:, None], single[None, :], pieces)
    return pieces.reshape(N_DP, N_EXPERT, SLOTS).astype(jnp.int32)


def steps_of(stream_key, shape, cuts, smallest, largest):
    loudness = 1.0
    for position, parts in cuts:
        heights = jax.random.uniform(jax.random.fold_in(jax.random.fold_in(stream_key, 6), position), (parts,), jnp.float32, smallest / len(cuts), largest / len(cuts))
        loudness = loudness * jnp.repeat(jnp.exp(heights), shape[position] // parts).reshape((-1,) + (1,) * (len(shape) - 1 - position))
    return loudness


def shared_out(rng, own, number, rows, amount, top, bound, lean):
    ranking = jax.random.permutation(rng, amount)
    packed, ordinary = load_shares(amount, rows * top, bound, lean, True), load_shares(amount, rows * top, bound, lean, False)
    places = jnp.arange(amount)

    def named(tallies, offset_by):
        used = int((tallies > 0).sum())
        fixed = max(1, used // 4)
        moved = fixed + (places - fixed + offset_by * (used - fixed)) % max(1, amount - fixed)
        return jnp.zeros((amount,), jnp.int32).at[ranking[jnp.where(places < fixed, places, moved)]].set(jnp.asarray(tallies, jnp.int32))

    tallies = jnp.where(number % 4 == 0, named(packed, number // 4), named(ordinary, number - number // 4 - 1))
    mixed = jax.random.permutation(jax.random.fold_in(own, 3), amount)
    donor, sink = mixed[0:amount // 2 * 2:2], mixed[1:amount // 2 * 2:2]
    slack = jnp.minimum(tallies[donor] - 1, bound - tallies[sink]) // 2
    slack = jnp.where((donor == ranking[0]) | (sink == ranking[0]) | (tallies[sink] == 0), 0, jnp.maximum(slack, 0))
    moved = jax.random.randint(jax.random.fold_in(own, 4), (amount // 2,), 0, 1 << 20) % (slack + 1)
    tallies = tallies.at[donor].add(-moved).at[sink].add(moved)
    items = jnp.searchsorted(jnp.cumsum(tallies), jnp.arange(rows * top), side="right").astype(jnp.int32)
    table = items.reshape(top, rows).T
    table = table[jax.random.permutation(jax.random.fold_in(own, 1), rows)]
    offset_by = jax.random.randint(jax.random.fold_in(own, 2), (rows, 1), 0, top)
    return jnp.take_along_axis(table, (jnp.arange(top)[None, :] + offset_by) % top, axis=1)


def load_shares(number_of, total, most, lean, full):
    weights = [(1 << 20) // math.isqrt(rank ** lean) + 1 for rank in range(1, number_of + 1)]
    largest = most if full else min(most, max(-(-total // number_of), total * weights[0] // sum(weights)))
    least = 1 if total - largest >= number_of - 1 else 0
    given, surplus = [largest] + [least] * (number_of - 1), total - largest - least * (number_of - 1)
    while surplus > 0:
        movable = [i for i in range(1, number_of) if given[i] < largest] or [i for i in range(1, number_of) if given[i] < most]
        whole, budget = sum([weights[i] for i in movable]), surplus
        for i in movable:
            more = min(most - given[i], max(1, budget * weights[i] // whole), surplus)
            given[i] = given[i] + more
            surplus = surplus - more
    return np.array(given)


def noise(rng, dims, deviation, most, cuts=(), held_as=jnp.bfloat16):
    gain = steps_of(rng, dims, cuts, -0.22, 0.18) if cuts else 1.0
    values = jax.random.normal(rng, dims, jnp.float32) * deviation * gain
    return jnp.minimum(jnp.maximum(values, -most), most).astype(held_as)


def setup_inputs(seed: int = 0) -> dict:
    key_of = jax.random.split(jax.random.key(seed), 18)
    inputs = noise(key_of[0], (TOKENS, D), 1.0, 6.0, ((0, 32),))
    cotangent = noise(key_of[1], (TOKENS, D), 1.0, 6.0, ((0, 32),))
    lengths = draw_lengths(jax.random.fold_in(key_of[17], 71), 0)
    routes_keys = jax.random.split(jax.random.fold_in(key_of[3], 1), N_DP * N_EXPERT * TOK_DEV // TOK_DEV)
    routes_turns = jax.random.permutation(jax.random.fold_in(key_of[3], 3), N_DP * N_EXPERT * TOK_DEV // TOK_DEV)
    routes = jax.vmap(lambda own, number: shared_out(jax.random.fold_in(key_of[3], 2), own, number, TOK_DEV, EXPERTS, TOP, CAP, 1))(routes_keys, routes_turns).reshape((N_DP, N_EXPERT, TOK_DEV, TOP))
    first_gain = jnp.clip(1.0 + 0.1 * jax.random.normal(key_of[4], (D,), jnp.float32), 0.5, 1.5).astype(jnp.bfloat16)
    first_bias = noise(key_of[5], (D,), 0.2, 1.1953125)
    router_weight = noise(key_of[6], (D, EXPERTS), D ** -0.5, 0.25)
    key_weight = noise(key_of[7], (D, HD), D ** -0.5, 0.25)
    value_weight = noise(key_of[8], (D, HD), D ** -0.5, 0.25)
    query_weight = noise(key_of[9], (EXPERTS, D, HD), D ** -0.5, 0.25, ((0, 2),))
    output_weight = noise(key_of[10], (EXPERTS, HD, D), 0.5, 3.0, ((0, 2),))
    second_gain = jnp.clip(1.0 + 0.1 * jax.random.normal(key_of[11], (D,), jnp.float32), 0.5, 1.5).astype(jnp.bfloat16)
    second_bias = noise(key_of[12], (D,), 0.2, 1.1953125)
    hidden_weight = noise(key_of[13], (D, FF), D ** -0.5, 0.25)
    hidden_bias = noise(key_of[14], (FF,), 0.2, 1.1953125)
    return_weight = noise(key_of[15], (FF, D), (FF // 4) ** -0.5, 0.25)
    return_bias = noise(key_of[16], (D,), 0.2, 1.1953125)
    return dict(inputs=inputs, cotangent=cotangent, lengths=lengths, routes=routes, first_gain=first_gain, first_bias=first_bias, router_weight=router_weight, key_weight=key_weight, value_weight=value_weight, query_weight=query_weight, output_weight=output_weight, second_gain=second_gain, second_bias=second_bias, hidden_weight=hidden_weight, hidden_bias=hidden_bias, return_weight=return_weight, return_bias=return_bias)


@jax.custom_vjp
def low(v):
    return lax.optimization_barrier(v.astype(jnp.bfloat16)).astype(jnp.float32)

@jax.custom_vjp
def low_back(v):
    return v

def low_keep(v):
    return (low(v), None)

def low_pass(kept, grad):
    return (grad,)

def back_keep(v):
    return (v, None)

def back_low(kept, grad):
    return (low(grad),)
low.defvjp(low_keep, low_pass)
low_back.defvjp(back_keep, back_low)

def matmul(left_op, right_op):
    return jnp.dot(left_op, right_op, precision=lax.Precision.HIGHEST)

def layer_norm(values, gain_vec, offset):
    row_mean = lax.optimization_barrier(jnp.mean(values, axis=-1, keepdims=True))
    centred = values - row_mean
    row_var = lax.optimization_barrier(jnp.mean(centred * centred, axis=-1, keepdims=True))
    return centred * lax.rsqrt(row_var + 1e-05) * gain_vec + offset

def segment_ids(spans, tok_count):
    bounds = jnp.cumsum(spans)
    places = jnp.arange(tok_count, dtype=jnp.int32)
    return lax.optimization_barrier(jnp.sum((places[:, None] >= bounds[None, :]).astype(jnp.int32), axis=1))

def select_expert(stacked, chosen, experts):
    picked = chosen[:, None] == jnp.arange(experts, dtype=jnp.int32)[None, :]
    return lax.optimization_barrier(jnp.sum(jnp.where(picked[:, :, None], stacked, 0.0), axis=1))

def encoder_layer(params, inputs, segment, routing):
    first_gain, first_bias, router_weight, key_weight, value_weight, query_weight, output_weight, second_gain, second_bias, hidden_weight, hidden_bias, return_weight, return_bias = params
    tok_count = inputs.shape[0]
    experts = query_weight.shape[0]
    valid_rows = (segment < SLOTS).astype(inputs.dtype)[:, None]
    normed = low(layer_norm(inputs, first_gain, first_bias))
    key_rows = low_back(low(matmul(normed, key_weight)))
    value_rows = low_back(low(matmul(normed, value_weight)))
    gate_values = jax.nn.softmax(jnp.take_along_axis(matmul(normed, router_weight), routing, axis=1), axis=1)
    same_sentence = segment[:, None] == segment[None, :]
    query_flat = jnp.transpose(query_weight, (1, 0, 2)).reshape(D, experts * HD)
    branch = jnp.zeros_like(inputs)
    for member in range(TOP):
        chosen = routing[:, member]
        routed = low_back(normed)
        query_all = matmul(routed, query_flat).reshape(tok_count, experts, HD)
        queries = low_back(low(select_expert(query_all, chosen, experts)))
        scores = low_back(matmul(queries, key_rows.T) * HD ** (-0.5))
        softmaxed = low(jax.nn.softmax(jnp.where(same_sentence, scores, -1e+30), axis=1))
        attended = low_back(low(matmul(softmaxed, value_rows)))
        outs_all = jnp.einsum('th,ehd->ted', attended, output_weight, precision=lax.Precision.HIGHEST)
        expert_out = low_back(low(select_expert(outs_all, chosen, experts)))
        branch = branch + gate_values[:, member:member + 1] * expert_out
    middle = inputs + valid_rows * branch
    hidden_in = low(layer_norm(middle, second_gain, second_bias))
    before_act = low_back(matmul(hidden_in, hidden_weight) + hidden_bias)
    activated = low(jax.nn.gelu(before_act))
    feed_out = low_back(matmul(activated, return_weight) + return_bias)
    return middle + valid_rows * feed_out

def reference(inputs, cotangent, lengths, routes, first_gain, first_bias, router_weight, key_weight, value_weight, query_weight, output_weight, second_gain, second_bias, hidden_weight, hidden_bias, return_weight, return_bias):
    device_count = N_DP * N_EXPERT
    params = tuple((weight.astype(jnp.float32) for weight in (first_gain, first_bias, router_weight, key_weight, value_weight, query_weight, output_weight, second_gain, second_bias, hidden_weight, hidden_bias, return_weight, return_bias)))
    segments_all = jax.vmap(lambda spans: segment_ids(spans, TOK_DEV))(lengths.reshape(device_count, SLOTS))
    routing_all = routes.reshape(device_count, TOK_DEV, TOP)
    blocks = inputs.astype(jnp.float32).reshape(device_count, TOK_DEV, D)
    layer_saved = jax.checkpoint(encoder_layer)

    def forward(weights, stacked):

        def step(carry, item):
            return (carry, layer_saved(weights, item[0], item[1], item[2]))
        return lax.scan(step, (), (stacked, segments_all, routing_all))[1]
    outputs, pullback = jax.vjp(forward, params, blocks)
    weight_grads, input_grads = pullback(cotangent.astype(jnp.float32).reshape(device_count, TOK_DEV, D))
    return (outputs.reshape(TOKENS, D), input_grads.reshape(TOKENS, D), weight_grads[0], weight_grads[1], weight_grads[2], weight_grads[3], weight_grads[4], weight_grads[5], weight_grads[6], weight_grads[7], weight_grads[8], weight_grads[9], weight_grads[10], weight_grads[11], weight_grads[12])
```

```python
import jax
import jax.numpy as jnp
from jax import lax
from jax.sharding import PartitionSpec as P

AXES = ("dp", "expert")


def norm_parts(values):
    row_mean = jnp.mean(values, axis=-1, keepdims=True)
    centred = values - row_mean
    inv_dev = lax.rsqrt(jnp.mean(centred * centred, axis=-1, keepdims=True) + 1e-05)
    return centred * inv_dev, inv_dev


def norm_back(d_out, unit, inv_dev, gain_vec):
    weighted = d_out * gain_vec
    mean_w = jnp.mean(weighted, axis=-1, keepdims=True)
    mean_wn = jnp.mean(weighted * unit, axis=-1, keepdims=True)
    return inv_dev * (weighted - mean_w - unit * mean_wn)


def segment_ids(spans, tok_count):
    bounds = jnp.cumsum(spans)
    places = jnp.arange(tok_count, dtype=jnp.int32)
    return jnp.sum((places[:, None] >= bounds[None, :]).astype(jnp.int32), axis=1)


def dot_nn(left_op, right_op):
    return jnp.dot(left_op, right_op, preferred_element_type=jnp.float32)


def dot_tn(left_op, right_op):
    return lax.dot_general(
        left_op, right_op, (((0,), (0,)), ((), ())), preferred_element_type=jnp.float32
    )


def dot_nt(left_op, right_op):
    return lax.dot_general(
        left_op, right_op, (((1,), (1,)), ((), ())), preferred_element_type=jnp.float32
    )


def low(values):
    return values.astype(jnp.bfloat16)


def step_bits(n_dp):
    count = n_dp.bit_length() - 1
    first = list(range(count))
    second = []
    for at in range(0, count, 2):
        second += first[at : at + 2][::-1]
    return first, second


def pairs_of(n_dp, step):
    orders = step_bits(n_dp)
    pairs = []
    for chip in range(n_dp):
        for core in range(2):
            pairs.append((chip * 2 + core, (chip ^ (1 << orders[core][step])) * 2 + core))
    return pairs


def core_pairs(n_dp):
    return [(at, at ^ 1) for at in range(2 * n_dp)]


def my_bit(step, n_dp):
    orders = step_bits(n_dp)
    chip, core = lax.axis_index("dp"), lax.axis_index("expert")
    return jnp.where(core == 0, (chip >> orders[0][step]) & 1, (chip >> orders[1][step]) & 1)


def half_of(values, which):
    pair = values.reshape((2, values.shape[0] // 2) + values.shape[1:])
    return lax.dynamic_index_in_dim(pair, which, 0, keepdims=False)


def joined(mine, other, bit):
    pair = jnp.where(bit == 0, jnp.stack([mine, other]), jnp.stack([other, mine]))
    return pair.reshape((2 * mine.shape[0],) + mine.shape[1:])


def add_low(left_op, right_op):
    return low(left_op.astype(jnp.float32) + right_op.astype(jnp.float32))


def reduce_chips(part, n_dp):
    steps = n_dp.bit_length() - 1
    for step in range(steps):
        bit = my_bit(step, n_dp)
        arrived = lax.ppermute(half_of(part, 1 - bit), AXES, pairs_of(n_dp, step))
        part = add_low(half_of(part, bit), arrived)
    for step in reversed(range(steps)):
        bit = my_bit(step, n_dp)
        part = joined(part, lax.ppermute(part, AXES, pairs_of(n_dp, step)), bit)
    return part


def local(
    inputs,
    cotangent,
    lengths,
    routes,
    first_gain,
    first_bias,
    router_weight,
    key_weight,
    value_weight,
    query_weight,
    output_weight,
    second_gain,
    second_bias,
    hidden_weight,
    hidden_bias,
    return_weight,
    return_bias,
):
    tok_count, width = inputs.shape
    n_dp = lax.axis_size("dp")
    core = lax.axis_index("expert")
    own, _, head = query_weight.shape
    experts = own * lax.axis_size("expert")
    scale = head ** (-0.5)
    wide = jnp.float32

    own_q = jnp.transpose(query_weight, (1, 0, 2)).reshape(width, own * head).T
    own_o = output_weight.reshape(own * head, width)
    mine = jnp.concatenate([own_q, own_o], axis=1)
    both = joined(mine, lax.ppermute(mine, AXES, core_pairs(n_dp)), core)
    wq, wo = both[:, :width], both[:, width:]

    spans = lax.dynamic_index_in_dim(lengths[0], core, 0, keepdims=False)
    segment = segment_ids(spans, tok_count)
    routing = lax.dynamic_index_in_dim(routes[0], core, 0, keepdims=False)
    valid = (segment < lengths.shape[2]).astype(wide)[:, None]
    same = segment[:, None] == segment[None, :]
    gain_one, gain_two = first_gain.astype(wide), second_gain.astype(wide)

    x_wide = inputs.astype(wide)
    unit_one, inv_one = norm_parts(x_wide)
    normed = low(unit_one * gain_one + first_bias.astype(wide))
    kv_weight = jnp.concatenate([key_weight, value_weight], axis=1)
    key_value = low(dot_nn(normed, kv_weight))
    keys, values = key_value[:, :head], key_value[:, head:]
    logits = dot_nn(normed, router_weight)
    q_all = low(dot_nt(normed, wq)).reshape(tok_count, experts, head)
    hits = [
        (routing[:, m : m + 1] == jnp.arange(experts, dtype=jnp.int32)[None, :]).astype(wide)
        for m in range(2)
    ]
    chosen = [jnp.sum(hit * logits, axis=1, keepdims=True) for hit in hits]
    top = jnp.maximum(chosen[0], chosen[1])
    powers = [jnp.exp(c - top) for c in chosen]
    gates = [p / (powers[0] + powers[1]) for p in powers]

    queries, weights, attended = [], [], []
    placed = jnp.zeros((tok_count, experts, head), wide)
    for m in range(2):
        q_m = low(jnp.sum(hits[m][:, :, None] * q_all.astype(wide), axis=1))
        scores = jnp.where(same, dot_nt(q_m, keys) * scale, -1e30)
        exps = jnp.exp(scores - jnp.max(scores, axis=1, keepdims=True))
        probs = exps / jnp.sum(exps, axis=1, keepdims=True)
        att = dot_nn(low(probs), values)
        queries.append(q_m)
        weights.append(low(probs))
        attended.append(att)
        placed = placed + hits[m][:, :, None] * (gates[m] * att)[:, None, :]
    placed = low(placed.reshape(tok_count, experts * head))
    middle = x_wide + valid * dot_nn(placed, wo)

    unit_two, inv_two = norm_parts(middle)
    hidden_in = low(unit_two * gain_two + second_bias.astype(wide))
    before = dot_nn(hidden_in, hidden_weight) + hidden_bias.astype(wide)
    activated, gelu_pull = jax.vjp(jax.nn.gelu, before)
    activated = low(activated)
    d_out = cotangent.astype(wide)
    d_feed = low(d_out * valid)
    return_grad = dot_tn(activated, d_feed)
    d_before = low(gelu_pull(dot_nt(d_feed, return_weight))[0])
    hidden_grad = dot_tn(d_before, hidden_in)
    return_bias_grad = jnp.sum(d_feed.astype(wide), axis=0)
    hidden_bias_grad = jnp.sum(d_before.astype(wide), axis=0)

    feed_grads = low(jnp.concatenate([return_grad, hidden_grad], axis=1))
    arrived = lax.ppermute(half_of(feed_grads, 1 - core), AXES, core_pairs(n_dp))
    feed_part = reduce_chips(add_low(half_of(feed_grads, core), arrived), n_dp)

    layer_out = middle + valid * (dot_nn(activated, return_weight) + return_bias.astype(wide))
    d_hidden = dot_nt(d_before, hidden_weight)
    second_gain_grad = jnp.sum(d_hidden * unit_two, axis=0)
    second_bias_grad = jnp.sum(d_hidden, axis=0)
    d_middle = d_out + norm_back(d_hidden, unit_two, inv_two, gain_two)
    d_branch = d_middle * valid
    d_low = low(d_branch)
    output_grad = dot_tn(placed, d_low)
    d_all = dot_nt(d_low, wo).reshape(tok_count, experts, head)
    d_keys = jnp.zeros((tok_count, head), wide)
    d_values = jnp.zeros((tok_count, head), wide)
    d_placed = jnp.zeros((tok_count, experts, head), wide)
    d_gates = []
    for m in range(2):
        d_raw = jnp.sum(hits[m][:, :, None] * d_all, axis=1)
        d_gates.append(jnp.sum(d_raw * attended[m], axis=1, keepdims=True))
        d_att = low(gates[m] * d_raw)
        inner = jnp.sum(d_att.astype(wide) * attended[m], axis=1, keepdims=True)
        d_scores = low(weights[m].astype(wide) * (dot_nt(d_att, values) - inner))
        d_q = dot_nn(d_scores, keys) * scale
        d_keys = d_keys + dot_tn(d_scores, queries[m]) * scale
        d_values = d_values + dot_tn(weights[m], d_att)
        d_placed = d_placed + hits[m][:, :, None] * d_q[:, None, :]
    d_placed = low(d_placed.reshape(tok_count, experts * head))
    mean_gate = gates[0] * d_gates[0] + gates[1] * d_gates[1]
    d_logits = sum(hits[m] * (gates[m] * (d_gates[m] - mean_gate)) for m in range(2))
    d_kv = low(jnp.concatenate([d_keys, d_values], axis=1))
    d_logits_high = low(d_logits)
    d_logits_rest = low(d_logits - d_logits_high.astype(wide))
    d_router = jnp.concatenate([d_logits_high, d_logits_rest], axis=1)

    query_grad = dot_tn(d_placed, normed)
    kv_grad = dot_tn(d_kv, normed)
    router_grad = dot_tn(d_router, normed)
    router_grad = router_grad[:experts] + router_grad[experts:]
    d_normed = (
        dot_nn(d_placed, wq)
        + dot_nt(d_kv, kv_weight)
        + dot_nt(d_router, jnp.concatenate([router_weight, router_weight], axis=1))
    )
    first_gain_grad = jnp.sum(d_normed * unit_one, axis=0)
    first_bias_grad = jnp.sum(d_normed, axis=0)
    input_grad = d_middle + norm_back(d_normed, unit_one, inv_one, gain_one)

    vectors = jnp.concatenate(
        [
            first_gain_grad,
            first_bias_grad,
            second_gain_grad,
            second_bias_grad,
            return_bias_grad,
            hidden_bias_grad,
        ]
    ).reshape(-1, width)
    shared = jnp.concatenate([kv_grad, router_grad, vectors], axis=0)
    unit = 16 * n_dp
    shared_rows = shared.shape[0]
    half_rows = own * head
    total = 2 * half_rows + shared_rows // 2
    total = -(-total // unit) * unit
    shared_half = total - 2 * half_rows
    shared = jnp.pad(shared, ((0, 2 * shared_half - shared_rows), (0, 0)))

    def for_core(which):
        return low(
            jnp.concatenate(
                [half_of(query_grad, which), half_of(output_grad, which), half_of(shared, which)],
                axis=0,
            )
        )

    arrived = lax.ppermute(for_core(1 - core), AXES, core_pairs(n_dp))
    rest = reduce_chips(add_low(for_core(core), arrived), n_dp)
    shared = joined(
        rest[2 * half_rows :],
        lax.ppermute(rest[2 * half_rows :], AXES, core_pairs(n_dp)),
        core,
    ).astype(wide)
    query_grad = jnp.transpose(rest[:half_rows].reshape(own, head, width), (0, 2, 1)).astype(wide)
    output_grad = rest[half_rows : 2 * half_rows].reshape(own, head, width).astype(wide)
    kv_grad = shared[: 2 * head].T
    router_grad = shared[2 * head : 2 * head + experts].T
    vectors = shared[2 * head + experts : shared_rows]

    feed_all = joined(feed_part, lax.ppermute(feed_part, AXES, core_pairs(n_dp)), core)
    return_grad = feed_all[:, :width].astype(wide)
    hidden_grad = feed_all[:, width:].T.astype(wide)
    return (
        layer_out,
        input_grad,
        vectors[0],
        vectors[1],
        router_grad,
        kv_grad[:, :head],
        kv_grad[:, head:],
        query_grad,
        output_grad,
        vectors[2],
        vectors[3],
        hidden_grad,
        vectors[5:].reshape(-1),
        return_grad,
        vectors[4],
    )


def solution(mesh):
    rows = P(AXES, None)
    cut = P("expert", None, None)
    in_specs = (
        (rows, rows, P("dp", None, None), P("dp", None, None, None))
        + (P(),) * 5
        + (cut, cut)
        + (P(),) * 6
    )
    out_specs = (rows, rows) + (P(),) * 5 + (cut, cut) + (P(),) * 6
    return jax.shard_map(local, mesh=mesh, in_specs=in_specs, out_specs=out_specs, check_vma=False)
```

```python
import functools

import jax
import jax.numpy as jnp
from jax import lax
from jax.experimental import pallas as pl
from jax.experimental.pallas import tpu as pltpu
from jax.sharding import PartitionSpec as P

AXES = ("dp", "expert")
WIDE = jnp.float32
LOW = jnp.bfloat16
EPS = 1e-05
MASKED = -1e30
ROWS = 256
CURVE = 0.7978845608028654
CUBIC = 0.044715
VMEM_LIMIT = 20 * 1024 * 1024


def low(values):
    return values.astype(LOW)


def wide(values):
    return values.astype(WIDE)


def dot_nn(left_op, right_op):
    return lax.dot_general(
        left_op, right_op, (((1,), (0,)), ((), ())), preferred_element_type=WIDE
    )


def dot_tn(left_op, right_op):
    return lax.dot_general(
        left_op, right_op, (((0,), (0,)), ((), ())), preferred_element_type=WIDE
    )


def dot_nt(left_op, right_op):
    return lax.dot_general(
        left_op, right_op, (((1,), (1,)), ((), ())), preferred_element_type=WIDE
    )


def norm_parts(values):
    row_mean = jnp.mean(values, axis=-1, keepdims=True)
    centred = values - row_mean
    inv_dev = lax.rsqrt(jnp.mean(centred * centred, axis=-1, keepdims=True) + EPS)
    return centred * inv_dev, inv_dev


def norm_back(d_out, unit, inv_dev, gain_vec):
    weighted = d_out * gain_vec
    mean_w = jnp.mean(weighted, axis=-1, keepdims=True)
    mean_wn = jnp.mean(weighted * unit, axis=-1, keepdims=True)
    return inv_dev * (weighted - mean_w - unit * mean_wn)


def bounds_of(lengths, place):
    ends, end = [], 0
    for slot in range(lengths.shape[1]):
        end = end + lengths[place[0], slot]
        ends.append(end)
    return ends


def segment_of(places, ends):
    return sum((places >= end).astype(jnp.int32) for end in ends)


def held(shape, dtype):
    return pltpu.VMEM(shape, dtype)


def there(shape, dtype):
    return jax.ShapeDtypeStruct(shape, dtype)


ANYWHERE = pl.BlockSpec(memory_space=pl.ANY)
INSIDE = pl.BlockSpec(memory_space=pltpu.VMEM)


def call(
    kernel, name, scalars, operands, out_shape, scratch=(), after=(), far=(), far_out=0, cost=1.0,
    loose=(),
):
    scalars = tuple(scalars)
    operands = tuple(pltpu.with_memory_space_constraint(v, pltpu.VMEM) for v in operands)
    operands += tuple(pltpu.with_memory_space_constraint(v, pltpu.HBM) for v in loose)
    far = tuple(pltpu.with_memory_space_constraint(v, pltpu.HBM) for v in far)
    count, waits = len(scalars) + len(operands) + len(far), len(after)

    def run(*refs):
        kernel(*refs[:count], *refs[count + waits :])

    single = not isinstance(out_shape, (list, tuple))
    outs = [out_shape] if single else list(out_shape)
    result = pl.pallas_call(
        run,
        in_specs=[pl.BlockSpec(memory_space=pltpu.SMEM)] * len(scalars)
        + [INSIDE] * len(operands)
        + [ANYWHERE] * (len(far) + waits),
        out_specs=[INSIDE] * (len(outs) - far_out) + [ANYWHERE] * far_out,
        out_shape=outs,
        scratch_shapes=list(scratch),
        compiler_params=pltpu.CompilerParams(vmem_limit_bytes=VMEM_LIMIT),
        cost_estimate=pl.CostEstimate(
            flops=int(cost * 1e9), bytes_accessed=1024, transcendentals=0
        ),
        name=name,
    )(*scalars, *operands, *far, *after)
    return result[0] if single else result


FIRST_GAIN, FIRST_BIAS, SECOND_GAIN, SECOND_BIAS, RETURN_BIAS, HIDDEN_BIAS = range(6)


def open_kernel(
    place, lengths, first_gain, first_bias, second_gain, second_bias, return_bias, hidden_bias,
    key_w, value_w, router_w, x_far, q_far, o_far,
    normed, vecs, keys_ext, key_t, value_n, values_ext, logits, x, q_own, o_own, sems,
):
    spans = [slice(at, at + ROWS) for at in range(0, x.shape[0], ROWS)]
    copies = [
        pltpu.make_async_copy(x_far.at[here, :], x.at[here, :], sems.at[j])
        for j, here in enumerate(spans)
    ]
    copies.append(pltpu.make_async_copy(q_far, q_own, sems.at[len(spans)]))
    copies.append(pltpu.make_async_copy(o_far, o_own, sems.at[len(spans) + 1]))
    for copy in copies:
        copy.start()
    ends = bounds_of(lengths, place)
    head = key_w.shape[0]
    width = x.shape[1]
    vecs[...] = jnp.zeros_like(vecs)
    for j, vec in enumerate((first_gain, first_bias, second_gain, second_bias, return_bias)):
        vecs[j : j + 1, :] = wide(vec[...]).reshape(1, width)
    for j in range(hidden_bias.shape[0] // width):
        part = hidden_bias[j * width : (j + 1) * width]
        vecs[HIDDEN_BIAS + j : HIDDEN_BIAS + j + 1, :] = wide(part).reshape(1, width)
    for j, here in enumerate(spans):
        at = j * ROWS
        copies[j].wait()
        unit, _ = norm_parts(wide(x[here, :]))
        rows = low(
            unit * vecs[FIRST_GAIN : FIRST_GAIN + 1, :] + vecs[FIRST_BIAS : FIRST_BIAS + 1, :]
        )
        normed[here, :] = rows
        key_t[:, here] = low(dot_nt(key_w[...], rows))
        values_ext[:head, here] = low(dot_nt(value_w[...], rows))
        values_ext[head:, here] = jnp.ones((values_ext.shape[0] - head, ROWS), LOW)
        logits[:, here] = dot_nt(router_w[...], rows)
        places = at + lax.broadcasted_iota(jnp.int32, (ROWS, head), 0)
        lanes = lax.broadcasted_iota(jnp.int32, (ROWS, head), 1)
        marks = low(jnp.where(segment_of(places, ends) == lanes, 1.0, 0.0))
        keys_ext[here, :] = jnp.concatenate([low(dot_nt(rows, key_w[...])), marks], axis=1)
        value_n[here, :] = jnp.concatenate(
            [low(dot_nt(rows, value_w[...])), jnp.ones((ROWS, head), LOW)], axis=1
        )
    for copy in copies[len(spans) :]:
        copy.wait()


def expert_hits(route, place, experts):
    own = experts // 2
    relative = lax.rem(route - place[0] * own + experts, experts)
    return [relative == e for e in range(experts)]


def forward_kernel(
    place, lengths, normed, x, vecs, q_own, q_other, o_own, o_other, keys_ext, values_ext, logits,
    routes, cot_far, hidden_w_far, return_w_far,
    exps, q_sel, attended, row_facts, placed, middle, hidden_in, hidden_in_t, d_feed, d_feed_t,
    bias_grad, cot, hidden_w, return_w, sems,
):
    copies = [
        pltpu.make_async_copy(far, near, sems.at[j])
        for j, (far, near) in enumerate(
            ((cot_far, cot), (hidden_w_far, hidden_w), (return_w_far, return_w))
        )
    ]
    for copy in copies:
        copy.start()
    ends = bounds_of(lengths, place)
    head = q_sel.shape[1]
    half = q_own.shape[0]
    experts = 2 * half // head
    own = experts // 2
    scale = head**-0.5
    for at in range(0, x.shape[0], ROWS):
        here = slice(at, at + ROWS)
        rows = normed[here, :]
        q_all = [low(dot_nt(q_own[...], rows)), low(dot_nt(q_other[...], rows))]
        places = at + lax.broadcasted_iota(jnp.int32, (head, ROWS), 1)
        subs = lax.broadcasted_iota(jnp.int32, (head, ROWS), 0)
        fence = low(jnp.where(segment_of(places, ends) == subs, 0.0, MASKED))
        chosen, hits, atts = [], [], []
        for m in range(2):
            route = routes[place[0], m : m + 1, here]
            picks = expert_hits(route, place, experts)
            hits.append(picks)
            query = jnp.zeros((head, ROWS), LOW)
            for e in range(experts):
                from_e = q_all[e // own][(e % own) * head : (e % own + 1) * head, :]
                query = jnp.where(picks[e], from_e, query)
            q_sel[m, :, here] = query
            spread = jnp.concatenate([low(wide(query) * scale), fence], axis=0)
            scores = dot_nn(keys_ext[...], spread)
            powers = low(jnp.exp(scores - jnp.max(scores, axis=0, keepdims=True)))
            exps[m, :, here] = powers
            summed = dot_nn(values_ext[...], powers)
            inv = 1.0 / summed[head : head + 1, :]
            att = summed[:head, :] * inv
            attended[m, :, here] = att
            atts.append(att)
            row_facts[2 + m : 3 + m, here] = inv
            ids = lax.broadcasted_iota(jnp.int32, (experts, ROWS), 0)
            chosen.append(
                jnp.sum(jnp.where(ids == route, logits[:, here], 0.0), axis=0, keepdims=True)
            )
        top = jnp.maximum(chosen[0], chosen[1])
        lifts = [jnp.exp(c - top) for c in chosen]
        inv_sum = 1.0 / (lifts[0] + lifts[1])
        for m in range(2):
            gate = lifts[m] * inv_sum
            row_facts[m : m + 1, here] = gate
            atts[m] = atts[m] * gate
        for e in range(experts):
            placed[e * head : (e + 1) * head, here] = low(
                jnp.where(hits[0][e], atts[0], jnp.where(hits[1][e], atts[1], 0.0))
            )
        branch = dot_tn(placed[:half, here], o_own[...]) + dot_tn(placed[half:, here], o_other[...])
        spots = at + lax.broadcasted_iota(jnp.int32, (ROWS, 1), 0)
        mid = wide(x[here, :]) + jnp.where(spots < ends[-1], branch, 0.0)
        middle[here, :] = mid
        unit, _ = norm_parts(mid)
        hidden = (
            unit * vecs[SECOND_GAIN : SECOND_GAIN + 1, :] + vecs[SECOND_BIAS : SECOND_BIAS + 1, :]
        )
        hidden_in[here, :] = low(hidden)
        hidden_in_t[:, here] = low(hidden.T)
    copies[0].wait()
    total = jnp.zeros(bias_grad.shape, WIDE)
    for at in range(0, x.shape[0], ROWS):
        here = slice(at, at + ROWS)
        spots = at + lax.broadcasted_iota(jnp.int32, (ROWS, 1), 0)
        masked = jnp.where(spots < ends[-1], wide(cot[here, :]), 0.0)
        d_feed[here, :] = low(masked)
        d_feed_t[:, here] = low(masked.T)
        total = total + jnp.sum(masked, axis=0, keepdims=True)
    bias_grad[...] = total
    for copy in copies[1:]:
        copy.wait()


def feed_kernel(
    which, place, hidden_in, hidden_in_t, d_feed, d_feed_t, vecs, hidden_w, return_w,
    act, d_before, grads, bias_grad,
):
    cols = act.shape[1]
    block = place[which]
    at = pl.ds(pl.multiple_of(block * cols, cols), cols)
    x = dot_nn(hidden_in[...], hidden_w[:, at]) + vecs[pl.ds(HIDDEN_BIAS + block, 1), :]
    squared = x * x
    rise = 0.5 + 0.5 * jnp.tanh(x * (CURVE + CURVE * CUBIC * squared))
    out = x * rise
    slope = rise + out * (1.0 - rise) * (2 * CURVE + 6 * CURVE * CUBIC * squared)
    act[...] = low(out)
    d_x = dot_nt(d_feed[...], return_w[at, :]) * slope
    d_before[...] = low(d_x)
    bias_grad[...] = jnp.sum(d_x, axis=0, keepdims=True)
    grads[0] = low(dot_nn(hidden_in_t[...], d_before[...]))
    grads[1] = low(dot_nn(d_feed_t[...], act[...]).T)


def middle_kernel(place, lengths, *refs):
    acts, d_befores = refs[:4], refs[4:8]
    hidden_w, return_w, vecs, middle, cot = refs[8:13]
    d_middle, d_low, gain_grad, bias_grad, layer_out_far, layer_out, sems = refs[13:]
    copies = []
    cols = acts[0].shape[1]
    end = bounds_of(lengths, place)[-1]
    spans = [pl.ds(pl.multiple_of(place[1 + j] * cols, cols), cols) for j in range(4)]
    gain_sum = jnp.zeros(gain_grad.shape, WIDE)
    bias_sum = jnp.zeros(bias_grad.shape, WIDE)
    for at in range(0, middle.shape[0], ROWS):
        here = slice(at, at + ROWS)
        feed = vecs[RETURN_BIAS : RETURN_BIAS + 1, :]
        d_hidden = 0.0
        for j in range(4):
            feed = feed + dot_nn(acts[j][here, :], return_w[spans[j], :])
            d_hidden = d_hidden + dot_nt(d_befores[j][here, :], hidden_w[:, spans[j]])
        valid = at + lax.broadcasted_iota(jnp.int32, (ROWS, 1), 0) < end
        mid = middle[here, :]
        layer_out[here, :] = mid + jnp.where(valid, feed, 0.0)
        copies.append(
            pltpu.make_async_copy(
                layer_out.at[here, :], layer_out_far.at[here, :], sems.at[len(copies)]
            )
        )
        copies[-1].start()
        unit, inv = norm_parts(mid)
        gain = vecs[SECOND_GAIN : SECOND_GAIN + 1, :]
        d_mid = wide(cot[here, :]) + norm_back(d_hidden, unit, inv, gain)
        d_middle[here, :] = d_mid
        d_low[here, :] = low(jnp.where(valid, d_mid, 0.0))
        gain_sum = gain_sum + jnp.sum(d_hidden * unit, axis=0, keepdims=True)
        bias_sum = bias_sum + jnp.sum(d_hidden, axis=0, keepdims=True)
    gain_grad[...] = gain_sum
    bias_grad[...] = bias_sum
    for copy in copies:
        copy.wait()


def attention_back_kernel(
    place, d_low, exps, q_sel, attended, row_facts, placed, key_t, value_n, o_own, o_other, routes,
    d_stack, d_keys, d_values, grad_o,
):
    head = key_t.shape[0]
    half = o_own.shape[0]
    experts = 2 * half // head
    own = experts // 2
    scale = head**-0.5
    tok = d_low.shape[0]
    d_keys[...] = jnp.zeros_like(d_keys)
    d_values[...] = jnp.zeros_like(d_values)
    for at in range(0, tok, ROWS):
        here = slice(at, at + ROWS)
        d_rows = d_low[here, :]
        d_all = [dot_nt(o_own[...], d_rows), dot_nt(o_other[...], d_rows)]
        hits, d_queries, d_gates = [], [], []
        for m in range(2):
            route = routes[place[0], m : m + 1, here]
            picks = expert_hits(route, place, experts)
            hits.append(picks)
            d_raw = jnp.zeros((head, ROWS), WIDE)
            for e in range(experts):
                from_e = d_all[e // own][(e % own) * head : (e % own + 1) * head, :]
                d_raw = jnp.where(picks[e], from_e, d_raw)
            att = attended[m, :, here]
            gate = row_facts[m : m + 1, here]
            inv = row_facts[2 + m : 3 + m, here]
            d_gates.append(jnp.sum(d_raw * att, axis=0, keepdims=True))
            d_att = low(d_raw * (gate * inv))
            inner = jnp.sum(wide(d_att) * att, axis=0, keepdims=True)
            inner_high = wide(low(inner))
            subs = lax.broadcasted_iota(jnp.int32, (head, ROWS), 0)
            tail = jnp.where(
                subs == 0, -inner_high, jnp.where(subs == 1, inner_high - inner, 0.0)
            )
            spread = jnp.concatenate([d_att, low(tail)], axis=0)
            d_score = low(wide(exps[m, :, here]) * dot_nn(value_n[...], spread))
            d_queries.append(dot_nn(key_t[...], d_score) * scale)
            d_keys[...] += dot_nt(d_score, q_sel[m, :, here])
            d_values[...] += dot_nt(exps[m, :, here], d_att)
        for e in range(experts):
            d_stack[e * head : (e + 1) * head, here] = low(
                jnp.where(hits[0][e], d_queries[0], jnp.where(hits[1][e], d_queries[1], 0.0))
            )
        gates = [row_facts[m : m + 1, here] for m in range(2)]
        mean_gate = gates[0] * d_gates[0] + gates[1] * d_gates[1]
        ids = lax.broadcasted_iota(jnp.int32, (experts, ROWS), 0)
        d_logits = sum(
            jnp.where(
                ids == routes[place[0], m : m + 1, here],
                gates[m] * (d_gates[m] - mean_gate),
                0.0,
            )
            for m in range(2)
        )
        high = wide(low(d_logits))
        d_stack[2 * half + 2 * head :, here] = low(jnp.concatenate([high, d_logits - high], axis=0))
    grad_o[...] = dot_nn(placed[...], d_low[...])
    for at in range(0, tok, ROWS):
        here = slice(at, at + ROWS)
        d_stack[2 * half : 2 * half + head, here] = low((d_keys[here, :] * scale).T)
        d_stack[2 * half + head : 2 * half + 2 * head, here] = low(d_values[here, :].T)


def close_kernel(
    place, d_stack, grad_o, q_own, q_other, normed, x, d_middle, vecs,
    return_bias_grad, second_gain_grad, second_bias_grad, bias_1, bias_2, bias_3, bias_4,
    key_w, value_w, router_w,
    own_grads, other_grads, input_grad_far, common, input_grad, sems,
):
    half = q_own.shape[0]
    head = key_w.shape[0]
    experts = router_w.shape[0]
    at_kv = 2 * half
    at_tail = at_kv + 2 * head
    owned = 2 * half
    shared = common.shape[0] // 2
    weights = jnp.concatenate([key_w[...], value_w[...], router_w[...], router_w[...]], axis=0)
    gain_sum = jnp.zeros((1, x.shape[1]), WIDE)
    bias_sum = jnp.zeros((1, x.shape[1]), WIDE)
    copies = []
    for at in range(0, x.shape[0], ROWS):
        here = slice(at, at + ROWS)
        d_normed = dot_tn(d_stack[:half, here], q_own[...])
        d_normed = d_normed + dot_tn(d_stack[half:at_kv, here], q_other[...])
        d_normed = d_normed + dot_tn(d_stack[at_kv:, here], weights)
        unit, inv = norm_parts(wide(x[here, :]))
        gain_sum = gain_sum + jnp.sum(d_normed * unit, axis=0, keepdims=True)
        bias_sum = bias_sum + jnp.sum(d_normed, axis=0, keepdims=True)
        gain = vecs[FIRST_GAIN : FIRST_GAIN + 1, :]
        input_grad[here, :] = d_middle[here, :] + norm_back(d_normed, unit, inv, gain)
        copies.append(
            pltpu.make_async_copy(
                input_grad.at[here, :], input_grad_far.at[here, :], sems.at[len(copies)]
            )
        )
        copies[-1].start()
    own_grads[:half, :] = low(dot_nn(d_stack[:half, :], normed[...]))
    other_grads[:half, :] = low(dot_nn(d_stack[half:at_kv, :], normed[...]))
    own_grads[half:owned, :] = low(grad_o[:half, :])
    other_grads[half:owned, :] = low(grad_o[half:, :])
    tail = dot_nn(d_stack[at_kv:, :], normed[...])
    common[...] = jnp.zeros_like(common)
    common[: 2 * head, :] = tail[: 2 * head, :]
    rest = shared
    common[rest : rest + experts, :] = (
        tail[2 * head : 2 * head + experts, :] + tail[2 * head + experts :, :]
    )
    rest = rest + experts
    rows = (gain_sum, bias_sum, second_gain_grad[...], second_bias_grad[...], return_bias_grad[...])
    for j, row in enumerate(rows):
        common[rest + j : rest + j + 1, :] = row
    for j, row in enumerate((bias_1, bias_2, bias_3, bias_4)):
        common[pl.ds(rest + HIDDEN_BIAS + place[1 + j], 1), :] = row[...]
    mine = pl.ds(pl.multiple_of(place[0] * shared, shared), shared)
    theirs = pl.ds(pl.multiple_of((1 - place[0]) * shared, shared), shared)
    own_grads[owned:, :] = low(common[mine, :])
    other_grads[owned:, :] = low(common[theirs, :])
    for copy in copies:
        copy.wait()


BLOCK, QUAD, HALVES = 1, 5, 6


def halvings(n_dp):
    return n_dp.bit_length() - 3


def step_orders(n_dp):
    first = list(range(halvings(n_dp)))
    second = []
    for at in range(0, len(first), 2):
        second += first[at : at + 2][::-1]
    return first, second


def pairs_of(n_dp, step):
    orders = step_orders(n_dp)
    return [
        (chip * 2 + core, (chip ^ (1 << orders[core][step])) * 2 + core)
        for chip in range(n_dp)
        for core in range(2)
    ]


def quad_pairs(n_dp, turn):
    return [
        (chip * 2 + core, (chip ^ (turn << halvings(n_dp))) * 2 + core)
        for chip in range(n_dp)
        for core in range(2)
    ]


def core_swap(values, n_dp):
    return lax.ppermute(values, AXES, [(at, at ^ 1) for at in range(2 * n_dp)])


def place_of(chip, core, n_dp):
    first, second = step_orders(n_dp)
    bits = [
        jnp.where(core == 0, (chip >> first[s]) & 1, (chip >> second[s]) & 1)
        for s in range(len(first))
    ]
    other_bit = jnp.where(core == 0, (chip >> second[0]) & 1, (chip >> first[0]) & 1)
    mine, other = 2 * core, 2 * (1 - core)
    entries = [core, other + 1 - other_bit, mine + 1 - bits[0], other + other_bit, mine + bits[0]]
    entries.append(chip >> halvings(n_dp))
    for bit in bits:
        entries += [1 - bit, bit]
    return jnp.stack(entries).astype(jnp.int32)


def add_kernel(*refs):
    total = wide(refs[0][...])
    for ref in refs[1:-1]:
        total = total + wide(ref[...])
    refs[-1][...] = low(total)


def add_call(name, *terms, after=()):
    return call(
        add_kernel, name, [], terms, there(terms[0].shape, LOW), after=after, cost=0.5
    )


def half_kernel(entry, place, left, right, out):
    size = out.shape[0]
    at = pl.ds(pl.multiple_of(place[entry] * size, size), size)
    out[...] = low(wide(left[at, :]) + wide(right[at, :]))


def half_call(name, place, entry, left, right, after=()):
    rows, cols = left.shape
    return call(
        functools.partial(half_kernel, entry), name, [place], [left, right],
        there((rows // 2, cols), LOW), after=after,
    )


def quarters_kernel(place, left, right, own, send_1, send_2, send_3, total):
    total[...] = wide(left[...]) + wide(right[...])
    cols = own.shape[1]
    for turn, out in enumerate((own, send_1, send_2, send_3)):
        spot = jnp.bitwise_xor(place[QUAD], turn)
        out[...] = low(total[:, pl.ds(pl.multiple_of(spot * cols, cols), cols)])


def quarters_call(name, place, left, right, after=()):
    rows, cols = left.shape
    return call(
        quarters_kernel, name, [place], [left, right], [there((rows, cols // 4), LOW)] * 4,
        scratch=[pltpu.VMEM((rows, cols), WIDE)], after=after,
    )


def row_of_four(place, own, got_1, got_2, got_3, out):
    cols = own.shape[1]
    for turn, piece in enumerate((own, got_1, got_2, got_3)):
        spot = jnp.bitwise_xor(place[QUAD], turn)
        out[:, pl.ds(pl.multiple_of(spot * cols, cols), cols)] = piece[...]


def four_call(name, place, pieces, after=()):
    rows, cols = pieces[0].shape
    return call(row_of_four, name, [place], pieces, there((rows, 4 * cols), LOW), after=after)


def join_kernel(entry, place, mine, got, out):
    size = mine.shape[0]
    out[pl.ds(pl.multiple_of(place[entry + 1] * size, size), size), :] = mine[...]
    out[pl.ds(pl.multiple_of(place[entry] * size, size), size), :] = got[...]


def join_call(name, place, entry, mine, got, after=()):
    rows, cols = mine.shape
    return call(
        functools.partial(join_kernel, entry), name, [place], [mine, got],
        there((2 * rows, cols), LOW), after=after,
    )


def place_kernel(which, place, quarter, *refs):
    hidden, returned, left, right, sems = refs[-5:]
    width, cols = left.shape
    left[...] = wide(quarter[:width, :])
    at = pl.ds(pl.multiple_of(place[which] * cols, cols), cols)
    first = pltpu.make_async_copy(left, hidden.at[:, at], sems.at[0])
    first.start()
    right[...] = wide(quarter[width:, :])
    second = pltpu.make_async_copy(right, returned.at[at, :], sems.at[1])
    second.start()
    first.wait()
    second.wait()


def place_call(place, which, quarter, ff, before=None):
    rows, cols = quarter.shape
    width = rows // 2
    anywhere = pl.BlockSpec(memory_space=pl.ANY)
    held_before = [] if before is None else list(before)
    return pl.pallas_call(
        functools.partial(place_kernel, which),
        in_specs=[
            pl.BlockSpec(memory_space=pltpu.SMEM),
            pl.BlockSpec(memory_space=pltpu.VMEM),
        ]
        + [anywhere] * len(held_before),
        out_specs=[anywhere, anywhere],
        out_shape=[there((width, ff), WIDE), there((ff, width), WIDE)],
        scratch_shapes=[
            pltpu.VMEM((width, cols), WIDE),
            pltpu.VMEM((width, cols), WIDE),
            pltpu.SemaphoreType.DMA((2,)),
        ],
        input_output_aliases={} if before is None else {2: 0, 3: 1},
        compiler_params=pltpu.CompilerParams(vmem_limit_bytes=VMEM_LIMIT),
        cost_estimate=pl.CostEstimate(flops=2 * 10**9, bytes_accessed=1024, transcendentals=0),
        name=f"place_{which}",
    )(place, pltpu.with_memory_space_constraint(quarter, pltpu.VMEM), *held_before)


def own_rows_kernel(entry, place, mine, got, query_grad, output_grad, shared, whole):
    size = mine.shape[0]
    whole[pl.ds(pl.multiple_of(place[entry + 1] * size, size), size), :] = wide(mine[...])
    whole[pl.ds(pl.multiple_of(place[entry] * size, size), size), :] = wide(got[...])
    half = query_grad.shape[0]
    query_grad[...] = whole[:half, :]
    output_grad[...] = whole[half : 2 * half, :]
    shared[...] = low(whole[2 * half :, :])


def shared_rows_kernel(place, mine, got, key_g, value_g, router_g, *refs):
    vectors, whole = refs[:-1], refs[-1]
    size = mine.shape[0]
    whole[pl.ds(pl.multiple_of(place[0] * size, size), size), :] = wide(mine[...])
    whole[pl.ds(pl.multiple_of((1 - place[0]) * size, size), size), :] = wide(got[...])
    head, experts = key_g.shape[0], router_g.shape[0]
    key_g[...] = whole[:head, :]
    value_g[...] = whole[head : 2 * head, :]
    router_g[...] = whole[size : size + experts, :]
    at = size + experts
    for j, vector in enumerate(vectors[:-1]):
        vector[...] = whole[at + j, :]
    width = mine.shape[1]
    at = at + len(vectors) - 1
    for j in range(vectors[-1].shape[0] // width):
        vectors[-1][j * width : (j + 1) * width] = whole[at + j, :]


def local(
    inputs, cotangent, lengths, routes, first_gain, first_bias, router_weight, key_weight,
    value_weight, query_weight, output_weight, second_gain, second_bias, hidden_weight,
    hidden_bias, return_weight, return_bias,
):
    tok, width = inputs.shape
    ff = hidden_weight.shape[1]
    n_dp = lax.axis_size("dp")
    chip, core = lax.axis_index("dp"), lax.axis_index("expert")
    own, _, head = query_weight.shape
    experts = 2 * own
    half = own * head

    q_own = jnp.transpose(query_weight, (0, 2, 1)).reshape(half, width)
    o_own = output_weight.reshape(half, width)
    q_other, o_other = core_swap(q_own, n_dp), core_swap(o_own, n_dp)
    key_w, value_w, router_w = key_weight.T, value_weight.T, router_weight.T
    place = place_of(chip, core, n_dp)
    spans = lengths[0]
    routes_t = jnp.transpose(routes[0], (0, 2, 1))
    vec_rows = 5 + ff // width

    blocks = tok // ROWS
    q_far, o_far = q_own, o_own
    normed, vecs, keys_ext, key_t, value_n, values_ext, logits, x, q_own, o_own = call(
        open_kernel, "first_norm", [place, spans], [],
        [
            held((tok, width), LOW), held((vec_rows + -vec_rows % 8, width), WIDE),
            held((tok, 2 * head), LOW), held((head, tok), LOW), held((tok, 2 * head), LOW),
            held((head + 16, tok), LOW), held((experts, tok), WIDE), held((tok, width), LOW),
            held((half, width), LOW), held((half, width), LOW),
        ],
        scratch=[pltpu.SemaphoreType.DMA((blocks + 2,))],
        loose=[
            first_gain, first_bias, second_gain, second_bias, return_bias, hidden_bias, key_w,
            value_w, router_w,
        ],
        far=[inputs, q_far, o_far],
        cost=2.0,
    )
    (
        exps, q_sel, attended, row_facts, placed, middle, hidden_in, hidden_in_t, d_feed, d_feed_t,
        return_bias_grad, cot, hidden_w, return_w,
    ) = call(
        forward_kernel, "attention_forward", [place, spans],
        [normed, x, vecs, q_own, q_other, o_own, o_other, keys_ext, values_ext, logits],
        [
            held((2, tok, tok), LOW), held((2, head, tok), LOW), held((2, head, tok), WIDE),
            held((8, tok), WIDE), held((2 * half, tok), LOW), held((tok, width), WIDE),
            held((tok, width), LOW), held((width, tok), LOW), held((tok, width), LOW),
            held((width, tok), LOW), held((1, width), WIDE), held((tok, width), LOW),
            held(hidden_weight.shape, LOW), held(return_weight.shape, LOW),
        ],
        scratch=[pltpu.SemaphoreType.DMA((3,))],
        loose=[routes_t],
        far=[cotangent, hidden_weight, return_weight],
        cost=10.0,
    )

    def feed(which, after=()):
        cols = width
        return call(
            functools.partial(feed_kernel, which), f"feed_{which}", [place],
            [hidden_in, hidden_in_t, d_feed, d_feed_t, vecs, hidden_w, return_w],
            [
                held((tok, cols), LOW), held((tok, cols), LOW), there((2, width, cols), LOW),
                held((1, cols), WIDE),
            ],
            after=after,
            cost=4.0,
        )

    flat = lambda v: v.reshape(2 * width, width)
    parts = [feed(BLOCK)]
    swapped_send = core_swap(flat(parts[0][2]), n_dp)
    parts.append(feed(BLOCK + 1))
    to_send = add_call("feed_add_send", flat(parts[1][2]), swapped_send)
    sent = lax.ppermute(to_send, AXES, pairs_of(n_dp, 0))
    parts.append(feed(BLOCK + 2, after=[to_send]))
    swapped_keep = core_swap(flat(parts[2][2]), n_dp)
    parts.append(feed(BLOCK + 3, after=[parts[2][2]]))
    kept = add_call("feed_add_keep", flat(parts[3][2]), swapped_keep)

    d_middle, d_low, second_gain_grad, second_bias_grad, layer_out = call(
        middle_kernel, "second_norm_back", [place, spans],
        [p[0] for p in parts] + [p[1] for p in parts]
        + [hidden_w, return_w, vecs, middle, cot],
        [
            held((tok, width), WIDE), held((tok, width), LOW), held((1, width), WIDE),
            held((1, width), WIDE), there((tok, width), WIDE),
        ],
        scratch=[pltpu.VMEM((tok, width), WIDE), pltpu.SemaphoreType.DMA((blocks,))],
        far_out=1,
        after=[kept],
        cost=6.0,
    )

    entry = HALVES + 2
    for step in range(1, halvings(n_dp)):
        send = half_call(f"feed_send_{step}", place, entry, kept, sent, after=[d_low])
        got = lax.ppermute(send, AXES, pairs_of(n_dp, step))
        kept = half_call(f"feed_keep_{step}", place, entry + 1, kept, sent, after=[send])
        sent = got
        entry += 2

    d_stack, _, _, grad_o = call(
        attention_back_kernel, "attention_backward", [place],
        [d_low, exps, q_sel, attended, row_facts, placed, key_t, value_n, o_own, o_other],
        [
            held((2 * half + 2 * head + 2 * experts, tok), LOW), held((tok, head), WIDE),
            held((tok, head), WIDE), held((2 * half, width), WIDE),
        ],
        after=[kept],
        loose=[routes_t],
        cost=9.0,
    )
    own, *sends = quarters_call("feed_cut", place, kept, sent, after=[d_stack])
    gots = [lax.ppermute(s, AXES, quad_pairs(n_dp, t + 1)) for t, s in enumerate(sends)]

    shared = 2 * head
    rows = 2 * half + shared
    unit = 4 * n_dp
    shared = shared + -rows % unit
    rows = 2 * half + shared
    own_grads, other_grads, input_grad = call(
        close_kernel, "first_norm_back", [place],
        [
            d_stack, grad_o, q_own, q_other, normed, x, d_middle, vecs, return_bias_grad,
            second_gain_grad, second_bias_grad, *[p[3] for p in parts],
        ],
        [there((rows, width), LOW), there((rows, width), LOW), there((tok, width), WIDE)],
        scratch=[
            pltpu.VMEM((2 * shared, width), WIDE), pltpu.VMEM((tok, width), WIDE),
            pltpu.SemaphoreType.DMA((blocks,)),
        ],
        far_out=1,
        after=[own],
        loose=[key_w, value_w, router_w],
        cost=4.0,
    )

    left, right = own_grads, core_swap(other_grads, n_dp)
    entry = HALVES
    for step in range(halvings(n_dp)):
        send = half_call(f"rest_send_{step}", place, entry, left, right)
        if step == 0:
            own = add_call("feed_sum", own, *gots, after=[send])
        got = lax.ppermute(send, AXES, pairs_of(n_dp, step))
        left, right = half_call(f"rest_keep_{step}", place, entry + 1, left, right), got
        entry += 2
    gots = [lax.ppermute(own, AXES, quad_pairs(n_dp, t)) for t in range(1, 4)]
    feed_part = four_call("feed_row", place, [own] + gots, after=[send])
    own, *sends = quarters_call("rest_cut", place, left, right)
    for step in reversed(range(1, halvings(n_dp))):
        got = lax.ppermute(feed_part, AXES, pairs_of(n_dp, step))
        feed_part = join_call(
            f"feed_join_{step}", place, HALVES + 2 * step, feed_part, got, after=[own]
        )
    got = lax.ppermute(feed_part, AXES, pairs_of(n_dp, 0))
    other_part = core_swap(feed_part, n_dp)
    other_got = core_swap(got, n_dp)
    written = place_call(place, BLOCK + 3, feed_part, ff)
    written = place_call(place, BLOCK + 2, other_part, ff, written)
    written = place_call(place, BLOCK + 1, got, ff, written)
    hidden_grad, return_grad = place_call(place, BLOCK, other_got, ff, written)

    gots = [lax.ppermute(s, AXES, quad_pairs(n_dp, t + 1)) for t, s in enumerate(sends)]
    own = add_call("rest_sum", own, *gots)
    gots = [lax.ppermute(own, AXES, quad_pairs(n_dp, t)) for t in range(1, 4)]
    rest = four_call("rest_row", place, [own] + gots)
    for step in reversed(range(1, halvings(n_dp))):
        got = lax.ppermute(rest, AXES, pairs_of(n_dp, step))
        rest = join_call(f"rest_join_{step}", place, HALVES + 2 * step, rest, got)
    got = lax.ppermute(rest, AXES, pairs_of(n_dp, 0))
    query_grad, output_grad, part = call(
        functools.partial(own_rows_kernel, HALVES), "own_rows", [place], [rest, got],
        [there((half, width), WIDE), there((half, width), WIDE), there((shared, width), LOW)],
        scratch=[pltpu.VMEM((rows, width), WIDE)],
    )
    vectors = [there((width,), WIDE)] * 5 + [there((ff,), WIDE)]
    key_g, value_g, router_g, fg, fb, sg, sb, rb, hb = call(
        shared_rows_kernel, "shared_rows", [place], [part, core_swap(part, n_dp)],
        [there((head, width), WIDE)] * 2 + [there((experts, width), WIDE)] + vectors,
        scratch=[pltpu.VMEM((2 * shared, width), WIDE)],
    )
    return (
        layer_out,
        input_grad,
        fg,
        fb,
        router_g.T,
        key_g.T,
        value_g.T,
        jnp.transpose(query_grad.reshape(-1, head, width), (0, 2, 1)),
        output_grad.reshape(-1, head, width),
        sg,
        sb,
        hidden_grad,
        hb,
        return_grad,
        rb,
    )


def solution(mesh):
    rows = P(AXES, None)
    cut = P("expert", None, None)
    in_specs = (
        (rows, rows, P("dp", None, None), P("dp", None, None, None))
        + (P(),) * 5
        + (cut, cut)
        + (P(),) * 6
    )
    out_specs = (rows, rows) + (P(),) * 5 + (cut, cut) + (P(),) * 6
    return jax.shard_map(local, mesh=mesh, in_specs=in_specs, out_specs=out_specs, check_vma=False)
```

```python
import functools

import jax
import jax.numpy as jnp
from jax import lax
from jax.experimental import pallas as pl
from jax.experimental.pallas import tpu as pltpu
from jax.sharding import PartitionSpec as P

AXES = ("dp", "expert")
WIDE = jnp.float32
LOW = jnp.bfloat16
EPS = 1e-05
MASKED = -1e30
ROWS = 256
SPAN = 512
CURVE = 0.7978845608028654
CUBIC = 0.044715
VMEM_LIMIT = 24 * 1024 * 1024


def low(values):
    return values.astype(LOW)


def wide(values):
    return values.astype(WIDE)


def dot_nn(left_op, right_op):
    return lax.dot_general(
        left_op, right_op, (((1,), (0,)), ((), ())), preferred_element_type=WIDE
    )


def dot_tn(left_op, right_op):
    return lax.dot_general(
        left_op, right_op, (((0,), (0,)), ((), ())), preferred_element_type=WIDE
    )


def dot_nt(left_op, right_op):
    return lax.dot_general(
        left_op, right_op, (((1,), (1,)), ((), ())), preferred_element_type=WIDE
    )


def norm_parts(values):
    row_mean = jnp.mean(values, axis=-1, keepdims=True)
    centred = values - row_mean
    inv_dev = lax.rsqrt(jnp.mean(centred * centred, axis=-1, keepdims=True) + EPS)
    return centred * inv_dev, inv_dev


def norm_back(d_out, unit, inv_dev, gain_vec):
    weighted = d_out * gain_vec
    mean_w = jnp.mean(weighted, axis=-1, keepdims=True)
    mean_wn = jnp.mean(weighted * unit, axis=-1, keepdims=True)
    return inv_dev * (weighted - mean_w - unit * mean_wn)


def core_here():
    return lax.axis_index("expert")


def segment_of(places, ends):
    return sum((places >= end).astype(jnp.int32) for end in ends)


def held(shape, dtype):
    return pltpu.VMEM(shape, dtype)


def there(shape, dtype):
    return jax.ShapeDtypeStruct(shape, dtype)


ANYWHERE = pl.BlockSpec(memory_space=pl.ANY)
INSIDE = pl.BlockSpec(memory_space=pltpu.VMEM)


class Program:
    def __init__(self):
        self.before = []

    def call(self, kernel, name, operands, out_shape, scratch=(), far=(), far_out=0, aliases=()):
        operands = [pltpu.with_memory_space_constraint(v, pltpu.VMEM) for v in operands]
        if not aliases:
            far = [pltpu.with_memory_space_constraint(v, pltpu.HBM) for v in far]
        count, waits = len(operands) + len(far), len(self.before)

        def run(*refs):
            kernel(*refs[:count], *refs[count + waits :])

        single = not isinstance(out_shape, (list, tuple))
        outs = [out_shape] if single else list(out_shape)
        near = len(outs) - far_out
        result = pl.pallas_call(
            run,
            in_specs=[INSIDE] * len(operands) + [ANYWHERE] * (len(far) + waits),
            out_specs=[INSIDE] * near + [ANYWHERE] * far_out,
            out_shape=outs,
            scratch_shapes=list(scratch),
            input_output_aliases={len(operands) + a: near + b for a, b in aliases},
            compiler_params=pltpu.CompilerParams(vmem_limit_bytes=VMEM_LIMIT),
            cost_estimate=pl.CostEstimate(flops=10**10, bytes_accessed=1, transcendentals=0),
            name=name,
        )(*operands, *far, *self.before)
        self.before = [result[0]]
        return result[0] if single else result


FIRST_GAIN, FIRST_BIAS, SECOND_GAIN, SECOND_BIAS, RETURN_BIAS, HIDDEN_BIAS = range(6)
SLOTS = 4
PARTS = 8


def bias_row(vecs, unit, cols):
    row = vecs[pl.ds(HIDDEN_BIAS + unit // 2, 1), :]
    return jnp.where(unit % 2 == 0, row[:, :cols], row[:, cols:])


def open_kernel(
    x_far, lengths_far, first_gain_far, first_bias_far, key_far, value_far, router_far, q_far,
    o_far, second_gain_far, second_bias_far, return_bias_far, hidden_bias_far, routes_far,
    normed, vecs, keys_ext, key_t, value_n, values_ext, logits, x, q_own, o_own, key_w, value_w,
    router_w, routes, ends_out,
    lengths, first_gain, first_bias, second_gain, second_bias, return_bias, hidden_bias, sems,
):
    spans = [slice(at, at + ROWS) for at in range(0, x.shape[0], ROWS)]
    moves = [(x_far.at[here, :], x.at[here, :]) for here in spans]
    needed = [
        (lengths_far, lengths), (first_gain_far, first_gain), (first_bias_far, first_bias),
        (key_far, key_w), (value_far, value_w), (router_far, router_w),
    ]
    later = [
        (q_far, q_own), (o_far, o_own), (second_gain_far, second_gain),
        (second_bias_far, second_bias), (return_bias_far, return_bias),
        (hidden_bias_far, hidden_bias), (routes_far.at[core_here()], routes),
    ]
    moves = moves[:1] + needed + moves[1:] + later
    copies = [pltpu.make_async_copy(*move, sems.at[j]) for j, move in enumerate(moves)]
    for copy in copies:
        copy.start()
    for copy in copies[: 1 + len(needed)]:
        copy.wait()
    head = key_w.shape[0]
    width = x.shape[1]
    ends, end = [], 0
    for slot in range(lengths.shape[1]):
        end = end + lengths[core_here(), slot]
        ends.append(end)
        ends_out[slot : slot + 1, :] = jnp.full((1, ends_out.shape[1]), end, jnp.int32)
    vecs[...] = jnp.zeros_like(vecs)
    for j, vec in enumerate((first_gain, first_bias)):
        vecs[j : j + 1, :] = wide(vec[...]).reshape(1, width)
    pair_w = jnp.concatenate([key_w[...], value_w[...]], axis=0)
    all_w = jnp.concatenate([key_w[...], value_w[...], router_w[...]], axis=0)
    for j, here in enumerate(spans):
        at = j * ROWS
        if j > 0:
            copies[len(needed) + j].wait()
        unit, _ = norm_parts(wide(x[here, :]))
        rows = low(
            unit * vecs[FIRST_GAIN : FIRST_GAIN + 1, :] + vecs[FIRST_BIAS : FIRST_BIAS + 1, :]
        )
        normed[here, :] = rows
        across = dot_nt(all_w, rows)
        key_t[:, here] = low(across[:head, :])
        values_ext[:head, here] = low(across[head : 2 * head, :])
        values_ext[head:, here] = jnp.ones((values_ext.shape[0] - head, ROWS), LOW)
        logits[:, here] = across[2 * head :, :]
        along = low(dot_nt(rows, pair_w))
        places = at + lax.broadcasted_iota(jnp.int32, (ROWS, head), 0)
        lanes = lax.broadcasted_iota(jnp.int32, (ROWS, head), 1)
        marks = low(jnp.where(segment_of(places, ends) == lanes, 1.0, 0.0))
        keys_ext[here, :] = jnp.concatenate([along[:, :head], marks], axis=1)
        value_n[here, :] = jnp.concatenate(
            [along[:, head:], jnp.ones((ROWS, head), LOW)], axis=1
        )
    for copy in copies[len(needed) + len(spans) :]:
        copy.wait()
    for j, vec in enumerate((second_gain, second_bias, return_bias)):
        vecs[SECOND_GAIN + j : SECOND_GAIN + j + 1, :] = wide(vec[...]).reshape(1, width)
    for j in range(hidden_bias.shape[0] // width):
        part = hidden_bias[j * width : (j + 1) * width]
        vecs[HIDDEN_BIAS + j : HIDDEN_BIAS + j + 1, :] = wide(part).reshape(1, width)


def expert_hits(route, experts):
    own = experts // 2
    relative = lax.rem(route - core_here() * own + experts, experts)
    return [relative == e for e in range(experts)]


def forward_kernel(
    normed, x, vecs, q_own, q_other, o_own, o_other, keys_ext, values_ext, logits, routes, ends_in,
    cot_far, hidden_w_far, return_w_far,
    exps, q_sel, attended, row_facts, placed, middle, hidden_in, hidden_in_t, d_feed, d_feed_t,
    bias_grad, cot, hidden_w, return_w, spread, sems,
):
    moves = ((cot_far, cot), (hidden_w_far, hidden_w), (return_w_far, return_w))
    copies = [pltpu.make_async_copy(*move, sems.at[j]) for j, move in enumerate(moves)]
    for copy in copies:
        copy.start()
    ends = [ends_in[slot, 0] for slot in range(SLOTS)]
    head = q_sel.shape[0]
    tok, half = x.shape[0], q_own.shape[0]
    experts = 2 * half // head
    own = experts // 2
    q_all = [low(dot_nt(q_own[...], normed[...])), low(dot_nt(q_other[...], normed[...]))]
    hits = [expert_hits(routes[m : m + 1, :], experts) for m in range(2)]
    places = lax.broadcasted_iota(jnp.int32, (head, tok), 1)
    subs = lax.broadcasted_iota(jnp.int32, (head, tok), 0)
    fence = low(jnp.where(segment_of(places, ends) == subs, 0.0, MASKED))
    for m in range(2):
        query = jnp.zeros((head, tok), LOW)
        for e in range(experts):
            from_e = q_all[e // own][(e % own) * head : (e % own + 1) * head, :]
            query = jnp.where(hits[m][e], from_e, query)
        lanes = slice(m * tok, (m + 1) * tok)
        q_sel[:, lanes] = query
        spread[:head, lanes] = low(wide(query) * head**-0.5)
        spread[head:, lanes] = fence

    def scores_of(at):
        return dot_nn(keys_ext[...], spread[:, at : at + SPAN])

    scores = scores_of(0)
    for at in range(0, 2 * tok, SPAN):
        later = scores_of(at + SPAN) if at + SPAN < 2 * tok else None
        here = slice(at, at + SPAN)
        powers = low(jnp.exp(scores - jnp.max(scores, axis=0, keepdims=True)))
        exps[:, here] = powers
        summed = dot_nn(values_ext[...], powers)
        inv = 1.0 / summed[head : head + 1, :]
        attended[:, here] = summed[:head, :] * inv
        row_facts[1:2, here] = inv
        scores = later
    ids = lax.broadcasted_iota(jnp.int32, (experts, tok), 0)
    chosen = [
        jnp.sum(jnp.where(ids == routes[m : m + 1, :], logits[...], 0.0), axis=0, keepdims=True)
        for m in range(2)
    ]
    top = jnp.maximum(chosen[0], chosen[1])
    lifts = [jnp.exp(c - top) for c in chosen]
    inv_sum = 1.0 / (lifts[0] + lifts[1])
    gated = []
    for m in range(2):
        lanes = slice(m * tok, (m + 1) * tok)
        gate = lifts[m] * inv_sum
        row_facts[0:1, lanes] = gate
        gated.append(attended[:, lanes] * gate)
    for e in range(experts):
        placed[e * head : (e + 1) * head, :] = low(
            jnp.where(hits[0][e], gated[0], jnp.where(hits[1][e], gated[1], 0.0))
        )
    copies[0].wait()
    total = jnp.zeros(bias_grad.shape, WIDE)
    for at in range(0, tok, SPAN):
        here = slice(at, at + SPAN)
        branch = dot_tn(placed[:half, here], o_own[...]) + dot_tn(placed[half:, here], o_other[...])
        spots = at + lax.broadcasted_iota(jnp.int32, (SPAN, 1), 0)
        mid = wide(x[here, :]) + jnp.where(spots < ends[-1], branch, 0.0)
        middle[here, :] = mid
        unit, _ = norm_parts(mid)
        hidden = (
            unit * vecs[SECOND_GAIN : SECOND_GAIN + 1, :] + vecs[SECOND_BIAS : SECOND_BIAS + 1, :]
        )
        hidden_in[here, :] = low(hidden)
        hidden_in_t[:, here] = low(hidden.T)
        masked = jnp.where(spots < ends[-1], wide(cot[here, :]), 0.0)
        d_feed[here, :] = low(masked)
        d_feed_t[:, here] = low(masked.T)
        total = total + jnp.sum(masked, axis=0, keepdims=True)
    bias_grad[...] = total
    for copy in copies[1:]:
        copy.wait()


def feed_kernel(
    units_of, joint, hidden_in, hidden_in_t, d_feed, d_feed_t, vecs, hidden_w, return_w, *outs
):
    units = units_of()
    grads_all = outs[-1] if joint else None
    for j, unit in enumerate(units):
        act, d_before, bias_grad = outs[3 * j : 3 * j + 3]
        cols = act.shape[1]
        at = rows_at(unit, cols)
        weight_in, weight_out = hidden_w[:, at], return_w[at, :]
        bias = bias_row(vecs, unit, cols)
        bias_sum = jnp.zeros(bias_grad.shape, WIDE)
        for row in range(0, act.shape[0], ROWS):
            here = slice(row, row + ROWS)
            x = dot_nn(hidden_in[here, :], weight_in) + bias
            d_act = dot_nt(d_feed[here, :], weight_out)
            squared = x * x
            rise = 0.5 + 0.5 * jnp.tanh(x * (CURVE + CURVE * CUBIC * squared))
            out = x * rise
            slope = rise + out * (1.0 - rise) * (2 * CURVE + 6 * CURVE * CUBIC * squared)
            act[here, :] = low(out)
            d_x = d_act * slope
            d_before[here, :] = low(d_x)
            bias_sum = bias_sum + jnp.sum(d_x, axis=0, keepdims=True)
        bias_grad[...] = bias_sum
        width = hidden_in.shape[1]
        rows = slice(j * width, (j + 1) * width)
        grads_all[rows, :cols] = low(dot_nn(hidden_in_t[...], d_before[...]))
        grads_all[rows, cols:] = low(dot_nn(d_feed_t[...], act[...]))


def middle_kernel(units_of, *refs):
    acts, d_befores = refs[:PARTS], refs[PARTS : 2 * PARTS]
    refs = refs[2 * PARTS :]
    hidden_w, return_w, vecs, middle, cot, ends_in = refs[:6]
    d_middle, d_low, gain_grad, bias_grad, layer_out_far, layer_out, sems = refs[6:]
    copies = []
    cols = acts[0].shape[1]
    end = ends_in[SLOTS - 1, 0]
    spans = [pl.ds(pl.multiple_of(block * cols, cols), cols) for block in units_of()]
    gain_sum = jnp.zeros(gain_grad.shape, WIDE)
    bias_sum = jnp.zeros(bias_grad.shape, WIDE)
    for at in range(0, middle.shape[0], ROWS):
        here = slice(at, at + ROWS)
        feed = vecs[RETURN_BIAS : RETURN_BIAS + 1, :]
        d_hidden = 0.0
        for j in range(PARTS):
            feed = feed + dot_nn(acts[j][here, :], return_w[spans[j], :])
            d_hidden = d_hidden + dot_nt(d_befores[j][here, :], hidden_w[:, spans[j]])
        valid = at + lax.broadcasted_iota(jnp.int32, (ROWS, 1), 0) < end
        mid = middle[here, :]
        layer_out[here, :] = mid + jnp.where(valid, feed, 0.0)
        copies.append(
            pltpu.make_async_copy(
                layer_out.at[here, :], layer_out_far.at[here, :], sems.at[len(copies)]
            )
        )
        copies[-1].start()
        unit, inv = norm_parts(mid)
        gain = vecs[SECOND_GAIN : SECOND_GAIN + 1, :]
        d_mid = wide(cot[here, :]) + norm_back(d_hidden, unit, inv, gain)
        d_middle[here, :] = d_mid
        d_low[here, :] = low(jnp.where(valid, d_mid, 0.0))
        gain_sum = gain_sum + jnp.sum(d_hidden * unit, axis=0, keepdims=True)
        bias_sum = bias_sum + jnp.sum(d_hidden, axis=0, keepdims=True)
    gain_grad[...] = gain_sum
    bias_grad[...] = bias_sum
    for copy in copies:
        copy.wait()


def attention_back_kernel(
    d_low, exps, q_sel, attended, row_facts, placed, key_t, value_n, o_own, o_other, routes,
    d_stack, grad_o, spread, d_scores, d_queries,
):
    head = key_t.shape[0]
    tok, half = d_low.shape[0], o_own.shape[0]
    experts = 2 * half // head
    own = experts // 2
    scale = head**-0.5
    d_all = [dot_nt(o_own[...], d_low[...]), dot_nt(o_other[...], d_low[...])]
    hits = [expert_hits(routes[m : m + 1, :], experts) for m in range(2)]
    halves = [slice(m * tok, (m + 1) * tok) for m in range(2)]
    gates = [row_facts[0:1, lanes] for lanes in halves]
    subs = lax.broadcasted_iota(jnp.int32, (head, tok), 0)
    d_gates = []
    for m, lanes in enumerate(halves):
        d_raw = jnp.zeros((head, tok), WIDE)
        for e in range(experts):
            from_e = d_all[e // own][(e % own) * head : (e % own + 1) * head, :]
            d_raw = jnp.where(hits[m][e], from_e, d_raw)
        att = attended[:, lanes]
        d_gates.append(jnp.sum(d_raw * att, axis=0, keepdims=True))
        d_att = low(d_raw * (gates[m] * row_facts[1:2, lanes]))
        inner = jnp.sum(wide(d_att) * att, axis=0, keepdims=True)
        inner_high = wide(low(inner))
        tail = jnp.where(subs == 0, -inner_high, jnp.where(subs == 1, inner_high - inner, 0.0))
        spread[:head, lanes] = d_att
        spread[head:, lanes] = low(tail)
    mean_gate = gates[0] * d_gates[0] + gates[1] * d_gates[1]
    ids = lax.broadcasted_iota(jnp.int32, (experts, tok), 0)
    d_logits = sum(
        jnp.where(ids == routes[m : m + 1, :], gates[m] * (d_gates[m] - mean_gate), 0.0)
        for m in range(2)
    )
    high = wide(low(d_logits))
    d_stack[2 * half + 2 * head :, :] = low(jnp.concatenate([high, d_logits - high], axis=0))
    for at in range(0, 2 * tok, ROWS):
        here = slice(at, at + ROWS)
        d_score = low(wide(exps[:, here]) * dot_nn(value_n[...], spread[:, here]))
        d_scores[:, here] = d_score
        d_queries[:, here] = dot_nn(key_t[...], d_score) * scale
    d_values = dot_nt(exps[...], spread[:head, :])
    d_keys = dot_nt(d_scores[...], q_sel[...]) * scale
    d_stack[2 * half : 2 * half + head, :] = low(d_keys.T)
    d_stack[2 * half + head : 2 * half + 2 * head, :] = low(d_values.T)
    first, second = d_queries[:, halves[0]], d_queries[:, halves[1]]
    for e in range(experts):
        d_stack[e * head : (e + 1) * head, :] = low(
            jnp.where(hits[0][e], first, jnp.where(hits[1][e], second, 0.0))
        )
    grad_o[...] = dot_nn(placed[...], d_low[...])


def close_kernel(
    units_of, d_stack, grad_o, q_own, q_other, normed, x, d_middle, vecs, return_bias_grad,
    second_gain_grad, second_bias_grad, key_w, value_w, router_w, *rest,
):
    bias_parts = rest[:PARTS]
    own_grads, other_grads, input_grad_far, common, input_grad, sems = rest[PARTS:]
    half = q_own.shape[0]
    head = key_w.shape[0]
    experts = router_w.shape[0]
    at_kv = 2 * half
    at_tail = at_kv + 2 * head
    owned = 2 * half
    weights = jnp.concatenate([key_w[...], value_w[...], router_w[...], router_w[...]], axis=0)
    gain_sum = jnp.zeros((1, x.shape[1]), WIDE)
    bias_sum = jnp.zeros((1, x.shape[1]), WIDE)
    copies = []
    for at in range(0, x.shape[0], ROWS):
        here = slice(at, at + ROWS)
        d_normed = dot_tn(d_stack[:half, here], q_own[...])
        d_normed = d_normed + dot_tn(d_stack[half:at_kv, here], q_other[...])
        d_normed = d_normed + dot_tn(d_stack[at_kv:, here], weights)
        unit, inv = norm_parts(wide(x[here, :]))
        gain_sum = gain_sum + jnp.sum(d_normed * unit, axis=0, keepdims=True)
        bias_sum = bias_sum + jnp.sum(d_normed, axis=0, keepdims=True)
        gain = vecs[FIRST_GAIN : FIRST_GAIN + 1, :]
        input_grad[here, :] = d_middle[here, :] + norm_back(d_normed, unit, inv, gain)
        copies.append(
            pltpu.make_async_copy(
                input_grad.at[here, :], input_grad_far.at[here, :], sems.at[len(copies)]
            )
        )
        copies[-1].start()
    own_grads[:half, :] = low(dot_nn(d_stack[:half, :], normed[...]))
    other_grads[:half, :] = low(dot_nn(d_stack[half:at_kv, :], normed[...]))
    own_grads[half:owned, :] = low(grad_o[:half, :])
    other_grads[half:owned, :] = low(grad_o[half:, :])
    tail = dot_nn(d_stack[at_kv:, :], normed[...])
    common[...] = jnp.zeros_like(common)
    common[: 2 * head, :] = tail[: 2 * head, :]
    row = 2 * head
    common[row : row + experts, :] = (
        tail[2 * head : 2 * head + experts, :] + tail[2 * head + experts :, :]
    )
    row = row + experts
    rows = (gain_sum, bias_sum, second_gain_grad[...], second_bias_grad[...], return_bias_grad[...])
    for j, values in enumerate(rows):
        common[row + j : row + j + 1, :] = values
    for unit, part in zip(units_of(), bias_parts):
        cols = part.shape[1]
        at = pl.ds(row + HIDDEN_BIAS + unit // 2, 1)
        there_now = common[at, :]
        doubled = jnp.concatenate([part[...], part[...]], axis=1)
        lanes = lax.broadcasted_iota(jnp.int32, doubled.shape, 1)
        common[at, :] = jnp.where(lanes // cols == unit % 2, doubled, there_now)
    own_grads[owned:, :] = low(common[...])
    other_grads[owned:, :] = low(common[...])
    for copy in copies:
        copy.wait()


def halvings(n_dp):
    return n_dp.bit_length() - 3


def step_orders(n_dp):
    first = list(range(halvings(n_dp)))
    second = []
    for at in range(0, len(first), 2):
        second += first[at : at + 2][::-1]
    return first, second


def pairs_of(n_dp, step):
    orders = step_orders(n_dp)
    return [
        (chip * 2 + core, (chip ^ (1 << orders[core][step])) * 2 + core)
        for chip in range(n_dp)
        for core in range(2)
    ]


def quad_pairs(n_dp, turn):
    return [
        (chip * 2 + core, (chip ^ (turn << halvings(n_dp))) * 2 + core)
        for chip in range(n_dp)
        for core in range(2)
    ]


def cross_pairs(n_dp, turn):
    low_bit = halvings(n_dp)
    return [
        (chip * 2 + core, (chip ^ (1 << (low_bit + (turn ^ core)))) * 2 + core)
        for chip in range(n_dp)
        for core in range(2)
    ]


def core_swap(values, n_dp):
    return lax.ppermute(values, AXES, [(at, at ^ 1) for at in range(2 * n_dp)])


def bit_here(n_dp, step, core=None):
    first, second = step_orders(n_dp)
    chip = lax.axis_index("dp")
    core = core_here() if core is None else core
    return jnp.where(core == 0, chip >> first[step], chip >> second[step]) & 1


def units_here(n_dp, entries):
    core = core_here()
    mine, theirs = bit_here(n_dp, 0), bit_here(n_dp, 0, 1 - core)
    other = 1 - core
    blocks = [2 * other + 1 - theirs, 2 * core + 1 - mine, 2 * other + theirs, 2 * core + mine]
    return [2 * blocks[entry // 2] + entry % 2 for entry in entries]


def rows_at(index, size):
    return pl.ds(pl.multiple_of(index * size, size), size)


def add_kernel(*refs):
    total = wide(refs[0][...])
    for ref in refs[1:-1]:
        total = total + wide(ref[...])
    refs[-1][...] = low(total)


def rows_of(ref, at, size):
    return wide(ref[pl.ds(pl.multiple_of(at, size), size), :])


def partial_sum(n_dp, terms, step, last_kept):
    start = step - len(terms) + 1
    size = terms[0][0].shape[0] >> (step - start + 1)
    at, total = 0, 0.0
    for j in range(step, start - 1, -1):
        bit = bit_here(n_dp, j)
        bit = bit if last_kept or j < step else 1 - bit
        at = at + bit * (size << (step - j))
        for ref in terms[j - start]:
            total = total + rows_of(ref, at, size)
    return total


def group(refs, counts):
    refs = list(refs)
    return [[refs.pop(0) for _ in range(count)] for count in counts]


def split_terms(terms, joint):
    parts = []
    for part in range(2):
        chosen = []
        for refs, flags in zip(terms, joint):
            chosen.append([])
            for ref, flag in zip(refs, flags):
                half = ref.shape[0] // 2
                if flag == 2:
                    chosen[-1].append(ref.at[pl.ds(part * half, half), :])
                elif flag == part:
                    chosen[-1].append(ref)
        parts.append(chosen)
    return parts


def send_kernel(n_dp, step, counts, joint, *refs):
    out = refs[-1]
    terms = group(refs[:-1], counts)
    if joint is None:
        out[...] = low(partial_sum(n_dp, terms, step, False))
        return
    size = out.shape[0] // 2
    for part, chosen in enumerate(split_terms(terms, joint)):
        out[part * size : (part + 1) * size, :] = low(partial_sum(n_dp, chosen, step, False))


def kept_kernel(n_dp, step, counts, *refs):
    *terms, last = group(refs[:-1], counts)
    refs[-1][...] = low(partial_sum(n_dp, terms, step, True) + wide(last[0][...]))


def spot_here(n_dp, turn):
    return jnp.bitwise_xor(lax.axis_index("dp") >> halvings(n_dp), turn)


def quarters_kernel(n_dp, step, counts, joint, *refs):
    count = sum(counts)
    terms = group(refs[:count], counts)
    outs, total = refs[count:-1], refs[-1]
    size = total.shape[0] // 2
    for part, (*chosen, last) in enumerate(split_terms(terms, joint)):
        total[part * size : (part + 1) * size, :] = partial_sum(
            n_dp, chosen, step, True
        ) + wide(last[0][...])
    cols = outs[0].shape[1]
    for turn, out in enumerate(outs):
        out[...] = low(total[:, rows_at(spot_here(n_dp, turn), cols)])


def row_of_four(n_dp, *refs):
    out = refs[-1]
    cols = refs[0].shape[1]
    for turn, piece in enumerate(refs[:-1]):
        out[:, rows_at(spot_here(n_dp, turn), cols)] = piece[...]


def join_parts_kernel(n_dp, step, mine, got, out):
    size = mine.shape[0] // 2
    bit = bit_here(n_dp, step)
    for part in range(2):
        here = slice(part * size, (part + 1) * size)
        out[rows_at(2 * part + bit, size), :] = mine[here, :]
        out[rows_at(2 * part + 1 - bit, size), :] = got[here, :]


def join_kernel(n_dp, step, mine, got, out):
    size = mine.shape[0]
    bit = bit_here(n_dp, step)
    out[rows_at(bit, size), :] = mine[...]
    out[rows_at(1 - bit, size), :] = got[...]


def place_kernel(units_of, both, *refs):
    token, hidden, returned, left, right, sems = refs[-6:]
    copies = []
    width = both.shape[0] // 2
    cols = both.shape[1] // 2
    for j, unit in enumerate(units_of()):
        here = slice(j * width, (j + 1) * width)
        at = rows_at(unit, cols)
        left[j] = wide(both[here, :cols])
        copies.append(pltpu.make_async_copy(left.at[j], hidden.at[:, at], sems.at[2 * j]))
        copies[-1].start()
        right[j] = wide(both[here, cols:]).T
        copies.append(pltpu.make_async_copy(right.at[j], returned.at[at, :], sems.at[2 * j + 1]))
        copies[-1].start()
    token[...] = jnp.zeros_like(token)
    for copy in copies:
        copy.wait()


def finish_kernel(n_dp, mine, got, query_g, output_g, key_g, value_g, router_g, *refs):
    vectors, whole = refs[:-1], refs[-1]
    size, width = mine.shape
    bit = bit_here(n_dp, 0)
    whole[rows_at(bit, size), :] = wide(mine[...])
    whole[rows_at(1 - bit, size), :] = wide(got[...])
    row = 0
    for out in (query_g, output_g, key_g, value_g, router_g):
        out[...] = whole[row : row + out.shape[0], :]
        row = row + out.shape[0]
    for j, vector in enumerate(vectors[:-1]):
        vector[...] = whole[row + j, :]
    row = row + len(vectors) - 1
    for j in range(vectors[-1].shape[0] // width):
        vectors[-1][j * width : (j + 1) * width] = whole[row + j, :]


def local(
    inputs, cotangent, lengths, routes, first_gain, first_bias, router_weight, key_weight,
    value_weight, query_weight, output_weight, second_gain, second_bias, hidden_weight,
    hidden_bias, return_weight, return_bias,
):
    tok, width = inputs.shape
    ff = hidden_weight.shape[1]
    n_dp = lax.axis_size("dp")
    own, _, head = query_weight.shape
    experts = 2 * own
    half = own * head
    blocks = tok // ROWS

    q_own = jnp.transpose(query_weight, (0, 2, 1)).reshape(half, width)
    o_own = output_weight.reshape(half, width)
    q_other, o_other = core_swap(q_own, n_dp), core_swap(o_own, n_dp)
    vec_rows = 5 + ff // width
    program = Program()
    call = program.call
    (
        normed, vecs, keys_ext, key_t, value_n, values_ext, logits, x, q_own, o_own, key_w, value_w,
        router_w, routes, ends,
    ) = call(
        open_kernel, "first_norm", [],
        [
            held((tok, width), LOW), held((vec_rows + -vec_rows % 8, width), WIDE),
            held((tok, 2 * head), LOW), held((head, tok), LOW), held((tok, 2 * head), LOW),
            held((head + 16, tok), LOW), held((experts, tok), WIDE), held((tok, width), LOW),
            held((half, width), LOW), held((half, width), LOW), held((head, width), LOW),
            held((head, width), LOW), held((experts, width), LOW), held((2, tok), jnp.int32),
            held((8, 128), jnp.int32),
        ],
        scratch=[pltpu.SMEM(lengths.shape[1:], jnp.int32)]
        + [pltpu.VMEM((width,), LOW)] * 5
        + [pltpu.VMEM((ff,), LOW), pltpu.SemaphoreType.DMA((blocks + 13,))],
        far=[
            inputs, lengths[0], first_gain, first_bias, key_weight.T, value_weight.T,
            router_weight.T, q_own, o_own, second_gain, second_bias, return_bias, hidden_bias,
            jnp.transpose(routes[0], (0, 2, 1)),
        ],
    )
    (
        exps, q_sel, attended, row_facts, placed, middle, hidden_in, hidden_in_t, d_feed, d_feed_t,
        return_bias_grad, cot, hidden_w, return_w,
    ) = call(
        forward_kernel, "attention_forward",
        [
            normed, x, vecs, q_own, q_other, o_own, o_other, keys_ext, values_ext, logits, routes,
            ends,
        ],
        [
            held((tok, 2 * tok), LOW), held((head, 2 * tok), LOW), held((head, 2 * tok), WIDE),
            held((8, 2 * tok), WIDE), held((2 * half, tok), LOW), held((tok, width), WIDE),
            held((tok, width), LOW), held((width, tok), LOW), held((tok, width), LOW),
            held((width, tok), LOW), held((1, width), WIDE), held((tok, width), LOW),
            held(hidden_weight.shape, LOW), held(return_weight.shape, LOW),
        ],
        scratch=[pltpu.VMEM((2 * head, 2 * tok), LOW), pltpu.SemaphoreType.DMA((3,))],
        far=[cotangent, hidden_weight, return_weight],
    )

    cols = ff // PARTS
    units = lambda *entries: functools.partial(units_here, n_dp, entries)
    steps = halvings(n_dp)

    def feed(*entries):
        outs = call(
            functools.partial(feed_kernel, units(*entries), True), f"feed_{entries[0]}",
            [hidden_in, hidden_in_t, d_feed, d_feed_t, vecs, hidden_w, return_w],
            [held((tok, cols), LOW), held((tok, cols), LOW), held((1, cols), WIDE)] * len(entries)
            + [there((len(entries) * width, 2 * cols), LOW)],
        )
        return list(zip(*[iter(outs[:-1])] * 3)), outs[-1]

    def add(name, *terms):
        return call(add_kernel, name, terms, there(terms[0].shape, LOW))

    parts_a, theirs_a = feed(0)
    parts_b, theirs_b = feed(1)
    swap_a, swap_b = core_swap(theirs_a, n_dp), core_swap(theirs_b, n_dp)
    parts_c, mine_a = feed(2)
    sent_a = lax.ppermute(add("feed_add_0", mine_a, swap_a), AXES, pairs_of(n_dp, 0))
    parts_d, mine_b = feed(3)
    sent_b = lax.ppermute(add("feed_add_1", mine_b, swap_b), AXES, pairs_of(n_dp, 0))
    parts_e, theirs = feed(4, 5)
    swapped = core_swap(theirs, n_dp)
    parts_f, mine = feed(6, 7)
    parts = parts_a + parts_b + parts_c + parts_d + parts_e + parts_f

    every = units(*range(PARTS))
    d_middle, d_low, second_gain_grad, second_bias_grad, layer_out = call(
        functools.partial(middle_kernel, every), "second_norm_back",
        [p[0] for p in parts] + [p[1] for p in parts]
        + [hidden_w, return_w, vecs, middle, cot, ends],
        [
            held((tok, width), WIDE), held((tok, width), LOW), held((1, width), WIDE),
            held((1, width), WIDE), there((tok, width), WIDE),
        ],
        scratch=[pltpu.VMEM((tok, width), WIDE), pltpu.SemaphoreType.DMA((blocks,))],
        far_out=1,
    )

    feed_terms, feed_joint = [[sent_a, sent_b, swapped, mine]], [[0, 1, 2, 2]]

    def feed_send(step):
        counts = [len(t) for t in feed_terms]
        part = call(
            functools.partial(send_kernel, n_dp, step, counts, list(feed_joint)),
            f"feed_send_{step}", sum(feed_terms, []), there((2 * width >> step, 2 * cols), LOW),
        )
        feed_terms.append([lax.ppermute(part, AXES, pairs_of(n_dp, step))])
        feed_joint.append([2])

    for step in range(1, steps):
        feed_send(step)
    d_stack, grad_o = call(
        attention_back_kernel, "attention_backward",
        [d_low, exps, q_sel, attended, row_facts, placed, key_t, value_n, o_own, o_other, routes],
        [held((2 * half + 2 * head + 2 * experts, tok), LOW), held((2 * half, width), WIDE)],
        scratch=[
            pltpu.VMEM((2 * head, 2 * tok), LOW), pltpu.VMEM((tok, 2 * tok), LOW),
            pltpu.VMEM((head, 2 * tok), WIDE),
        ],
    )
    counts = [len(t) for t in feed_terms]
    own_piece, *pieces = call(
        functools.partial(quarters_kernel, n_dp, steps - 1, counts, feed_joint), "feed_cut",
        sum(feed_terms, []), [there((2 * width >> (steps - 1), cols // 2), LOW)] * 4,
        scratch=[pltpu.VMEM((2 * width >> (steps - 1), 2 * cols), WIDE)],
    )

    def across(values):
        return [
            lax.ppermute(v, AXES, quad_pairs(n_dp, t + 1)) for t, v in enumerate(values)
        ]

    pieces = across(pieces)
    shared = 2 * head + experts + 5 + ff // width
    shared = shared + -(2 * half + shared) % (16 << steps)
    rows = 2 * half + shared
    own_grads, other_grads, input_grad = call(
        functools.partial(close_kernel, every), "first_norm_back",
        [
            d_stack, grad_o, q_own, q_other, normed, x, d_middle, vecs, return_bias_grad,
            second_gain_grad, second_bias_grad, key_w, value_w, router_w, *[p[2] for p in parts],
        ],
        [there((rows, width), LOW), there((rows, width), LOW), there((tok, width), WIDE)],
        scratch=[
            pltpu.VMEM((shared, width), WIDE), pltpu.VMEM((tok, width), WIDE),
            pltpu.SemaphoreType.DMA((blocks,)),
        ],
        far_out=1,
    )

    rest_terms = [[own_grads, core_swap(other_grads, n_dp)]]

    def rest_send(step):
        counts = [len(t) for t in rest_terms]
        part = call(
            functools.partial(send_kernel, n_dp, step, counts, None), f"rest_send_{step}",
            sum(rest_terms, []), there((rows >> (step + 1), width), LOW),
        )
        rest_terms.append([lax.ppermute(part, AXES, pairs_of(n_dp, step))])

    def rest_join(step, mine, got):
        size = mine.shape[0]
        kernel = functools.partial(join_kernel, n_dp, step)
        return call(kernel, f"rest_join_{step}", [mine, got], there((2 * size, width), LOW))

    own_piece = add("feed_sum", own_piece, *pieces)
    pieces = across([own_piece] * 3)
    rest_send(0)
    for step in range(1, steps):
        rest_send(step)
    size = own_piece.shape[0]
    joined = call(
        functools.partial(row_of_four, n_dp), "feed_row", [own_piece] + pieces,
        there((size, 2 * cols), LOW),
    )
    got = lax.ppermute(joined, AXES, pairs_of(n_dp, steps - 1))
    counts = [len(t) for t in rest_terms]
    rest = call(
        functools.partial(kept_kernel, n_dp, steps - 1, counts), "rest_sum", sum(rest_terms, []),
        there((rows >> steps, width), LOW),
    )
    rest_got = lax.ppermute(rest, AXES, cross_pairs(n_dp, 0))
    rest = add("rest_add_0", rest, rest_got)
    rest_got = lax.ppermute(rest, AXES, cross_pairs(n_dp, 1))
    for step in reversed(range(1, steps)):
        size = 2 * size
        joined = call(
            functools.partial(join_parts_kernel, n_dp, step), f"feed_join_{step}", [joined, got],
            there((size, 2 * cols), LOW),
        )
        got = lax.ppermute(joined, AXES, pairs_of(n_dp, step - 1))

    written = None

    def place(name, entries, both):
        nonlocal written
        _, *written = call(
            functools.partial(place_kernel, units(*entries)), name, [both],
            [held((8, 128), WIDE), there((width, ff), WIDE), there((ff, width), WIDE)],
            scratch=[
                pltpu.VMEM((2, width, cols), WIDE), pltpu.VMEM((2, cols, width), WIDE),
                pltpu.SemaphoreType.DMA((4,)),
            ],
            far=[] if written is None else written,
            far_out=2,
            aliases=[] if written is None else [(0, 0), (1, 1)],
        )

    place("place_own", (6, 7), joined)
    rest = add("rest_add_1", rest, rest_got)
    rest_got = lax.ppermute(rest, AXES, pairs_of(n_dp, steps - 1))
    place("place_other", (4, 5), core_swap(joined, n_dp))
    for step in reversed(range(1, steps)):
        rest = rest_join(step, rest, rest_got)
        rest_got = lax.ppermute(rest, AXES, pairs_of(n_dp, step - 1))
    place("place_got", (2, 3), got)
    vectors = [there((width,), WIDE)] * 5 + [there((ff,), WIDE)]
    query_grad, output_grad, key_g, value_g, router_g, fg, fb, sg, sb, rb, hb = call(
        functools.partial(finish_kernel, n_dp), "finish", [rest, rest_got],
        [there((half, width), WIDE)] * 2 + [there((head, width), WIDE)] * 2
        + [there((experts, width), WIDE)] + vectors,
        scratch=[pltpu.VMEM((rows, width), WIDE)],
    )
    place("place_far", (0, 1), core_swap(got, n_dp))
    hidden_grad, return_grad = written
    return (
        layer_out,
        input_grad,
        fg,
        fb,
        router_g.T,
        key_g.T,
        value_g.T,
        jnp.transpose(query_grad.reshape(-1, head, width), (0, 2, 1)),
        output_grad.reshape(-1, head, width),
        sg,
        sb,
        hidden_grad,
        hb,
        return_grad,
        rb,
    )


def solution(mesh):
    rows = P(AXES, None)
    cut = P("expert", None, None)
    in_specs = (
        (rows, rows, P("dp", None, None), P("dp", None, None, None))
        + (P(),) * 5
        + (cut, cut)
        + (P(),) * 6
    )
    out_specs = (rows, rows) + (P(),) * 5 + (cut, cut) + (P(),) * 6
    return jax.shard_map(local, mesh=mesh, in_specs=in_specs, out_specs=out_specs, check_vma=False)
```

```python
import functools

import jax
import jax.numpy as jnp
from jax import lax
from jax.experimental import pallas as pl
from jax.experimental.pallas import tpu as pltpu
from jax.sharding import PartitionSpec as P

AXES = ("dp", "expert")
WIDE = jnp.float32
LOW = jnp.bfloat16
EPS = 1e-05
MASKED = -1e30
ROWS = 256
SPAN = 512
CURVE = 0.7978845608028654
CUBIC = 0.044715
VMEM_LIMIT = 24 * 1024 * 1024


def low(values):
    return values.astype(LOW)


def wide(values):
    return values.astype(WIDE)


def dot_nn(left_op, right_op):
    return lax.dot_general(
        left_op, right_op, (((1,), (0,)), ((), ())), preferred_element_type=WIDE
    )


def dot_tn(left_op, right_op):
    return lax.dot_general(
        left_op, right_op, (((0,), (0,)), ((), ())), preferred_element_type=WIDE
    )


def dot_nt(left_op, right_op):
    return lax.dot_general(
        left_op, right_op, (((1,), (1,)), ((), ())), preferred_element_type=WIDE
    )


def norm_parts(values):
    row_mean = jnp.mean(values, axis=-1, keepdims=True)
    centred = values - row_mean
    inv_dev = lax.rsqrt(jnp.mean(centred * centred, axis=-1, keepdims=True) + EPS)
    return centred * inv_dev, inv_dev


def norm_back(d_out, unit, inv_dev, gain_vec):
    weighted = d_out * gain_vec
    mean_w = jnp.mean(weighted, axis=-1, keepdims=True)
    mean_wn = jnp.mean(weighted * unit, axis=-1, keepdims=True)
    return inv_dev * (weighted - mean_w - unit * mean_wn)


def core_here():
    return lax.axis_index("expert")


def segment_of(places, ends):
    return sum((places >= end).astype(jnp.int32) for end in ends)


def held(shape, dtype):
    return pltpu.VMEM(shape, dtype)


def there(shape, dtype):
    return jax.ShapeDtypeStruct(shape, dtype)


ANYWHERE = pl.BlockSpec(memory_space=pl.ANY)
INSIDE = pl.BlockSpec(memory_space=pltpu.VMEM)


class Program:
    def __init__(self):
        self.before = []

    def call(self, kernel, name, operands, out_shape, scratch=(), far=(), far_out=0, aliases=()):
        operands = [pltpu.with_memory_space_constraint(v, pltpu.VMEM) for v in operands]
        if not aliases:
            far = [pltpu.with_memory_space_constraint(v, pltpu.HBM) for v in far]
        count, waits = len(operands) + len(far), len(self.before)

        def run(*refs):
            kernel(*refs[:count], *refs[count + waits :])

        single = not isinstance(out_shape, (list, tuple))
        outs = [out_shape] if single else list(out_shape)
        near = len(outs) - far_out
        result = pl.pallas_call(
            run,
            in_specs=[INSIDE] * len(operands) + [ANYWHERE] * (len(far) + waits),
            out_specs=[INSIDE] * near + [ANYWHERE] * far_out,
            out_shape=outs,
            scratch_shapes=list(scratch),
            input_output_aliases={len(operands) + a: near + b for a, b in aliases},
            compiler_params=pltpu.CompilerParams(vmem_limit_bytes=VMEM_LIMIT),
            cost_estimate=pl.CostEstimate(flops=10**10, bytes_accessed=1, transcendentals=0),
            name=name,
        )(*operands, *far, *self.before)
        self.before = [result[0]]
        return result[0] if single else result


FIRST_GAIN, FIRST_BIAS, SECOND_GAIN, SECOND_BIAS, RETURN_BIAS, HIDDEN_BIAS = range(6)
SLOTS = 4
PARTS = 8


def bias_row(vecs, unit, cols):
    row = vecs[pl.ds(HIDDEN_BIAS + unit // 2, 1), :]
    return jnp.where(unit % 2 == 0, row[:, :cols], row[:, cols:])


def open_kernel(
    x_far, lengths_far, first_gain_far, first_bias_far, key_far, value_far, router_far, q_far,
    o_far, second_gain_far, second_bias_far, return_bias_far, hidden_bias_far, routes_far,
    normed, vecs, keys_ext, key_t, value_n, values_ext, logits, x, q_own, o_own, key_w, value_w,
    router_w, routes, ends_out,
    lengths, first_gain, first_bias, second_gain, second_bias, return_bias, hidden_bias, sems,
):
    spans = [slice(at, at + ROWS) for at in range(0, x.shape[0], ROWS)]
    moves = [(x_far.at[here, :], x.at[here, :]) for here in spans]
    needed = [
        (lengths_far, lengths), (first_gain_far, first_gain), (first_bias_far, first_bias),
        (key_far, key_w), (value_far, value_w), (router_far, router_w),
    ]
    later = [
        (q_far, q_own), (o_far, o_own), (second_gain_far, second_gain),
        (second_bias_far, second_bias), (return_bias_far, return_bias),
        (hidden_bias_far, hidden_bias), (routes_far.at[core_here()], routes),
    ]
    moves = moves[:1] + needed + moves[1:] + later
    copies = [pltpu.make_async_copy(*move, sems.at[j]) for j, move in enumerate(moves)]
    for copy in copies:
        copy.start()
    for copy in copies[: len(needed) + len(spans)]:
        copy.wait()
    head = key_w.shape[0]
    width = x.shape[1]
    ends, end = [], 0
    for slot in range(lengths.shape[1]):
        end = end + lengths[core_here(), slot]
        ends.append(end)
        ends_out[slot : slot + 1, :] = jnp.full((1, ends_out.shape[1]), end, jnp.int32)
    vecs[...] = jnp.zeros_like(vecs)
    for j, vec in enumerate((first_gain, first_bias)):
        vecs[j : j + 1, :] = wide(vec[...]).reshape(1, width)
    pair_w = jnp.concatenate([key_w[...], value_w[...]], axis=0)
    all_w = jnp.concatenate([key_w[...], value_w[...], router_w[...]], axis=0)
    for j, here in enumerate(spans):
        at = j * ROWS
        unit, _ = norm_parts(wide(x[here, :]))
        rows = low(
            unit * vecs[FIRST_GAIN : FIRST_GAIN + 1, :] + vecs[FIRST_BIAS : FIRST_BIAS + 1, :]
        )
        normed[here, :] = rows
        across = dot_nt(all_w, rows)
        key_t[:, here] = low(across[:head, :])
        values_ext[:head, here] = low(across[head : 2 * head, :])
        values_ext[head:, here] = jnp.ones((values_ext.shape[0] - head, ROWS), LOW)
        logits[:, here] = across[2 * head :, :]
        along = low(dot_nt(rows, pair_w))
        places = at + lax.broadcasted_iota(jnp.int32, (ROWS, head), 0)
        lanes = lax.broadcasted_iota(jnp.int32, (ROWS, head), 1)
        marks = low(jnp.where(segment_of(places, ends) == lanes, 1.0, 0.0))
        keys_ext[here, :] = jnp.concatenate([along[:, :head], marks], axis=1)
        value_n[here, :] = jnp.concatenate(
            [along[:, head:], jnp.ones((ROWS, head), LOW)], axis=1
        )
    for copy in copies[len(needed) + len(spans) :]:
        copy.wait()
    for j, vec in enumerate((second_gain, second_bias, return_bias)):
        vecs[SECOND_GAIN + j : SECOND_GAIN + j + 1, :] = wide(vec[...]).reshape(1, width)
    for j in range(hidden_bias.shape[0] // width):
        part = hidden_bias[j * width : (j + 1) * width]
        vecs[HIDDEN_BIAS + j : HIDDEN_BIAS + j + 1, :] = wide(part).reshape(1, width)


def expert_hits(route, experts):
    own = experts // 2
    relative = lax.rem(route - core_here() * own + experts, experts)
    return [relative == e for e in range(experts)]


def forward_kernel(
    normed, x, vecs, q_own, q_other, o_own, o_other, keys_ext, values_ext, logits, routes, ends_in,
    cot_far, hidden_w_far, return_w_far,
    exps, q_sel, attended, row_facts, placed, middle, hidden_in, hidden_in_t, d_feed, d_feed_t,
    bias_grad, cot, hidden_w, return_w, spread, sems,
):
    moves = ((cot_far, cot), (hidden_w_far, hidden_w), (return_w_far, return_w))
    copies = [pltpu.make_async_copy(*move, sems.at[j]) for j, move in enumerate(moves)]
    for copy in copies:
        copy.start()
    ends = [ends_in[slot, 0] for slot in range(SLOTS)]
    head = q_sel.shape[0]
    tok, half = x.shape[0], q_own.shape[0]
    experts = 2 * half // head
    own = experts // 2
    q_all = [low(dot_nt(q_own[...], normed[...])), low(dot_nt(q_other[...], normed[...]))]
    hits = [expert_hits(routes[m : m + 1, :], experts) for m in range(2)]
    places = lax.broadcasted_iota(jnp.int32, (head, tok), 1)
    subs = lax.broadcasted_iota(jnp.int32, (head, tok), 0)
    fence = low(jnp.where(segment_of(places, ends) == subs, 0.0, MASKED))
    for m in range(2):
        query = jnp.zeros((head, tok), LOW)
        for e in range(experts):
            from_e = q_all[e // own][(e % own) * head : (e % own + 1) * head, :]
            query = jnp.where(hits[m][e], from_e, query)
        lanes = slice(m * tok, (m + 1) * tok)
        q_sel[:, lanes] = query
        spread[:head, lanes] = low(wide(query) * head**-0.5)
        spread[head:, lanes] = fence

    def scores_of(at):
        return dot_nn(keys_ext[...], spread[:, at : at + SPAN])

    scores = scores_of(0)
    for at in range(0, 2 * tok, SPAN):
        later = scores_of(at + SPAN) if at + SPAN < 2 * tok else None
        here = slice(at, at + SPAN)
        powers = low(jnp.exp(scores - jnp.max(scores, axis=0, keepdims=True)))
        exps[:, here] = powers
        summed = dot_nn(values_ext[...], powers)
        inv = 1.0 / summed[head : head + 1, :]
        attended[:, here] = summed[:head, :] * inv
        row_facts[1:2, here] = inv
        scores = later
    ids = lax.broadcasted_iota(jnp.int32, (experts, tok), 0)
    chosen = [
        jnp.sum(jnp.where(ids == routes[m : m + 1, :], logits[...], 0.0), axis=0, keepdims=True)
        for m in range(2)
    ]
    top = jnp.maximum(chosen[0], chosen[1])
    lifts = [jnp.exp(c - top) for c in chosen]
    inv_sum = 1.0 / (lifts[0] + lifts[1])
    gated = []
    for m in range(2):
        lanes = slice(m * tok, (m + 1) * tok)
        gate = lifts[m] * inv_sum
        row_facts[0:1, lanes] = gate
        gated.append(attended[:, lanes] * gate)
    for e in range(experts):
        placed[e * head : (e + 1) * head, :] = low(
            jnp.where(hits[0][e], gated[0], jnp.where(hits[1][e], gated[1], 0.0))
        )
    copies[0].wait()
    total = jnp.zeros(bias_grad.shape, WIDE)
    for at in range(0, tok, SPAN):
        here = slice(at, at + SPAN)
        branch = dot_tn(placed[:half, here], o_own[...]) + dot_tn(placed[half:, here], o_other[...])
        spots = at + lax.broadcasted_iota(jnp.int32, (SPAN, 1), 0)
        mid = wide(x[here, :]) + jnp.where(spots < ends[-1], branch, 0.0)
        middle[here, :] = mid
        unit, _ = norm_parts(mid)
        hidden = (
            unit * vecs[SECOND_GAIN : SECOND_GAIN + 1, :] + vecs[SECOND_BIAS : SECOND_BIAS + 1, :]
        )
        hidden_in[here, :] = low(hidden)
        hidden_in_t[:, here] = low(hidden.T)
        masked = jnp.where(spots < ends[-1], wide(cot[here, :]), 0.0)
        d_feed[here, :] = low(masked)
        d_feed_t[:, here] = low(masked.T)
        total = total + jnp.sum(masked, axis=0, keepdims=True)
    bias_grad[...] = total
    for copy in copies[1:]:
        copy.wait()


def feed_kernel(
    units_of, joint, hidden_in, hidden_in_t, d_feed, d_feed_t, vecs, hidden_w, return_w, *outs
):
    units = units_of()
    grads_all = outs[-1] if joint else None
    for j, unit in enumerate(units):
        act, d_before, bias_grad = outs[3 * j : 3 * j + 3]
        cols = act.shape[1]
        at = rows_at(unit, cols)
        weight_in, weight_out = hidden_w[:, at], return_w[at, :]
        bias = bias_row(vecs, unit, cols)
        bias_sum = jnp.zeros(bias_grad.shape, WIDE)
        for row in range(0, act.shape[0], ROWS):
            here = slice(row, row + ROWS)
            x = dot_nn(hidden_in[here, :], weight_in) + bias
            d_act = dot_nt(d_feed[here, :], weight_out)
            squared = x * x
            rise = 0.5 + 0.5 * jnp.tanh(x * (CURVE + CURVE * CUBIC * squared))
            out = x * rise
            slope = rise + out * (1.0 - rise) * (2 * CURVE + 6 * CURVE * CUBIC * squared)
            act[here, :] = low(out)
            d_x = d_act * slope
            d_before[here, :] = low(d_x)
            bias_sum = bias_sum + jnp.sum(d_x, axis=0, keepdims=True)
        bias_grad[...] = bias_sum
        width = hidden_in.shape[1]
        rows = slice(j * width, (j + 1) * width)
        grads_all[rows, :cols] = low(dot_nn(hidden_in_t[...], d_before[...]))
        grads_all[rows, cols:] = low(dot_nn(d_feed_t[...], act[...]))


def spans_of(units, cols):
    return [rows_at(unit, cols) for unit in units]


def middle_kernel(units_of, *refs):
    d_befores, (hidden_w, vecs, middle, cot, ends_in) = refs[:PARTS], refs[PARTS : PARTS + 5]
    d_middle, d_low, gain_grad, bias_grad = refs[PARTS + 5 :]
    end = ends_in[SLOTS - 1, 0]
    spans = spans_of(units_of(), d_befores[0].shape[1])
    gain = vecs[SECOND_GAIN : SECOND_GAIN + 1, :]
    gain_sum = jnp.zeros(gain_grad.shape, WIDE)
    bias_sum = jnp.zeros(bias_grad.shape, WIDE)
    for at in range(0, middle.shape[0], ROWS):
        here = slice(at, at + ROWS)
        d_hidden = 0.0
        for part, span in zip(d_befores, spans):
            d_hidden = d_hidden + dot_nt(part[here, :], hidden_w[:, span])
        valid = at + lax.broadcasted_iota(jnp.int32, (ROWS, 1), 0) < end
        unit, inv = norm_parts(middle[here, :])
        d_mid = wide(cot[here, :]) + norm_back(d_hidden, unit, inv, gain)
        d_middle[here, :] = d_mid
        d_low[here, :] = low(jnp.where(valid, d_mid, 0.0))
        gain_sum = gain_sum + jnp.sum(d_hidden * unit, axis=0, keepdims=True)
        bias_sum = bias_sum + jnp.sum(d_hidden, axis=0, keepdims=True)
    gain_grad[...] = gain_sum
    bias_grad[...] = bias_sum


def write_out(near, far, here, sems, copies):
    copies.append(
        pltpu.make_async_copy(near.at[here, :], far.at[here, :], sems.at[len(copies)])
    )
    copies[-1].start()


def layer_kernel(units_of, *refs):
    acts, (return_w, vecs, middle, ends_in) = refs[:PARTS], refs[PARTS : PARTS + 4]
    token, far, near, sems = refs[PARTS + 4 :]
    token[...] = jnp.zeros_like(token)
    end = ends_in[SLOTS - 1, 0]
    spans = spans_of(units_of(), acts[0].shape[1])
    copies = []
    for at in range(0, middle.shape[0], ROWS):
        here = slice(at, at + ROWS)
        feed = vecs[RETURN_BIAS : RETURN_BIAS + 1, :]
        for part, span in zip(acts, spans):
            feed = feed + dot_nn(part[here, :], return_w[span, :])
        valid = at + lax.broadcasted_iota(jnp.int32, (ROWS, 1), 0) < end
        near[here, :] = middle[here, :] + jnp.where(valid, feed, 0.0)
        write_out(near, far, here, sems, copies)
    for copy in copies:
        copy.wait()


def attention_back_kernel(
    d_low, exps, q_sel, attended, row_facts, placed, key_t, value_n, o_own, o_other, routes,
    d_stack, grad_o, spread, d_scores, d_queries,
):
    head = key_t.shape[0]
    tok, half = d_low.shape[0], o_own.shape[0]
    experts = 2 * half // head
    own = experts // 2
    scale = head**-0.5
    d_all = [dot_nt(o_own[...], d_low[...]), dot_nt(o_other[...], d_low[...])]
    hits = [expert_hits(routes[m : m + 1, :], experts) for m in range(2)]
    halves = [slice(m * tok, (m + 1) * tok) for m in range(2)]
    gates = [row_facts[0:1, lanes] for lanes in halves]
    subs = lax.broadcasted_iota(jnp.int32, (head, tok), 0)
    d_gates = []
    for m, lanes in enumerate(halves):
        d_raw = jnp.zeros((head, tok), WIDE)
        for e in range(experts):
            from_e = d_all[e // own][(e % own) * head : (e % own + 1) * head, :]
            d_raw = jnp.where(hits[m][e], from_e, d_raw)
        att = attended[:, lanes]
        d_gates.append(jnp.sum(d_raw * att, axis=0, keepdims=True))
        d_att = low(d_raw * (gates[m] * row_facts[1:2, lanes]))
        inner = jnp.sum(wide(d_att) * att, axis=0, keepdims=True)
        inner_high = wide(low(inner))
        tail = jnp.where(subs == 0, -inner_high, jnp.where(subs == 1, inner_high - inner, 0.0))
        spread[:head, lanes] = d_att
        spread[head:, lanes] = low(tail)
    mean_gate = gates[0] * d_gates[0] + gates[1] * d_gates[1]
    ids = lax.broadcasted_iota(jnp.int32, (experts, tok), 0)
    d_logits = sum(
        jnp.where(ids == routes[m : m + 1, :], gates[m] * (d_gates[m] - mean_gate), 0.0)
        for m in range(2)
    )
    high = wide(low(d_logits))
    d_stack[2 * half + 2 * head :, :] = low(jnp.concatenate([high, d_logits - high], axis=0))

    def d_probs_of(at):
        return dot_nn(value_n[...], spread[:, at : at + ROWS])

    d_probs = d_probs_of(0)
    for at in range(0, 2 * tok, ROWS):
        later = d_probs_of(at + ROWS) if at + ROWS < 2 * tok else None
        here = slice(at, at + ROWS)
        d_score = low(wide(exps[:, here]) * d_probs)
        d_scores[:, here] = d_score
        d_queries[:, here] = dot_nn(key_t[...], d_score) * scale
        d_probs = later
    d_values = dot_nt(exps[...], spread[:head, :])
    d_keys = dot_nt(d_scores[...], q_sel[...]) * scale
    d_stack[2 * half : 2 * half + head, :] = low(d_keys.T)
    d_stack[2 * half + head : 2 * half + 2 * head, :] = low(d_values.T)
    first, second = d_queries[:, halves[0]], d_queries[:, halves[1]]
    for e in range(experts):
        d_stack[e * head : (e + 1) * head, :] = low(
            jnp.where(hits[0][e], first, jnp.where(hits[1][e], second, 0.0))
        )
    grad_o[...] = dot_nn(placed[...], d_low[...])


def close_kernel(
    units_of, d_stack, grad_o, q_own, q_other, normed, vecs, return_bias_grad, second_gain_grad,
    second_bias_grad, key_w, value_w, router_w, *rest,
):
    bias_parts, (own_grads, other_grads, common) = rest[:PARTS], rest[PARTS:]
    half, head, experts = q_own.shape[0], key_w.shape[0], router_w.shape[0]
    owned = at_kv = 2 * half
    rows_in = normed[...]
    parts = ((0, half, q_own[...]), (half, at_kv, q_other[...]))
    tail_w = jnp.concatenate([key_w[...], value_w[...], router_w[...], router_w[...]], axis=0)
    parts = parts + ((at_kv, d_stack.shape[0], tail_w),)
    bias_sum, product_sum, grads = 0.0, 0.0, []
    for start, stop, weights in parts:
        stack = d_stack[start:stop, :]
        grad = dot_nn(stack, rows_in)
        grads.append(grad)
        row_sums = jnp.sum(wide(stack), axis=1, keepdims=True)
        bias_sum = bias_sum + jnp.sum(row_sums * wide(weights), axis=0, keepdims=True)
        product_sum = product_sum + jnp.sum(grad * wide(weights), axis=0, keepdims=True)
    gain = vecs[FIRST_GAIN : FIRST_GAIN + 1, :]
    gain_sum = (product_sum - vecs[FIRST_BIAS : FIRST_BIAS + 1, :] * bias_sum) / gain
    own_grads[:half, :] = low(grads[0])
    other_grads[:half, :] = low(grads[1])
    own_grads[half:owned, :] = low(grad_o[:half, :])
    other_grads[half:owned, :] = low(grad_o[half:, :])
    tail = grads[2]
    common[...] = jnp.zeros_like(common)
    common[: 2 * head, :] = tail[: 2 * head, :]
    row = 2 * head
    common[row : row + experts, :] = (
        tail[2 * head : 2 * head + experts, :] + tail[2 * head + experts :, :]
    )
    row = row + experts
    rows = (gain_sum, bias_sum, second_gain_grad[...], second_bias_grad[...], return_bias_grad[...])
    for j, values in enumerate(rows):
        common[row + j : row + j + 1, :] = values
    for unit, part in zip(units_of(), bias_parts):
        cols = part.shape[1]
        at = pl.ds(row + HIDDEN_BIAS + unit // 2, 1)
        there_now = common[at, :]
        doubled = jnp.concatenate([part[...], part[...]], axis=1)
        lanes = lax.broadcasted_iota(jnp.int32, doubled.shape, 1)
        common[at, :] = jnp.where(lanes // cols == unit % 2, doubled, there_now)
    own_grads[owned:, :] = low(common[...])
    other_grads[owned:, :] = low(common[...])


def input_kernel(
    d_stack, q_own, q_other, key_w, value_w, router_w, x, d_middle, vecs,
    token, far, near, sems,
):
    token[...] = jnp.zeros_like(token)
    half = q_own.shape[0]
    at_kv = 2 * half
    tail_w = jnp.concatenate([key_w[...], value_w[...], router_w[...], router_w[...]], axis=0)
    gain = vecs[FIRST_GAIN : FIRST_GAIN + 1, :]
    copies = []
    for at in range(0, x.shape[0], ROWS):
        here = slice(at, at + ROWS)
        d_normed = dot_tn(d_stack[:half, here], q_own[...])
        d_normed = d_normed + dot_tn(d_stack[half:at_kv, here], q_other[...])
        d_normed = d_normed + dot_tn(d_stack[at_kv:, here], tail_w)
        unit, inv = norm_parts(wide(x[here, :]))
        near[here, :] = d_middle[here, :] + norm_back(d_normed, unit, inv, gain)
        write_out(near, far, here, sems, copies)
    for copy in copies:
        copy.wait()


def halvings(n_dp):
    return n_dp.bit_length() - 3


def step_orders(n_dp):
    first = list(range(halvings(n_dp)))
    second = []
    for at in range(0, len(first), 2):
        second += first[at : at + 2][::-1]
    return first, second


def pairs_of(n_dp, step):
    orders = step_orders(n_dp)
    return [
        (chip * 2 + core, (chip ^ (1 << orders[core][step])) * 2 + core)
        for chip in range(n_dp)
        for core in range(2)
    ]


def quad_pairs(n_dp, turn):
    return [
        (chip * 2 + core, (chip ^ (turn << halvings(n_dp))) * 2 + core)
        for chip in range(n_dp)
        for core in range(2)
    ]


def cross_pairs(n_dp, turn):
    low_bit = halvings(n_dp)
    return [
        (chip * 2 + core, (chip ^ (1 << (low_bit + turn))) * 2 + core)
        for chip in range(n_dp)
        for core in range(2)
    ]


def core_swap(values, n_dp):
    return lax.ppermute(values, AXES, [(at, at ^ 1) for at in range(2 * n_dp)])


def bit_here(n_dp, step, core=None):
    first, second = step_orders(n_dp)
    chip = lax.axis_index("dp")
    core = core_here() if core is None else core
    return jnp.where(core == 0, chip >> first[step], chip >> second[step]) & 1


def units_here(n_dp, entries):
    core = core_here()
    mine, theirs = bit_here(n_dp, 0), bit_here(n_dp, 0, 1 - core)
    other = 1 - core
    blocks = [2 * other + 1 - theirs, 2 * core + 1 - mine, 2 * other + theirs, 2 * core + mine]
    return [2 * blocks[entry // 2] + entry % 2 for entry in entries]


def rows_at(index, size):
    return pl.ds(pl.multiple_of(index * size, size), size)


def add_kernel(*refs):
    total = wide(refs[0][...])
    for ref in refs[1:-1]:
        total = total + wide(ref[...])
    refs[-1][...] = low(total)


def rows_of(ref, at, size):
    return wide(ref[pl.ds(pl.multiple_of(at, size), size), :])


def partial_sum(n_dp, terms, step, last_kept):
    start = step - len(terms) + 1
    size = terms[0][0].shape[0] >> (step - start + 1)
    at, total = 0, 0.0
    for j in range(step, start - 1, -1):
        bit = bit_here(n_dp, j)
        bit = bit if last_kept or j < step else 1 - bit
        at = at + bit * (size << (step - j))
        for ref in terms[j - start]:
            total = total + rows_of(ref, at, size)
    return total


def group(refs, counts):
    refs = list(refs)
    return [[refs.pop(0) for _ in range(count)] for count in counts]


def split_terms(terms, joint):
    parts = []
    for part in range(2):
        chosen = []
        for refs, flags in zip(terms, joint):
            chosen.append([])
            for ref, flag in zip(refs, flags):
                half = ref.shape[0] // 2
                if flag == 2:
                    chosen[-1].append(ref.at[pl.ds(part * half, half), :])
                elif flag == part:
                    chosen[-1].append(ref)
        parts.append(chosen)
    return parts


def send_kernel(n_dp, step, counts, joint, *refs):
    out = refs[-1]
    terms = group(refs[:-1], counts)
    if joint is None:
        out[...] = low(partial_sum(n_dp, terms, step, False))
        return
    size = out.shape[0] // 2
    for part, chosen in enumerate(split_terms(terms, joint)):
        out[part * size : (part + 1) * size, :] = low(partial_sum(n_dp, chosen, step, False))


def kept_kernel(n_dp, step, counts, *refs):
    *terms, last = group(refs[:-1], counts)
    refs[-1][...] = low(partial_sum(n_dp, terms, step, True) + wide(last[0][...]))


def spot_here(n_dp, turn):
    return jnp.bitwise_xor(lax.axis_index("dp") >> halvings(n_dp), turn)


def quarters_kernel(n_dp, step, counts, joint, *refs):
    count = sum(counts)
    terms = group(refs[:count], counts)
    outs, total = refs[count:-1], refs[-1]
    size = total.shape[0] // 2
    for part, (*chosen, last) in enumerate(split_terms(terms, joint)):
        total[part * size : (part + 1) * size, :] = partial_sum(
            n_dp, chosen, step, True
        ) + wide(last[0][...])
    cols = outs[0].shape[1]
    for turn, out in enumerate(outs):
        out[...] = low(total[:, rows_at(spot_here(n_dp, turn), cols)])


def row_of_four(n_dp, part, *refs):
    pieces, out = refs[:4], refs[4]
    size, cols = out.shape[0], pieces[0].shape[1]
    for turn, piece in enumerate(pieces):
        at = rows_at(spot_here(n_dp, turn), cols)
        out[:, at] = piece[part * size : (part + 1) * size, :]


def join_kernel(n_dp, step, mine, got, out):
    size = mine.shape[0]
    bit = bit_here(n_dp, step)
    out[rows_at(bit, size), :] = mine[...]
    out[rows_at(1 - bit, size), :] = got[...]


def place_kernel(units_of, count, more, *refs):
    hidden, returned, left, right, sems = refs[-5:]
    copies = []
    for j, (unit, part) in enumerate(zip(units_of(), refs[:count])):
        cols = part.shape[1] // 2
        at = rows_at(unit, cols)
        left[j] = wide(part[:, :cols])
        copies.append(pltpu.make_async_copy(left.at[j], hidden.at[:, at], sems.at[2 * j]))
        copies[-1].start()
        right[j] = wide(part[:, cols:]).T
        copies.append(pltpu.make_async_copy(right.at[j], returned.at[at, :], sems.at[2 * j + 1]))
        copies[-1].start()
    if more:
        refs[-6][...] = refs[0][...]
    for copy in copies:
        copy.wait()


def finish_kernel(n_dp, mine, got, token, query_g, output_g, key_g, value_g, router_g, *refs):
    vectors, whole = refs[:-1], refs[-1]
    token[...] = jnp.zeros_like(token)
    size, width = mine.shape
    bit = bit_here(n_dp, 0)
    whole[rows_at(bit, size), :] = wide(mine[...])
    whole[rows_at(1 - bit, size), :] = wide(got[...])
    row = 0
    for out in (query_g, output_g, key_g, value_g, router_g):
        out[...] = whole[row : row + out.shape[0], :]
        row = row + out.shape[0]
    for j, vector in enumerate(vectors[:-1]):
        vector[...] = whole[row + j, :]
    row = row + len(vectors) - 1
    for j in range(vectors[-1].shape[0] // width):
        vectors[-1][j * width : (j + 1) * width] = whole[row + j, :]


def local(
    inputs, cotangent, lengths, routes, first_gain, first_bias, router_weight, key_weight,
    value_weight, query_weight, output_weight, second_gain, second_bias, hidden_weight,
    hidden_bias, return_weight, return_bias,
):
    tok, width = inputs.shape
    ff = hidden_weight.shape[1]
    n_dp = lax.axis_size("dp")
    own, _, head = query_weight.shape
    experts = 2 * own
    half = own * head
    blocks = tok // ROWS

    q_own = jnp.transpose(query_weight, (0, 2, 1)).reshape(half, width)
    o_own = output_weight.reshape(half, width)
    q_other, o_other = core_swap(q_own, n_dp), core_swap(o_own, n_dp)
    vec_rows = 5 + ff // width
    program = Program()
    call = program.call
    (
        normed, vecs, keys_ext, key_t, value_n, values_ext, logits, x, q_own, o_own, key_w, value_w,
        router_w, routes, ends,
    ) = call(
        open_kernel, "first_norm", [],
        [
            held((tok, width), LOW), held((vec_rows + -vec_rows % 8, width), WIDE),
            held((tok, 2 * head), LOW), held((head, tok), LOW), held((tok, 2 * head), LOW),
            held((head + 16, tok), LOW), held((experts, tok), WIDE), held((tok, width), LOW),
            held((half, width), LOW), held((half, width), LOW), held((head, width), LOW),
            held((head, width), LOW), held((experts, width), LOW), held((2, tok), jnp.int32),
            held((8, 128), jnp.int32),
        ],
        scratch=[pltpu.SMEM(lengths.shape[1:], jnp.int32)]
        + [pltpu.VMEM((width,), LOW)] * 5
        + [pltpu.VMEM((ff,), LOW), pltpu.SemaphoreType.DMA((blocks + 13,))],
        far=[
            inputs, lengths[0], first_gain, first_bias, key_weight.T, value_weight.T,
            router_weight.T, q_own, o_own, second_gain, second_bias, return_bias, hidden_bias,
            jnp.transpose(routes[0], (0, 2, 1)),
        ],
    )
    (
        exps, q_sel, attended, row_facts, placed, middle, hidden_in, hidden_in_t, d_feed, d_feed_t,
        return_bias_grad, cot, hidden_w, return_w,
    ) = call(
        forward_kernel, "attention_forward",
        [
            normed, x, vecs, q_own, q_other, o_own, o_other, keys_ext, values_ext, logits, routes,
            ends,
        ],
        [
            held((tok, 2 * tok), LOW), held((head, 2 * tok), LOW), held((head, 2 * tok), WIDE),
            held((8, 2 * tok), WIDE), held((2 * half, tok), LOW), held((tok, width), WIDE),
            held((tok, width), LOW), held((width, tok), LOW), held((tok, width), LOW),
            held((width, tok), LOW), held((1, width), WIDE), held((tok, width), LOW),
            held(hidden_weight.shape, LOW), held(return_weight.shape, LOW),
        ],
        scratch=[pltpu.VMEM((2 * head, 2 * tok), LOW), pltpu.SemaphoreType.DMA((3,))],
        far=[cotangent, hidden_weight, return_weight],
    )

    cols = ff // PARTS
    units = lambda *entries: functools.partial(units_here, n_dp, entries)
    steps = halvings(n_dp)

    def feed(*entries):
        outs = call(
            functools.partial(feed_kernel, units(*entries), True), f"feed_{entries[0]}",
            [hidden_in, hidden_in_t, d_feed, d_feed_t, vecs, hidden_w, return_w],
            [held((tok, cols), LOW), held((tok, cols), LOW), held((1, cols), WIDE)] * len(entries)
            + [there((len(entries) * width, 2 * cols), LOW)],
        )
        return list(zip(*[iter(outs[:-1])] * 3)), outs[-1]

    def add(name, *terms):
        return call(add_kernel, name, terms, there(terms[0].shape, LOW))

    parts_a, theirs_a = feed(0)
    parts_b, theirs_b = feed(1)
    swap_a, swap_b = core_swap(theirs_a, n_dp), core_swap(theirs_b, n_dp)
    parts_c, mine_a = feed(2)
    sent_a = lax.ppermute(add("feed_add_0", mine_a, swap_a), AXES, pairs_of(n_dp, 0))
    parts_d, mine_b = feed(3)
    sent_b = lax.ppermute(add("feed_add_1", mine_b, swap_b), AXES, pairs_of(n_dp, 0))
    parts_e, theirs = feed(4, 5)
    swapped = core_swap(theirs, n_dp)
    parts_f, mine = feed(6, 7)
    parts = parts_a + parts_b + parts_c + parts_d + parts_e + parts_f

    every = units(*range(PARTS))
    d_middle, d_low, second_gain_grad, second_bias_grad = call(
        functools.partial(middle_kernel, every), "second_norm_back",
        [p[1] for p in parts] + [hidden_w, vecs, middle, cot, ends],
        [
            held((tok, width), WIDE), held((tok, width), LOW), held((1, width), WIDE),
            held((1, width), WIDE),
        ],
    )

    feed_terms, feed_joint = [[sent_a, sent_b, swapped, mine]], [[0, 1, 2, 2]]

    def feed_send(step):
        counts = [len(t) for t in feed_terms]
        part = call(
            functools.partial(send_kernel, n_dp, step, counts, list(feed_joint)),
            f"feed_send_{step}", sum(feed_terms, []), there((2 * width >> step, 2 * cols), LOW),
        )
        feed_terms.append([lax.ppermute(part, AXES, pairs_of(n_dp, step))])
        feed_joint.append([2])

    for step in range(1, steps):
        feed_send(step)
    d_stack, grad_o = call(
        attention_back_kernel, "attention_backward",
        [d_low, exps, q_sel, attended, row_facts, placed, key_t, value_n, o_own, o_other, routes],
        [held((2 * half + 2 * head + 2 * experts, tok), LOW), held((2 * half, width), WIDE)],
        scratch=[
            pltpu.VMEM((2 * head, 2 * tok), LOW), pltpu.VMEM((tok, 2 * tok), LOW),
            pltpu.VMEM((head, 2 * tok), WIDE),
        ],
    )
    shared = 2 * head + experts + 5 + ff // width
    shared = shared + -(2 * half + shared) % (16 << steps)
    rows = 2 * half + shared
    own_grads, other_grads = call(
        functools.partial(close_kernel, every), "projection_grads",
        [
            d_stack, grad_o, q_own, q_other, normed, vecs, return_bias_grad, second_gain_grad,
            second_bias_grad, key_w, value_w, router_w, *[p[2] for p in parts],
        ],
        [there((rows, width), LOW), there((rows, width), LOW)],
        scratch=[pltpu.VMEM((shared, width), WIDE)],
    )

    def output(kernel, name, operands):
        _, out = call(
            kernel, name, operands, [held((8, 128), WIDE), there((tok, width), WIDE)],
            scratch=[pltpu.VMEM((tok, width), WIDE), pltpu.SemaphoreType.DMA((blocks,))],
            far_out=1,
        )
        return out

    rest_terms = [[own_grads, core_swap(other_grads, n_dp)]]
    counts = [len(t) for t in feed_terms]
    own_piece, *pieces = call(
        functools.partial(quarters_kernel, n_dp, steps - 1, counts, feed_joint), "feed_cut",
        sum(feed_terms, []), [there((2 * width >> (steps - 1), cols // 2), LOW)] * 4,
        scratch=[pltpu.VMEM((2 * width >> (steps - 1), 2 * cols), WIDE)],
    )

    def across(values):
        return [
            lax.ppermute(v, AXES, quad_pairs(n_dp, t + 1)) for t, v in enumerate(values)
        ]

    pieces = across(pieces)


    def rest_send(step):
        counts = [len(t) for t in rest_terms]
        part = call(
            functools.partial(send_kernel, n_dp, step, counts, None), f"rest_send_{step}",
            sum(rest_terms, []), there((rows >> (step + 1), width), LOW),
        )
        rest_terms.append([lax.ppermute(part, AXES, pairs_of(n_dp, step))])

    def join(name, step, mine, got):
        size, wide_cols = mine.shape
        kernel = functools.partial(join_kernel, n_dp, step)
        joined = call(kernel, name, [mine, got], there((2 * size, wide_cols), LOW))
        return joined, lax.ppermute(joined, AXES, pairs_of(n_dp, step - 1))

    written = None

    def place(name, entries, values, more=True):
        nonlocal written
        count = len(values)
        *copied, one, two = call(
            functools.partial(place_kernel, units(*entries), count, more), name, values,
            [there(values[0].shape, LOW)] * more
            + [there((width, ff), WIDE), there((ff, width), WIDE)],
            scratch=[
                pltpu.VMEM((count, width, cols), WIDE), pltpu.VMEM((count, cols, width), WIDE),
                pltpu.SemaphoreType.DMA((2 * count,)),
            ],
            far=[] if written is None else written,
            far_out=2,
            aliases=[] if written is None else [(0, 0), (1, 1)],
        )
        written = [one, two]
        return copied[0] if more else None

    rest_send(0)
    layer_out = output(
        functools.partial(layer_kernel, every), "layer_out",
        [p[0] for p in parts] + [return_w, vecs, middle, ends],
    )
    for step in range(1, steps):
        rest_send(step)
    own_piece = add("feed_sum", own_piece, *pieces)
    pieces = across([own_piece] * 3)
    counts = [len(t) for t in rest_terms]
    rest = call(
        functools.partial(kept_kernel, n_dp, steps - 1, counts), "rest_sum", sum(rest_terms, []),
        there((rows >> steps, width), LOW),
    )
    rest_got = lax.ppermute(rest, AXES, cross_pairs(n_dp, 0))
    input_grad = output(
        input_kernel, "first_norm_back",
        [d_stack, q_own, q_other, key_w, value_w, router_w, x, d_middle, vecs],
    )
    size = own_piece.shape[0] // 2
    joined, got, others = [None] * 2, [None] * 2, []
    for part in range(2):
        joined[part] = call(
            functools.partial(row_of_four, n_dp, part), f"feed_row_{part}", [own_piece] + pieces,
            there((size, 2 * cols), LOW),
        )
        got[part] = lax.ppermute(joined[part], AXES, pairs_of(n_dp, steps - 1))
    rest = add("rest_add_0", rest, rest_got)
    rest_got = lax.ppermute(rest, AXES, cross_pairs(n_dp, 1))
    for step in reversed(range(1, steps)):
        for part in range(2):
            name = f"feed_join_{step}_{part}"
            joined[part], got[part] = join(name, step, joined[part], got[part])
            if step == 1:
                copied = place(f"place_own_{part}", (6 + part,), [joined[part]])
                others.append(core_swap(copied, n_dp))
    rest = add("rest_add_1", rest, rest_got)
    rest_got = lax.ppermute(rest, AXES, pairs_of(n_dp, steps - 1))
    place("place_other", (4, 5), others)
    place("place_got_0", (2,), got[:1])
    for step in reversed(range(1, steps)):
        rest, rest_got = join(f"rest_join_{step}", step, rest, rest_got)
    place("place_got_1", (3,), got[1:])
    place("place_far", (0, 1), [core_swap(row, n_dp) for row in got])
    vectors = [there((width,), WIDE)] * 5 + [there((ff,), WIDE)]
    _, query_grad, output_grad, key_g, value_g, router_g, fg, fb, sg, sb, rb, hb = call(
        functools.partial(finish_kernel, n_dp), "finish", [rest, rest_got],
        [held((8, 128), WIDE)] + [there((half, width), WIDE)] * 2 + [there((head, width), WIDE)] * 2
        + [there((experts, width), WIDE)] + vectors,
        scratch=[pltpu.VMEM((rows, width), WIDE)],
    )
    hidden_grad, return_grad = written
    return (
        layer_out,
        input_grad,
        fg,
        fb,
        router_g.T,
        key_g.T,
        value_g.T,
        jnp.transpose(query_grad.reshape(-1, head, width), (0, 2, 1)),
        output_grad.reshape(-1, head, width),
        sg,
        sb,
        hidden_grad,
        hb,
        return_grad,
        rb,
    )


def solution(mesh):
    rows = P(AXES, None)
    cut = P("expert", None, None)
    in_specs = (
        (rows, rows, P("dp", None, None), P("dp", None, None, None))
        + (P(),) * 5
        + (cut, cut)
        + (P(),) * 6
    )
    out_specs = (rows, rows) + (P(),) * 5 + (cut, cut) + (P(),) * 6
    return jax.shard_map(local, mesh=mesh, in_specs=in_specs, out_specs=out_specs, check_vma=False)
```

```python
import functools

import jax
import jax.numpy as jnp
from jax import lax
from jax.experimental import pallas as pl
from jax.experimental.pallas import tpu as pltpu
from jax.sharding import PartitionSpec as P

AXES = ("dp", "expert")
WIDE = jnp.float32
LOW = jnp.bfloat16
EPS = 1e-05
MASKED = -1e30
REACH = 40.0
ROWS = 256
SPAN = 512
CURVE = 0.7978845608028654
CUBIC = 0.044715
VMEM_LIMIT = 16 * 1024 * 1024


def low(values):
    return values.astype(LOW)


def wide(values):
    return values.astype(WIDE)


def dot_nn(left_op, right_op):
    return lax.dot_general(
        left_op, right_op, (((1,), (0,)), ((), ())), preferred_element_type=WIDE
    )


def dot_tn(left_op, right_op):
    return lax.dot_general(
        left_op, right_op, (((0,), (0,)), ((), ())), preferred_element_type=WIDE
    )


def dot_nt(left_op, right_op):
    return lax.dot_general(
        left_op, right_op, (((1,), (1,)), ((), ())), preferred_element_type=WIDE
    )


def norm_parts(values):
    row_mean = jnp.mean(values, axis=-1, keepdims=True)
    centred = values - row_mean
    inv_dev = lax.rsqrt(jnp.mean(centred * centred, axis=-1, keepdims=True) + EPS)
    return centred * inv_dev, inv_dev


def norm_back(d_out, unit, inv_dev, gain_vec):
    weighted = d_out * gain_vec
    mean_w = jnp.mean(weighted, axis=-1, keepdims=True)
    mean_wn = jnp.mean(weighted * unit, axis=-1, keepdims=True)
    return inv_dev * (weighted - mean_w - unit * mean_wn)


def core_here():
    return lax.axis_index("expert")


def segment_of(places, ends):
    return sum((places >= end).astype(jnp.int32) for end in ends)


def held(shape, dtype):
    return pltpu.VMEM(shape, dtype)


def there(shape, dtype):
    return jax.ShapeDtypeStruct(shape, dtype)


ANYWHERE = pl.BlockSpec(memory_space=pl.ANY)
INSIDE = pl.BlockSpec(memory_space=pltpu.VMEM)


class Program:
    def __init__(self):
        self.before = []

    def call(self, kernel, name, operands, out_shape, scratch=(), far=(), far_out=0, aliases=()):
        operands = [pltpu.with_memory_space_constraint(v, pltpu.VMEM) for v in operands]
        if not aliases:
            far = [pltpu.with_memory_space_constraint(v, pltpu.HBM) for v in far]
        count, waits = len(operands) + len(far), len(self.before)

        def run(*refs):
            kernel(*refs[:count], *refs[count + waits :])

        single = not isinstance(out_shape, (list, tuple))
        outs = [out_shape] if single else list(out_shape)
        near = len(outs) - far_out
        result = pl.pallas_call(
            run,
            in_specs=[INSIDE] * len(operands) + [ANYWHERE] * (len(far) + waits),
            out_specs=[INSIDE] * near + [ANYWHERE] * far_out,
            out_shape=outs,
            scratch_shapes=list(scratch),
            input_output_aliases={len(operands) + a: near + b for a, b in aliases},
            compiler_params=pltpu.CompilerParams(vmem_limit_bytes=VMEM_LIMIT),
            cost_estimate=pl.CostEstimate(flops=3 * 10**10 if name == "rest_add_1" else 10**10, bytes_accessed=1, transcendentals=0),
            name=name,
        )(*operands, *far, *self.before)
        self.before = [result[0]]
        return result[0] if single else result


FIRST_GAIN, FIRST_BIAS, SECOND_GAIN, SECOND_BIAS, RETURN_BIAS, HIDDEN_BIAS = range(6)
SLOTS = 4
PARTS = 8


def bias_row(vecs, unit, cols):
    row = vecs[pl.ds(HIDDEN_BIAS + unit // 2, 1), :]
    return jnp.where(unit % 2 == 0, row[:, :cols], row[:, cols:])


def open_kernel(
    x_far, lengths_far, first_gain_far, first_bias_far, key_far, value_far, router_far, q_far,
    o_far, second_gain_far, second_bias_far, return_bias_far, hidden_bias_far, routes_far,
    normed, vecs, keys_ext, key_t, value_n, values_ext, logits, x, q_own, o_own, key_w, value_w,
    router_w, routes, ends_out,
    lengths, first_gain, first_bias, second_gain, second_bias, return_bias, hidden_bias, sems,
):
    spans = [slice(at, at + ROWS) for at in range(0, x.shape[0], ROWS)]
    moves = [(x_far.at[here, :], x.at[here, :]) for here in spans]
    needed = [
        (lengths_far, lengths), (first_gain_far, first_gain), (first_bias_far, first_bias),
        (key_far, key_w), (value_far, value_w), (router_far, router_w),
    ]
    later = [
        (q_far, q_own), (o_far, o_own), (second_gain_far, second_gain),
        (second_bias_far, second_bias), (return_bias_far, return_bias),
        (hidden_bias_far, hidden_bias), (routes_far.at[core_here()], routes),
    ]
    moves = moves[:1] + needed + moves[1:] + later
    copies = [pltpu.make_async_copy(*move, sems.at[j]) for j, move in enumerate(moves)]
    for copy in copies:
        copy.start()
    for copy in copies[: len(needed) + len(spans)]:
        copy.wait()
    head = key_w.shape[0]
    width = x.shape[1]
    ends, end = [], 0
    for slot in range(lengths.shape[1]):
        end = end + lengths[core_here(), slot]
        ends.append(end)
        ends_out[slot : slot + 1, :] = jnp.full((1, ends_out.shape[1]), end, jnp.int32)
    vecs[...] = jnp.zeros_like(vecs)
    for j, vec in enumerate((first_gain, first_bias)):
        vecs[j : j + 1, :] = wide(vec[...]).reshape(1, width)
    pair_w = jnp.concatenate([key_w[...], value_w[...]], axis=0)
    all_w = jnp.concatenate([key_w[...], value_w[...], router_w[...]], axis=0)
    for j, here in enumerate(spans):
        at = j * ROWS
        unit, _ = norm_parts(wide(x[here, :]))
        rows = low(
            unit * vecs[FIRST_GAIN : FIRST_GAIN + 1, :] + vecs[FIRST_BIAS : FIRST_BIAS + 1, :]
        )
        normed[here, :] = rows
        across = dot_nt(all_w, rows)
        key_t[:, here] = low(across[:head, :])
        values_ext[:head, here] = low(across[head : 2 * head, :])
        values_ext[head:, here] = jnp.ones((values_ext.shape[0] - head, ROWS), LOW)
        logits[:, here] = across[2 * head :, :]
        along = low(dot_nt(rows, pair_w))
        places = at + lax.broadcasted_iota(jnp.int32, (ROWS, head), 0)
        lanes = lax.broadcasted_iota(jnp.int32, (ROWS, head), 1)
        marks = low(jnp.where(segment_of(places, ends) == lanes, 1.0, 0.0))
        keys_ext[here, :] = jnp.concatenate([along[:, :head], marks], axis=1)
        value_n[here, :] = jnp.concatenate(
            [along[:, head:], jnp.ones((ROWS, head), LOW)], axis=1
        )
    for copy in copies[len(needed) + len(spans) :]:
        copy.wait()
    for j, vec in enumerate((second_gain, second_bias, return_bias)):
        vecs[SECOND_GAIN + j : SECOND_GAIN + j + 1, :] = wide(vec[...]).reshape(1, width)
    for j in range(hidden_bias.shape[0] // width):
        part = hidden_bias[j * width : (j + 1) * width]
        vecs[HIDDEN_BIAS + j : HIDDEN_BIAS + j + 1, :] = wide(part).reshape(1, width)


def expert_hits(route, experts):
    own = experts // 2
    relative = lax.rem(route - core_here() * own + experts, experts)
    return [relative == e for e in range(experts)]


def forward_kernel(
    normed, x, vecs, q_own, q_other, o_own, o_other, keys_ext, values_ext, logits, routes, ends_in,
    key_t, cot_far, hidden_w_far, return_w_far,
    exps, q_sel, attended, row_facts, placed, middle, hidden_in, hidden_in_t, d_feed, d_feed_t,
    bias_grad, cot, hidden_w, return_w, spread, sems,
):
    moves = ((cot_far, cot), (hidden_w_far, hidden_w), (return_w_far, return_w))
    copies = [pltpu.make_async_copy(*move, sems.at[j]) for j, move in enumerate(moves)]
    for copy in copies:
        copy.start()
    ends = [ends_in[slot, 0] for slot in range(SLOTS)]
    head = q_sel.shape[0]
    tok, half = x.shape[0], q_own.shape[0]
    experts = 2 * half // head
    own = experts // 2
    q_all = [low(dot_nt(q_own[...], normed[...])), low(dot_nt(q_other[...], normed[...]))]
    hits = [expert_hits(routes[m : m + 1, :], experts) for m in range(2)]
    places = lax.broadcasted_iota(jnp.int32, (head, tok), 1)
    subs = lax.broadcasted_iota(jnp.int32, (head, tok), 0)
    fence = low(jnp.where(segment_of(places, ends) == subs, 0.0, MASKED))
    for m in range(2):
        query = jnp.zeros((head, tok), LOW)
        for e in range(experts):
            from_e = q_all[e // own][(e % own) * head : (e % own + 1) * head, :]
            query = jnp.where(hits[m][e], from_e, query)
        lanes = slice(m * tok, (m + 1) * tok)
        q_sel[:, lanes] = query
        spread[:head, lanes] = low(wide(query) * head**-0.5)
        spread[head:, lanes] = fence

    def scores_of(at):
        return dot_nn(keys_ext[...], spread[:, at : at + SPAN])

    def attend(at, powers):
        here = slice(at, at + SPAN)
        exps[:, here] = powers
        summed = dot_nn(values_ext[...], powers)
        inv = 1.0 / summed[head : head + 1, :]
        attended[:, here] = summed[:head, :] * inv
        row_facts[1:2, here] = inv

    longest_query = jnp.max(jnp.sum(jnp.square(wide(spread[:head, :])), axis=0, keepdims=True))
    longest_key = jnp.max(jnp.sum(jnp.square(wide(key_t[...])), axis=0, keepdims=True))
    within = longest_query * longest_key < REACH * REACH

    @pl.when(within)
    def _():
        for at in range(0, 2 * tok, SPAN):
            attend(at, low(jnp.exp(scores_of(at))))

    @pl.when(jnp.logical_not(within))
    def _():
        for at in range(0, 2 * tok, SPAN):
            scores = scores_of(at)
            attend(at, low(jnp.exp(scores - jnp.max(scores, axis=0, keepdims=True))))

    ids = lax.broadcasted_iota(jnp.int32, (experts, tok), 0)
    chosen = [
        jnp.sum(jnp.where(ids == routes[m : m + 1, :], logits[...], 0.0), axis=0, keepdims=True)
        for m in range(2)
    ]
    top = jnp.maximum(chosen[0], chosen[1])
    lifts = [jnp.exp(c - top) for c in chosen]
    inv_sum = 1.0 / (lifts[0] + lifts[1])
    gated = []
    for m in range(2):
        lanes = slice(m * tok, (m + 1) * tok)
        gate = lifts[m] * inv_sum
        row_facts[0:1, lanes] = gate
        gated.append(attended[:, lanes] * gate)
    for e in range(experts):
        placed[e * head : (e + 1) * head, :] = low(
            jnp.where(hits[0][e], gated[0], jnp.where(hits[1][e], gated[1], 0.0))
        )
    copies[0].wait()
    total = jnp.zeros(bias_grad.shape, WIDE)
    for at in range(0, tok, SPAN):
        here = slice(at, at + SPAN)
        branch = dot_tn(placed[:half, here], o_own[...]) + dot_tn(placed[half:, here], o_other[...])
        spots = at + lax.broadcasted_iota(jnp.int32, (SPAN, 1), 0)
        mid = wide(x[here, :]) + jnp.where(spots < ends[-1], branch, 0.0)
        middle[here, :] = mid
        unit, _ = norm_parts(mid)
        hidden = (
            unit * vecs[SECOND_GAIN : SECOND_GAIN + 1, :] + vecs[SECOND_BIAS : SECOND_BIAS + 1, :]
        )
        hidden_in[here, :] = low(hidden)
        hidden_in_t[:, here] = low(hidden.T)
        masked = jnp.where(spots < ends[-1], wide(cot[here, :]), 0.0)
        d_feed[here, :] = low(masked)
        d_feed_t[:, here] = low(masked.T)
        total = total + jnp.sum(masked, axis=0, keepdims=True)
    bias_grad[...] = total
    for copy in copies[1:]:
        copy.wait()


def feed_kernel(
    units_of, joint, hidden_in, hidden_in_t, d_feed, d_feed_t, vecs, hidden_w, return_w, *outs
):
    units = units_of()
    grads_all = outs[-1] if joint else None
    for j, unit in enumerate(units):
        act, d_before, bias_grad = outs[3 * j : 3 * j + 3]
        cols = act.shape[1]
        at = rows_at(unit, cols)
        weight_in, weight_out = hidden_w[:, at], return_w[at, :]
        bias = bias_row(vecs, unit, cols)
        bias_sum = jnp.zeros(bias_grad.shape, WIDE)
        for row in range(0, act.shape[0], ROWS):
            here = slice(row, row + ROWS)
            x = dot_nn(hidden_in[here, :], weight_in) + bias
            d_act = dot_nt(d_feed[here, :], weight_out)
            squared = x * x
            rise = 0.5 + 0.5 * jnp.tanh(x * (CURVE + CURVE * CUBIC * squared))
            out = x * rise
            slope = rise + out * (1.0 - rise) * (2 * CURVE + 6 * CURVE * CUBIC * squared)
            act[here, :] = low(out)
            d_x = d_act * slope
            d_before[here, :] = low(d_x)
            bias_sum = bias_sum + jnp.sum(d_x, axis=0, keepdims=True)
        bias_grad[...] = bias_sum
        width = hidden_in.shape[1]
        rows = slice(j * width, (j + 1) * width)
        grads_all[rows, :cols] = low(dot_nn(hidden_in_t[...], d_before[...]))
        grads_all[rows, cols:] = low(dot_nn(d_feed_t[...], act[...]))


def spans_of(units, cols):
    return [rows_at(unit, cols) for unit in units]


def middle_kernel(units_of, *refs):
    d_befores, (hidden_w, vecs, middle, cot, ends_in) = refs[:PARTS], refs[PARTS : PARTS + 5]
    d_middle, d_low, gain_grad, bias_grad = refs[PARTS + 5 :]
    end = ends_in[SLOTS - 1, 0]
    spans = spans_of(units_of(), d_befores[0].shape[1])
    gain = vecs[SECOND_GAIN : SECOND_GAIN + 1, :]
    gain_sum = jnp.zeros(gain_grad.shape, WIDE)
    bias_sum = jnp.zeros(bias_grad.shape, WIDE)
    for at in range(0, middle.shape[0], ROWS):
        here = slice(at, at + ROWS)
        d_hidden = 0.0
        for part, span in zip(d_befores, spans):
            d_hidden = d_hidden + dot_nt(part[here, :], hidden_w[:, span])
        valid = at + lax.broadcasted_iota(jnp.int32, (ROWS, 1), 0) < end
        unit, inv = norm_parts(middle[here, :])
        d_mid = wide(cot[here, :]) + norm_back(d_hidden, unit, inv, gain)
        d_middle[here, :] = d_mid
        d_low[here, :] = low(jnp.where(valid, d_mid, 0.0))
        gain_sum = gain_sum + jnp.sum(d_hidden * unit, axis=0, keepdims=True)
        bias_sum = bias_sum + jnp.sum(d_hidden, axis=0, keepdims=True)
    gain_grad[...] = gain_sum
    bias_grad[...] = bias_sum


def write_out(near, far, here, sems, copies):
    copies.append(
        pltpu.make_async_copy(near.at[here, :], far.at[here, :], sems.at[len(copies)])
    )
    copies[-1].start()


def layer_kernel(units_of, *refs):
    acts, (return_w, vecs, middle, ends_in) = refs[:PARTS], refs[PARTS : PARTS + 4]
    token, far, near, sems = refs[PARTS + 4 :]
    token[...] = jnp.zeros_like(token)
    end = ends_in[SLOTS - 1, 0]
    spans = spans_of(units_of(), acts[0].shape[1])
    copies = []
    for at in range(0, middle.shape[0], ROWS):
        here = slice(at, at + ROWS)
        feed = vecs[RETURN_BIAS : RETURN_BIAS + 1, :]
        for part, span in zip(acts, spans):
            feed = feed + dot_nn(part[here, :], return_w[span, :])
        valid = at + lax.broadcasted_iota(jnp.int32, (ROWS, 1), 0) < end
        near[here, :] = middle[here, :] + jnp.where(valid, feed, 0.0)
        write_out(near, far, here, sems, copies)
    for copy in copies:
        copy.wait()


def attention_back_kernel(
    d_low, exps, q_sel, attended, row_facts, placed, key_t, value_n, o_own, o_other, routes,
    d_stack, grad_o, spread, d_scores, d_queries,
):
    head = key_t.shape[0]
    tok, half = d_low.shape[0], o_own.shape[0]
    experts = 2 * half // head
    own = experts // 2
    scale = head**-0.5
    d_all = [dot_nt(o_own[...], d_low[...]), dot_nt(o_other[...], d_low[...])]
    hits = [expert_hits(routes[m : m + 1, :], experts) for m in range(2)]
    halves = [slice(m * tok, (m + 1) * tok) for m in range(2)]
    gates = [row_facts[0:1, lanes] for lanes in halves]
    subs = lax.broadcasted_iota(jnp.int32, (head, tok), 0)
    d_gates = []
    for m, lanes in enumerate(halves):
        d_raw = jnp.zeros((head, tok), WIDE)
        for e in range(experts):
            from_e = d_all[e // own][(e % own) * head : (e % own + 1) * head, :]
            d_raw = jnp.where(hits[m][e], from_e, d_raw)
        att = attended[:, lanes]
        d_gates.append(jnp.sum(d_raw * att, axis=0, keepdims=True))
        d_att = low(d_raw * (gates[m] * row_facts[1:2, lanes]))
        inner = jnp.sum(wide(d_att) * att, axis=0, keepdims=True)
        inner_high = wide(low(inner))
        tail = jnp.where(subs == 0, -inner_high, jnp.where(subs == 1, inner_high - inner, 0.0))
        spread[:head, lanes] = d_att
        spread[head:, lanes] = low(tail)
    mean_gate = gates[0] * d_gates[0] + gates[1] * d_gates[1]
    ids = lax.broadcasted_iota(jnp.int32, (experts, tok), 0)
    d_logits = sum(
        jnp.where(ids == routes[m : m + 1, :], gates[m] * (d_gates[m] - mean_gate), 0.0)
        for m in range(2)
    )
    high = wide(low(d_logits))
    d_stack[2 * half + 2 * head :, :] = low(jnp.concatenate([high, d_logits - high], axis=0))

    def d_probs_of(at):
        return dot_nn(value_n[...], spread[:, at : at + ROWS])

    d_probs = d_probs_of(0)
    for at in range(0, 2 * tok, ROWS):
        later = d_probs_of(at + ROWS) if at + ROWS < 2 * tok else None
        here = slice(at, at + ROWS)
        d_score = low(wide(exps[:, here]) * d_probs)
        d_scores[:, here] = d_score
        d_queries[:, here] = dot_nn(key_t[...], d_score) * scale
        d_probs = later
    d_values = dot_nt(exps[...], spread[:head, :])
    d_keys = dot_nt(d_scores[...], q_sel[...]) * scale
    d_stack[2 * half : 2 * half + head, :] = low(d_keys.T)
    d_stack[2 * half + head : 2 * half + 2 * head, :] = low(d_values.T)
    first, second = d_queries[:, halves[0]], d_queries[:, halves[1]]
    for e in range(experts):
        d_stack[e * head : (e + 1) * head, :] = low(
            jnp.where(hits[0][e], first, jnp.where(hits[1][e], second, 0.0))
        )
    grad_o[...] = dot_nn(placed[...], d_low[...])


def close_kernel(
    units_of, d_stack, grad_o, q_own, q_other, normed, vecs, return_bias_grad, second_gain_grad,
    second_bias_grad, key_w, value_w, router_w, *rest,
):
    bias_parts, (own_grads, other_grads, common) = rest[:PARTS], rest[PARTS:]
    half, head, experts = q_own.shape[0], key_w.shape[0], router_w.shape[0]
    owned = at_kv = 2 * half
    rows_in = normed[...]
    parts = ((0, half, q_own[...]), (half, at_kv, q_other[...]))
    tail_w = jnp.concatenate([key_w[...], value_w[...], router_w[...], router_w[...]], axis=0)
    parts = parts + ((at_kv, d_stack.shape[0], tail_w),)
    bias_sum, product_sum, grads = 0.0, 0.0, []
    for start, stop, weights in parts:
        stack = d_stack[start:stop, :]
        grad = dot_nn(stack, rows_in)
        grads.append(grad)
        row_sums = jnp.sum(wide(stack), axis=1, keepdims=True)
        bias_sum = bias_sum + jnp.sum(row_sums * wide(weights), axis=0, keepdims=True)
        product_sum = product_sum + jnp.sum(grad * wide(weights), axis=0, keepdims=True)
    gain = vecs[FIRST_GAIN : FIRST_GAIN + 1, :]
    gain_sum = (product_sum - vecs[FIRST_BIAS : FIRST_BIAS + 1, :] * bias_sum) / gain
    own_grads[:half, :] = low(grads[0])
    other_grads[:half, :] = low(grads[1])
    own_grads[half:owned, :] = low(grad_o[:half, :])
    other_grads[half:owned, :] = low(grad_o[half:, :])
    tail = grads[2]
    common[...] = jnp.zeros_like(common)
    common[: 2 * head, :] = tail[: 2 * head, :]
    row = 2 * head
    common[row : row + experts, :] = (
        tail[2 * head : 2 * head + experts, :] + tail[2 * head + experts :, :]
    )
    row = row + experts
    rows = (gain_sum, bias_sum, second_gain_grad[...], second_bias_grad[...], return_bias_grad[...])
    for j, values in enumerate(rows):
        common[row + j : row + j + 1, :] = values
    for unit, part in zip(units_of(), bias_parts):
        cols = part.shape[1]
        at = pl.ds(row + HIDDEN_BIAS + unit // 2, 1)
        there_now = common[at, :]
        doubled = jnp.concatenate([part[...], part[...]], axis=1)
        lanes = lax.broadcasted_iota(jnp.int32, doubled.shape, 1)
        common[at, :] = jnp.where(lanes // cols == unit % 2, doubled, there_now)
    own_grads[owned:, :] = low(common[...])
    other_grads[owned:, :] = low(common[...])


def input_kernel(
    d_stack, q_own, q_other, key_w, value_w, router_w, x, d_middle, vecs,
    token, far, near, sems,
):
    token[...] = jnp.zeros_like(token)
    half = q_own.shape[0]
    at_kv = 2 * half
    tail_w = jnp.concatenate([key_w[...], value_w[...], router_w[...], router_w[...]], axis=0)
    gain = vecs[FIRST_GAIN : FIRST_GAIN + 1, :]
    copies = []
    for at in range(0, x.shape[0], ROWS):
        here = slice(at, at + ROWS)
        d_normed = dot_tn(d_stack[:half, here], q_own[...])
        d_normed = d_normed + dot_tn(d_stack[half:at_kv, here], q_other[...])
        d_normed = d_normed + dot_tn(d_stack[at_kv:, here], tail_w)
        unit, inv = norm_parts(wide(x[here, :]))
        near[here, :] = d_middle[here, :] + norm_back(d_normed, unit, inv, gain)
        write_out(near, far, here, sems, copies)
    for copy in copies:
        copy.wait()


def halvings(n_dp):
    return n_dp.bit_length() - 3


def step_orders(n_dp):
    first = list(range(halvings(n_dp)))
    second = []
    for at in range(0, len(first), 2):
        second += first[at : at + 2][::-1]
    return first, second


def pairs_of(n_dp, step):
    orders = step_orders(n_dp)
    return [
        (chip * 2 + core, (chip ^ (1 << orders[core][step])) * 2 + core)
        for chip in range(n_dp)
        for core in range(2)
    ]


def quad_pairs(n_dp, turn):
    return [
        (chip * 2 + core, (chip ^ (turn << halvings(n_dp))) * 2 + core)
        for chip in range(n_dp)
        for core in range(2)
    ]


def cross_pairs(n_dp, turn):
    low_bit = halvings(n_dp)
    return [
        (chip * 2 + core, (chip ^ (1 << (low_bit + turn))) * 2 + core)
        for chip in range(n_dp)
        for core in range(2)
    ]


def core_swap(values, n_dp):
    return lax.ppermute(values, AXES, [(at, at ^ 1) for at in range(2 * n_dp)])


def bit_here(n_dp, step, core=None):
    first, second = step_orders(n_dp)
    chip = lax.axis_index("dp")
    core = core_here() if core is None else core
    return jnp.where(core == 0, chip >> first[step], chip >> second[step]) & 1


def units_here(n_dp, entries):
    core = core_here()
    mine, theirs = bit_here(n_dp, 0), bit_here(n_dp, 0, 1 - core)
    other = 1 - core
    blocks = [2 * other + 1 - theirs, 2 * core + 1 - mine, 2 * other + theirs, 2 * core + mine]
    return [2 * blocks[entry // 2] + entry % 2 for entry in entries]


def rows_at(index, size):
    return pl.ds(pl.multiple_of(index * size, size), size)


def add_kernel(*refs):
    total = wide(refs[0][...])
    for ref in refs[1:-1]:
        total = total + wide(ref[...])
    refs[-1][...] = low(total)


def rows_of(ref, at, size):
    return wide(ref[pl.ds(pl.multiple_of(at, size), size), :])


def partial_sum(n_dp, terms, step, last_kept):
    start = step - len(terms) + 1
    size = terms[0][0].shape[0] >> (step - start + 1)
    at, total = 0, 0.0
    for j in range(step, start - 1, -1):
        bit = bit_here(n_dp, j)
        bit = bit if last_kept or j < step else 1 - bit
        at = at + bit * (size << (step - j))
        for ref in terms[j - start]:
            total = total + rows_of(ref, at, size)
    return total


def group(refs, counts):
    refs = list(refs)
    return [[refs.pop(0) for _ in range(count)] for count in counts]


def split_terms(terms, joint):
    parts = []
    for part in range(2):
        chosen = []
        for refs, flags in zip(terms, joint):
            chosen.append([])
            for ref, flag in zip(refs, flags):
                half = ref.shape[0] // 2
                if flag == 2:
                    chosen[-1].append(ref.at[pl.ds(part * half, half), :])
                elif flag == part:
                    chosen[-1].append(ref)
        parts.append(chosen)
    return parts


def send_kernel(n_dp, step, counts, joint, *refs):
    out = refs[-1]
    terms = group(refs[:-1], counts)
    if joint is None:
        out[...] = low(partial_sum(n_dp, terms, step, False))
        return
    size = out.shape[0] // 2
    for part, chosen in enumerate(split_terms(terms, joint)):
        out[part * size : (part + 1) * size, :] = low(partial_sum(n_dp, chosen, step, False))


def kept_kernel(n_dp, step, counts, *refs):
    *terms, last = group(refs[:-1], counts)
    refs[-1][...] = low(partial_sum(n_dp, terms, step, True) + wide(last[0][...]))


def spot_here(n_dp, turn):
    return jnp.bitwise_xor(lax.axis_index("dp") >> halvings(n_dp), turn)


def quarters_kernel(n_dp, step, counts, joint, *refs):
    count = sum(counts)
    terms = group(refs[:count], counts)
    outs, total = refs[count:-1], refs[-1]
    size = total.shape[0] // 2
    for part, (*chosen, last) in enumerate(split_terms(terms, joint)):
        total[part * size : (part + 1) * size, :] = partial_sum(
            n_dp, chosen, step, True
        ) + wide(last[0][...])
    cols = outs[0].shape[1]
    for turn, out in enumerate(outs):
        out[...] = low(total[:, rows_at(spot_here(n_dp, turn), cols)])


def row_of_four(n_dp, part, *refs):
    pieces, out = refs[:4], refs[4]
    size, cols = out.shape[0], pieces[0].shape[1]
    for turn, piece in enumerate(pieces):
        at = rows_at(spot_here(n_dp, turn), cols)
        out[:, at] = piece[part * size : (part + 1) * size, :]


def join_kernel(n_dp, step, mine, got, out):
    size = mine.shape[0]
    bit = bit_here(n_dp, step)
    out[rows_at(bit, size), :] = mine[...]
    out[rows_at(1 - bit, size), :] = got[...]


def pass_kernel(source, out):
    out[...] = source[...]


def stack_kernel(first, second, out):
    size = first.shape[0]
    out[:size, :] = first[...]
    out[size:, :] = second[...]


def place_kernel(units_of, count, more, *refs):
    hidden, returned, left, right, sems = refs[-5:]
    copies = []
    width = left.shape[1]
    parts = []
    for ref in refs[:count]:
        parts += [ref.at[pl.ds(row, width), :] for row in range(0, ref.shape[0], width)]
    for j, (unit, part) in enumerate(zip(units_of(), parts)):
        cols = part.shape[1] // 2
        at = rows_at(unit, cols)
        left[j] = wide(part[:, :cols])
        copies.append(pltpu.make_async_copy(left.at[j], hidden.at[:, at], sems.at[2 * j]))
        copies[-1].start()
        right[j] = wide(part[:, cols:]).T
        copies.append(pltpu.make_async_copy(right.at[j], returned.at[at, :], sems.at[2 * j + 1]))
        copies[-1].start()
    if more:
        refs[-6][...] = jnp.zeros_like(refs[-6])
    for copy in copies:
        copy.wait()


def finish_kernel(n_dp, mine, got, token, query_g, output_g, key_g, value_g, router_g, *refs):
    vectors, whole = refs[:-1], refs[-1]
    token[...] = jnp.zeros_like(token)
    size, width = mine.shape
    bit = bit_here(n_dp, 0)
    whole[rows_at(bit, size), :] = wide(mine[...])
    whole[rows_at(1 - bit, size), :] = wide(got[...])
    row = 0
    for out in (query_g, output_g, key_g, value_g, router_g):
        out[...] = whole[row : row + out.shape[0], :]
        row = row + out.shape[0]
    for j, vector in enumerate(vectors[:-1]):
        vector[...] = whole[row + j, :]
    row = row + len(vectors) - 1
    for j in range(vectors[-1].shape[0] // width):
        vectors[-1][j * width : (j + 1) * width] = whole[row + j, :]


def local(
    inputs, cotangent, lengths, routes, first_gain, first_bias, router_weight, key_weight,
    value_weight, query_weight, output_weight, second_gain, second_bias, hidden_weight,
    hidden_bias, return_weight, return_bias,
):
    tok, width = inputs.shape
    ff = hidden_weight.shape[1]
    n_dp = lax.axis_size("dp")
    own, _, head = query_weight.shape
    experts = 2 * own
    half = own * head
    blocks = tok // ROWS

    q_own = jnp.transpose(query_weight, (0, 2, 1)).reshape(half, width)
    o_own = output_weight.reshape(half, width)
    q_other, o_other = core_swap(q_own, n_dp), core_swap(o_own, n_dp)
    vec_rows = 5 + ff // width
    program = Program()
    call = program.call
    (
        normed, vecs, keys_ext, key_t, value_n, values_ext, logits, x, q_own, o_own, key_w, value_w,
        router_w, routes, ends,
    ) = call(
        open_kernel, "first_norm", [],
        [
            held((tok, width), LOW), held((vec_rows + -vec_rows % 8, width), WIDE),
            held((tok, 2 * head), LOW), held((head, tok), LOW), held((tok, 2 * head), LOW),
            held((head + 16, tok), LOW), held((experts, tok), WIDE), held((tok, width), LOW),
            held((half, width), LOW), held((half, width), LOW), held((head, width), LOW),
            held((head, width), LOW), held((experts, width), LOW), held((2, tok), jnp.int32),
            held((8, 128), jnp.int32),
        ],
        scratch=[pltpu.SMEM(lengths.shape[1:], jnp.int32)]
        + [pltpu.VMEM((width,), LOW)] * 5
        + [pltpu.VMEM((ff,), LOW), pltpu.SemaphoreType.DMA((blocks + 13,))],
        far=[
            inputs, lengths[0], first_gain, first_bias, key_weight.T, value_weight.T,
            router_weight.T, q_own, o_own, second_gain, second_bias, return_bias, hidden_bias,
            jnp.transpose(routes[0], (0, 2, 1)),
        ],
    )
    (
        exps, q_sel, attended, row_facts, placed, middle, hidden_in, hidden_in_t, d_feed, d_feed_t,
        return_bias_grad, cot, hidden_w, return_w,
    ) = call(
        forward_kernel, "attention_forward",
        [
            normed, x, vecs, q_own, q_other, o_own, o_other, keys_ext, values_ext, logits, routes,
            ends, key_t,
        ],
        [
            held((tok, 2 * tok), LOW), held((head, 2 * tok), LOW), held((head, 2 * tok), WIDE),
            held((8, 2 * tok), WIDE), held((2 * half, tok), LOW), held((tok, width), WIDE),
            held((tok, width), LOW), held((width, tok), LOW), held((tok, width), LOW),
            held((width, tok), LOW), held((1, width), WIDE), held((tok, width), LOW),
            held(hidden_weight.shape, LOW), held(return_weight.shape, LOW),
        ],
        scratch=[pltpu.VMEM((2 * head, 2 * tok), LOW), pltpu.SemaphoreType.DMA((3,))],
        far=[cotangent, hidden_weight, return_weight],
    )

    cols = ff // PARTS
    units = lambda *entries: functools.partial(units_here, n_dp, entries)
    steps = halvings(n_dp)

    def feed(*entries):
        outs = call(
            functools.partial(feed_kernel, units(*entries), True), f"feed_{entries[0]}",
            [hidden_in, hidden_in_t, d_feed, d_feed_t, vecs, hidden_w, return_w],
            [held((tok, cols), LOW), held((tok, cols), LOW), held((1, cols), WIDE)] * len(entries)
            + [there((len(entries) * width, 2 * cols), LOW)],
        )
        return list(zip(*[iter(outs[:-1])] * 3)), outs[-1]

    def add(name, *terms):
        return call(add_kernel, name, terms, there(terms[0].shape, LOW))

    parts_a, theirs = feed(0)
    swapped = core_swap(theirs, n_dp)
    parts_c, mine = feed(2)
    sent_a = lax.ppermute(add("feed_add_0", mine, swapped), AXES, pairs_of(n_dp, 0))
    parts_b, theirs = feed(1)
    swapped = core_swap(theirs, n_dp)
    parts_d, mine = feed(3)
    sent_b = lax.ppermute(add("feed_add_1", mine, swapped), AXES, pairs_of(n_dp, 0))
    parts_e, theirs = feed(4, 5)
    swapped = core_swap(theirs, n_dp)
    parts_f, mine = feed(6, 7)
    parts = parts_a + parts_b + parts_c + parts_d + parts_e + parts_f

    every = units(*range(PARTS))
    d_middle, d_low, second_gain_grad, second_bias_grad = call(
        functools.partial(middle_kernel, every), "second_norm_back",
        [p[1] for p in parts] + [hidden_w, vecs, middle, cot, ends],
        [
            held((tok, width), WIDE), held((tok, width), LOW), held((1, width), WIDE),
            held((1, width), WIDE),
        ],
    )

    feed_terms, feed_joint = [[sent_a, sent_b, swapped, mine]], [[0, 1, 2, 2]]

    def feed_send(step):
        counts = [len(t) for t in feed_terms]
        part = call(
            functools.partial(send_kernel, n_dp, step, counts, list(feed_joint)),
            f"feed_send_{step}", sum(feed_terms, []), there((2 * width >> step, 2 * cols), LOW),
        )
        feed_terms.append([lax.ppermute(part, AXES, pairs_of(n_dp, step))])
        feed_joint.append([2])

    for step in range(1, steps):
        feed_send(step)
    d_stack, grad_o = call(
        attention_back_kernel, "attention_backward",
        [d_low, exps, q_sel, attended, row_facts, placed, key_t, value_n, o_own, o_other, routes],
        [held((2 * half + 2 * head + 2 * experts, tok), LOW), held((2 * half, width), WIDE)],
        scratch=[
            pltpu.VMEM((2 * head, 2 * tok), LOW), pltpu.VMEM((tok, 2 * tok), LOW),
            pltpu.VMEM((head, 2 * tok), WIDE),
        ],
    )
    shared = 2 * head + experts + 5 + ff // width
    shared = shared + -(2 * half + shared) % (16 << steps)
    rows = 2 * half + shared
    own_grads, other_grads = call(
        functools.partial(close_kernel, every), "projection_grads",
        [
            d_stack, grad_o, q_own, q_other, normed, vecs, return_bias_grad, second_gain_grad,
            second_bias_grad, key_w, value_w, router_w, *[p[2] for p in parts],
        ],
        [there((rows, width), LOW), there((rows, width), LOW)],
        scratch=[pltpu.VMEM((shared, width), WIDE)],
    )

    def output(kernel, name, operands):
        _, out = call(
            kernel, name, operands, [held((8, 128), WIDE), there((tok, width), WIDE)],
            scratch=[pltpu.VMEM((tok, width), WIDE), pltpu.SemaphoreType.DMA((blocks,))],
            far_out=1,
        )
        return out

    rest_terms = [[own_grads, core_swap(other_grads, n_dp)]]
    counts = [len(t) for t in feed_terms]
    own_piece, *pieces = call(
        functools.partial(quarters_kernel, n_dp, steps - 1, counts, feed_joint), "feed_cut",
        sum(feed_terms, []), [there((2 * width >> (steps - 1), cols // 2), LOW)] * 4,
        scratch=[pltpu.VMEM((2 * width >> (steps - 1), 2 * cols), WIDE)],
    )

    def across(values):
        return [
            lax.ppermute(v, AXES, quad_pairs(n_dp, t + 1)) for t, v in enumerate(values)
        ]

    pieces = across(pieces)


    def rest_send(step):
        counts = [len(t) for t in rest_terms]
        part = call(
            functools.partial(send_kernel, n_dp, step, counts, None), f"rest_send_{step}",
            sum(rest_terms, []), there((rows >> (step + 1), width), LOW),
        )
        rest_terms.append([lax.ppermute(part, AXES, pairs_of(n_dp, step))])

    def join(name, step, mine, got):
        size, wide_cols = mine.shape
        kernel = functools.partial(join_kernel, n_dp, step)
        joined = call(kernel, name, [mine, got], there((2 * size, wide_cols), LOW))
        return joined, lax.ppermute(joined, AXES, pairs_of(n_dp, step - 1))

    written = None

    def place(name, entries, values, more=True):
        nonlocal written
        count = len(values)
        *_, one, two = call(
            functools.partial(place_kernel, units(*entries), count, more), name, values,
            [held((8, 128), WIDE)] * more + [there((width, ff), WIDE), there((ff, width), WIDE)],
            scratch=[
                pltpu.VMEM((len(entries), width, cols), WIDE),
                pltpu.VMEM((len(entries), cols, width), WIDE),
                pltpu.SemaphoreType.DMA((2 * len(entries),)),
            ],
            far=[] if written is None else written,
            far_out=2,
            aliases=[] if written is None else [(0, 0), (1, 1)],
        )
        written = [one, two]

    rest_send(0)
    layer_out = output(
        functools.partial(layer_kernel, every), "layer_out",
        [p[0] for p in parts] + [return_w, vecs, middle, ends],
    )
    for step in range(1, steps):
        rest_send(step)
    own_piece = add("feed_sum", own_piece, *pieces)
    pieces = across([own_piece] * 3)
    counts = [len(t) for t in rest_terms]
    rest = call(
        functools.partial(kept_kernel, n_dp, steps - 1, counts), "rest_sum", sum(rest_terms, []),
        there((rows >> steps, width), LOW),
    )
    rest_got = lax.ppermute(rest, AXES, cross_pairs(n_dp, 0))
    input_grad = output(
        input_kernel, "first_norm_back",
        [d_stack, q_own, q_other, key_w, value_w, router_w, x, d_middle, vecs],
    )
    size = own_piece.shape[0] // 2
    joined, got = [None] * 2, [None] * 2
    for part in range(2):
        joined[part] = call(
            functools.partial(row_of_four, n_dp, part), f"feed_row_{part}", [own_piece] + pieces,
            there((size, 2 * cols), LOW),
        )
        got[part] = lax.ppermute(joined[part], AXES, pairs_of(n_dp, steps - 1))
    rest = add("rest_add_0", rest, rest_got)
    rest_got = lax.ppermute(rest, AXES, cross_pairs(n_dp, 1))
    for step in reversed(range(1, steps)):
        for part in range(2):
            name = f"feed_join_{step}_{part}"
            joined[part], got[part] = join(name, step, joined[part], got[part])
            if step == 1:
                place(f"place_own_{part}", (6 + part,), [joined[part]])
    both = call(stack_kernel, "feed_own", joined, there((2 * width, 2 * cols), LOW))
    other = core_swap(both, n_dp)
    rest = add("rest_add_1", rest, rest_got)
    rest_got = lax.ppermute(rest, AXES, pairs_of(n_dp, steps - 1))
    place("place_other", (4, 5), [other])
    far = []

    def place_got(part):
        row = call(pass_kernel, f"feed_got_{part}", [got[part]], there((width, 2 * cols), LOW))
        far.append(core_swap(row, n_dp))
        place(f"place_got_{part}", (2 + part,), [row])

    place_got(0)
    for step in reversed(range(1, steps)):
        rest, rest_got = join(f"rest_join_{step}", step, rest, rest_got)
    place_got(1)
    place("place_far", (0, 1), far)
    vectors = [there((width,), WIDE)] * 5 + [there((ff,), WIDE)]
    _, query_grad, output_grad, key_g, value_g, router_g, fg, fb, sg, sb, rb, hb = call(
        functools.partial(finish_kernel, n_dp), "finish", [rest, rest_got],
        [held((8, 128), WIDE)] + [there((half, width), WIDE)] * 2 + [there((head, width), WIDE)] * 2
        + [there((experts, width), WIDE)] + vectors,
        scratch=[pltpu.VMEM((rows, width), WIDE)],
    )
    hidden_grad, return_grad = written
    return (
        layer_out,
        input_grad,
        fg,
        fb,
        router_g.T,
        key_g.T,
        value_g.T,
        jnp.transpose(query_grad.reshape(-1, head, width), (0, 2, 1)),
        output_grad.reshape(-1, head, width),
        sg,
        sb,
        hidden_grad,
        hb,
        return_grad,
        rb,
    )


def solution(mesh):
    rows = P(AXES, None)
    cut = P("expert", None, None)
    in_specs = (
        (rows, rows, P("dp", None, None), P("dp", None, None, None))
        + (P(),) * 5
        + (cut, cut)
        + (P(),) * 6
    )
    out_specs = (rows, rows) + (P(),) * 5 + (cut, cut) + (P(),) * 6
    return jax.shard_map(local, mesh=mesh, in_specs=in_specs, out_specs=out_specs, check_vma=False)
```

```python
import functools

import jax
import jax.numpy as jnp
from jax import lax
from jax.experimental import pallas as pl
from jax.experimental.pallas import tpu as pltpu
from jax.sharding import PartitionSpec as P

AXES = ("dp", "expert")
WIDE = jnp.float32
LOW = jnp.bfloat16
EPS = 1e-05
MASKED = -1e30
REACH = 40.0
ROWS = 256
SPAN = 512
CURVE = 0.7978845608028654
CUBIC = 0.044715
VMEM_LIMIT = 16 * 1024 * 1024


def low(values):
    return values.astype(LOW)


def wide(values):
    return values.astype(WIDE)


def dot_nn(left_op, right_op):
    return lax.dot_general(
        left_op, right_op, (((1,), (0,)), ((), ())), preferred_element_type=WIDE
    )


def dot_tn(left_op, right_op):
    return lax.dot_general(
        left_op, right_op, (((0,), (0,)), ((), ())), preferred_element_type=WIDE
    )


def dot_nt(left_op, right_op):
    return lax.dot_general(
        left_op, right_op, (((1,), (1,)), ((), ())), preferred_element_type=WIDE
    )


def norm_parts(values):
    row_mean = jnp.mean(values, axis=-1, keepdims=True)
    centred = values - row_mean
    inv_dev = lax.rsqrt(jnp.mean(centred * centred, axis=-1, keepdims=True) + EPS)
    return centred * inv_dev, inv_dev


def norm_back(d_out, unit, inv_dev, gain_vec):
    weighted = d_out * gain_vec
    mean_w = jnp.mean(weighted, axis=-1, keepdims=True)
    mean_wn = jnp.mean(weighted * unit, axis=-1, keepdims=True)
    return inv_dev * (weighted - mean_w - unit * mean_wn)


def core_here():
    return lax.axis_index("expert")


def segment_of(places, ends):
    return sum((places >= end).astype(jnp.int32) for end in ends)


def held(shape, dtype):
    return pltpu.VMEM(shape, dtype)


def there(shape, dtype):
    return jax.ShapeDtypeStruct(shape, dtype)


ANYWHERE = pl.BlockSpec(memory_space=pl.ANY)
INSIDE = pl.BlockSpec(memory_space=pltpu.VMEM)


class Program:
    def __init__(self):
        self.before = []

    def call(self, kernel, name, operands, out_shape, scratch=(), far=(), far_out=0, aliases=()):
        operands = [pltpu.with_memory_space_constraint(v, pltpu.VMEM) for v in operands]
        if not aliases:
            far = [pltpu.with_memory_space_constraint(v, pltpu.HBM) for v in far]
        count, waits = len(operands) + len(far), len(self.before)

        def run(*refs):
            kernel(*refs[:count], *refs[count + waits :])

        single = not isinstance(out_shape, (list, tuple))
        outs = [out_shape] if single else list(out_shape)
        near = len(outs) - far_out
        result = pl.pallas_call(
            run,
            in_specs=[INSIDE] * len(operands) + [ANYWHERE] * (len(far) + waits),
            out_specs=[INSIDE] * near + [ANYWHERE] * far_out,
            out_shape=outs,
            scratch_shapes=list(scratch),
            input_output_aliases={len(operands) + a: near + b for a, b in aliases},
            compiler_params=pltpu.CompilerParams(vmem_limit_bytes=VMEM_LIMIT),
            cost_estimate=pl.CostEstimate(flops=3 * 10**10 if name == "rest_add_1" else 10**10, bytes_accessed=1, transcendentals=0),
            name=name,
        )(*operands, *far, *self.before)
        self.before = [result[0]]
        return result[0] if single else result


FIRST_GAIN, FIRST_BIAS, SECOND_GAIN, SECOND_BIAS, RETURN_BIAS, HIDDEN_BIAS = range(6)
SLOTS = 4
PARTS = 8


def bias_row(vecs, unit, cols):
    row = vecs[pl.ds(HIDDEN_BIAS + unit // 2, 1), :]
    return jnp.where(unit % 2 == 0, row[:, :cols], row[:, cols:])


def open_kernel(
    x_far, lengths_far, first_gain_far, first_bias_far, key_far, value_far, router_far, q_far,
    o_far, second_gain_far, second_bias_far, return_bias_far, hidden_bias_far, routes_far,
    normed, vecs, keys_ext, key_t, value_n, values_ext, logits, x, q_own, o_own, key_w, value_w,
    router_w, routes, ends_out,
    lengths, first_gain, first_bias, second_gain, second_bias, return_bias, hidden_bias, sems,
):
    spans = [slice(at, at + ROWS) for at in range(0, x.shape[0], ROWS)]
    moves = [(x_far.at[here, :], x.at[here, :]) for here in spans]
    needed = [
        (lengths_far, lengths), (first_gain_far, first_gain), (first_bias_far, first_bias),
        (key_far, key_w), (value_far, value_w), (router_far, router_w),
    ]
    later = [
        (q_far, q_own), (o_far, o_own), (second_gain_far, second_gain),
        (second_bias_far, second_bias), (return_bias_far, return_bias),
        (hidden_bias_far, hidden_bias), (routes_far.at[core_here()], routes),
    ]
    moves = moves[:1] + needed + moves[1:] + later
    copies = [pltpu.make_async_copy(*move, sems.at[j]) for j, move in enumerate(moves)]
    for copy in copies:
        copy.start()
    for copy in copies[: len(needed) + len(spans)]:
        copy.wait()
    head = key_w.shape[0]
    width = x.shape[1]
    ends, end = [], 0
    for slot in range(lengths.shape[1]):
        end = end + lengths[core_here(), slot]
        ends.append(end)
        ends_out[slot : slot + 1, :] = jnp.full((1, ends_out.shape[1]), end, jnp.int32)
    vecs[...] = jnp.zeros_like(vecs)
    for j, vec in enumerate((first_gain, first_bias)):
        vecs[j : j + 1, :] = wide(vec[...]).reshape(1, width)
    pair_w = jnp.concatenate([key_w[...], value_w[...]], axis=0)
    all_w = jnp.concatenate([key_w[...], value_w[...], router_w[...]], axis=0)
    for j, here in enumerate(spans):
        at = j * ROWS
        unit, _ = norm_parts(wide(x[here, :]))
        rows = low(
            unit * vecs[FIRST_GAIN : FIRST_GAIN + 1, :] + vecs[FIRST_BIAS : FIRST_BIAS + 1, :]
        )
        normed[here, :] = rows
        across = dot_nt(all_w, rows)
        key_t[:, here] = low(across[:head, :])
        values_ext[:head, here] = low(across[head : 2 * head, :])
        values_ext[head:, here] = jnp.ones((values_ext.shape[0] - head, ROWS), LOW)
        logits[:, here] = across[2 * head :, :]
        along = low(dot_nt(rows, pair_w))
        places = at + lax.broadcasted_iota(jnp.int32, (ROWS, head), 0)
        lanes = lax.broadcasted_iota(jnp.int32, (ROWS, head), 1)
        marks = low(jnp.where(segment_of(places, ends) == lanes, 1.0, 0.0))
        keys_ext[here, :] = jnp.concatenate([along[:, :head], marks], axis=1)
        value_n[here, :] = jnp.concatenate(
            [along[:, head:], jnp.ones((ROWS, head), LOW)], axis=1
        )
    for copy in copies[len(needed) + len(spans) :]:
        copy.wait()
    for j, vec in enumerate((second_gain, second_bias, return_bias)):
        vecs[SECOND_GAIN + j : SECOND_GAIN + j + 1, :] = wide(vec[...]).reshape(1, width)
    for j in range(hidden_bias.shape[0] // width):
        part = hidden_bias[j * width : (j + 1) * width]
        vecs[HIDDEN_BIAS + j : HIDDEN_BIAS + j + 1, :] = wide(part).reshape(1, width)


def expert_hits(route, experts):
    own = experts // 2
    relative = lax.rem(route - core_here() * own + experts, experts)
    return [relative == e for e in range(experts)]


def forward_kernel(
    normed, x, vecs, q_own, q_other, o_own, o_other, keys_ext, values_ext, logits, routes, ends_in,
    key_t, cot_far, hidden_w_far, return_w_far,
    exps, q_sel, attended, row_facts, placed, middle, hidden_in, hidden_in_t, d_feed, d_feed_t,
    bias_grad, cot, hidden_w, return_w, spread, sems,
):
    moves = ((cot_far, cot), (hidden_w_far, hidden_w), (return_w_far, return_w))
    copies = [pltpu.make_async_copy(*move, sems.at[j]) for j, move in enumerate(moves)]
    for copy in copies:
        copy.start()
    ends = [ends_in[slot, 0] for slot in range(SLOTS)]
    head = q_sel.shape[0]
    tok, half = x.shape[0], q_own.shape[0]
    experts = 2 * half // head
    own = experts // 2
    q_all = [low(dot_nt(q_own[...], normed[...])), low(dot_nt(q_other[...], normed[...]))]
    hits = [expert_hits(routes[m : m + 1, :], experts) for m in range(2)]
    places = lax.broadcasted_iota(jnp.int32, (head, tok), 1)
    subs = lax.broadcasted_iota(jnp.int32, (head, tok), 0)
    fence = low(jnp.where(segment_of(places, ends) == subs, 0.0, MASKED))
    for m in range(2):
        query = jnp.zeros((head, tok), LOW)
        for e in range(experts):
            from_e = q_all[e // own][(e % own) * head : (e % own + 1) * head, :]
            query = jnp.where(hits[m][e], from_e, query)
        lanes = slice(m * tok, (m + 1) * tok)
        q_sel[:, lanes] = query
        spread[:head, lanes] = low(wide(query) * head**-0.5)
        spread[head:, lanes] = fence

    def scores_of(here):
        return dot_nn(keys_ext[...], spread[:, here])

    def attend(here, powers):
        exps[:, here] = powers
        summed = dot_nn(values_ext[...], powers)
        inv = 1.0 / summed[head : head + 1, :]
        attended[:, here] = summed[:head, :] * inv
        row_facts[1:2, here] = inv

    longest_query = jnp.max(jnp.sum(jnp.square(wide(spread[:head, :])), axis=0, keepdims=True))
    longest_key = jnp.max(jnp.sum(jnp.square(wide(key_t[...])), axis=0, keepdims=True))
    within = longest_query * longest_key < REACH * REACH

    @pl.when(within)
    def _():
        for at in range(0, 2 * tok, SPAN):
            here = slice(at, at + SPAN)
            attend(here, low(jnp.exp(scores_of(here))))

    @pl.when(jnp.logical_not(within))
    def _():
        @pl.loop(0, 2 * tok // SPAN)
        def _(turn):
            here = rows_at(turn, SPAN)
            scores = scores_of(here)
            attend(here, low(jnp.exp(scores - jnp.max(scores, axis=0, keepdims=True))))

    ids = lax.broadcasted_iota(jnp.int32, (experts, tok), 0)
    chosen = [
        jnp.sum(jnp.where(ids == routes[m : m + 1, :], logits[...], 0.0), axis=0, keepdims=True)
        for m in range(2)
    ]
    top = jnp.maximum(chosen[0], chosen[1])
    lifts = [jnp.exp(c - top) for c in chosen]
    inv_sum = 1.0 / (lifts[0] + lifts[1])
    gated = []
    for m in range(2):
        lanes = slice(m * tok, (m + 1) * tok)
        gate = lifts[m] * inv_sum
        row_facts[0:1, lanes] = gate
        gated.append(attended[:, lanes] * gate)
    for e in range(experts):
        placed[e * head : (e + 1) * head, :] = low(
            jnp.where(hits[0][e], gated[0], jnp.where(hits[1][e], gated[1], 0.0))
        )
    copies[0].wait()
    total = jnp.zeros(bias_grad.shape, WIDE)
    for at in range(0, tok, SPAN):
        here = slice(at, at + SPAN)
        branch = dot_tn(placed[:half, here], o_own[...]) + dot_tn(placed[half:, here], o_other[...])
        spots = at + lax.broadcasted_iota(jnp.int32, (SPAN, 1), 0)
        mid = wide(x[here, :]) + jnp.where(spots < ends[-1], branch, 0.0)
        middle[here, :] = mid
        unit, _ = norm_parts(mid)
        hidden = (
            unit * vecs[SECOND_GAIN : SECOND_GAIN + 1, :] + vecs[SECOND_BIAS : SECOND_BIAS + 1, :]
        )
        hidden_in[here, :] = low(hidden)
        hidden_in_t[:, here] = low(hidden.T)
        masked = jnp.where(spots < ends[-1], wide(cot[here, :]), 0.0)
        d_feed[here, :] = low(masked)
        d_feed_t[:, here] = low(masked.T)
        total = total + jnp.sum(masked, axis=0, keepdims=True)
    bias_grad[...] = total
    for copy in copies[1:]:
        copy.wait()


def feed_kernel(
    units_of, joint, hidden_in, hidden_in_t, d_feed, d_feed_t, vecs, hidden_w, return_w, *outs
):
    units = units_of()
    grads_all = outs[-1] if joint else None
    for j, unit in enumerate(units):
        act, d_before, bias_grad = outs[3 * j : 3 * j + 3]
        cols = act.shape[1]
        at = rows_at(unit, cols)
        weight_in, weight_out = hidden_w[:, at], return_w[at, :]
        bias = bias_row(vecs, unit, cols)
        bias_sum = jnp.zeros(bias_grad.shape, WIDE)
        for row in range(0, act.shape[0], ROWS):
            here = slice(row, row + ROWS)
            x = dot_nn(hidden_in[here, :], weight_in) + bias
            d_act = dot_nt(d_feed[here, :], weight_out)
            squared = x * x
            rise = 0.5 + 0.5 * jnp.tanh(x * (CURVE + CURVE * CUBIC * squared))
            out = x * rise
            slope = rise + out * (1.0 - rise) * (2 * CURVE + 6 * CURVE * CUBIC * squared)
            act[here, :] = low(out)
            d_x = d_act * slope
            d_before[here, :] = low(d_x)
            bias_sum = bias_sum + jnp.sum(d_x, axis=0, keepdims=True)
        bias_grad[...] = bias_sum
        width = hidden_in.shape[1]
        rows = slice(j * width, (j + 1) * width)
        grads_all[rows, :cols] = low(dot_nn(hidden_in_t[...], d_before[...]))
        grads_all[rows, cols:] = low(dot_nn(d_feed_t[...], act[...]))


def spans_of(units, cols):
    return [rows_at(unit, cols) for unit in units]


def middle_kernel(units_of, *refs):
    d_befores, (hidden_w, vecs, middle, cot, ends_in) = refs[:PARTS], refs[PARTS : PARTS + 5]
    d_middle, d_low, gain_grad, bias_grad = refs[PARTS + 5 :]
    end = ends_in[SLOTS - 1, 0]
    spans = spans_of(units_of(), d_befores[0].shape[1])
    gain = vecs[SECOND_GAIN : SECOND_GAIN + 1, :]
    gain_sum = jnp.zeros(gain_grad.shape, WIDE)
    bias_sum = jnp.zeros(bias_grad.shape, WIDE)
    for at in range(0, middle.shape[0], ROWS):
        here = slice(at, at + ROWS)
        d_hidden = 0.0
        for part, span in zip(d_befores, spans):
            d_hidden = d_hidden + dot_nt(part[here, :], hidden_w[:, span])
        valid = at + lax.broadcasted_iota(jnp.int32, (ROWS, 1), 0) < end
        unit, inv = norm_parts(middle[here, :])
        d_mid = wide(cot[here, :]) + norm_back(d_hidden, unit, inv, gain)
        d_middle[here, :] = d_mid
        d_low[here, :] = low(jnp.where(valid, d_mid, 0.0))
        gain_sum = gain_sum + jnp.sum(d_hidden * unit, axis=0, keepdims=True)
        bias_sum = bias_sum + jnp.sum(d_hidden, axis=0, keepdims=True)
    gain_grad[...] = gain_sum
    bias_grad[...] = bias_sum


def rows_out(near, far, sems, compute):
    blocks = near.shape[0] // ROWS

    def leaving(turn):
        here = rows_at(turn, ROWS)
        return pltpu.make_async_copy(near.at[here, :], far.at[here, :], sems.at[turn])

    @pl.loop(0, blocks)
    def _(turn):
        compute(rows_at(turn, ROWS), turn * ROWS)
        leaving(turn).start()

    for turn in range(blocks):
        leaving(turn).wait()


def layer_kernel(units_of, *refs):
    acts, (return_w, vecs, middle, ends_in) = refs[:PARTS], refs[PARTS : PARTS + 4]
    token, far, near, sems = refs[PARTS + 4 :]
    token[...] = jnp.zeros_like(token)
    end = ends_in[SLOTS - 1, 0]
    spans = spans_of(units_of(), acts[0].shape[1])

    def compute(here, at):
        feed = vecs[RETURN_BIAS : RETURN_BIAS + 1, :]
        for part, span in zip(acts, spans):
            feed = feed + dot_nn(part[here, :], return_w[span, :])
        valid = at + lax.broadcasted_iota(jnp.int32, (ROWS, 1), 0) < end
        near[here, :] = middle[here, :] + jnp.where(valid, feed, 0.0)

    rows_out(near, far, sems, compute)


def attention_back_kernel(
    d_low, exps, q_sel, attended, row_facts, placed, key_t, value_n, o_own, o_other, routes,
    d_stack, grad_o, spread, d_scores, d_queries,
):
    head = key_t.shape[0]
    tok, half = d_low.shape[0], o_own.shape[0]
    experts = 2 * half // head
    own = experts // 2
    scale = head**-0.5
    d_all = [dot_nt(o_own[...], d_low[...]), dot_nt(o_other[...], d_low[...])]
    hits = [expert_hits(routes[m : m + 1, :], experts) for m in range(2)]
    halves = [slice(m * tok, (m + 1) * tok) for m in range(2)]
    gates = [row_facts[0:1, lanes] for lanes in halves]
    subs = lax.broadcasted_iota(jnp.int32, (head, tok), 0)
    d_gates = []
    for m, lanes in enumerate(halves):
        d_raw = jnp.zeros((head, tok), WIDE)
        for e in range(experts):
            from_e = d_all[e // own][(e % own) * head : (e % own + 1) * head, :]
            d_raw = jnp.where(hits[m][e], from_e, d_raw)
        att = attended[:, lanes]
        d_gates.append(jnp.sum(d_raw * att, axis=0, keepdims=True))
        d_att = low(d_raw * (gates[m] * row_facts[1:2, lanes]))
        inner = jnp.sum(wide(d_att) * att, axis=0, keepdims=True)
        inner_high = wide(low(inner))
        tail = jnp.where(subs == 0, -inner_high, jnp.where(subs == 1, inner_high - inner, 0.0))
        spread[:head, lanes] = d_att
        spread[head:, lanes] = low(tail)
    mean_gate = gates[0] * d_gates[0] + gates[1] * d_gates[1]
    ids = lax.broadcasted_iota(jnp.int32, (experts, tok), 0)
    d_logits = sum(
        jnp.where(ids == routes[m : m + 1, :], gates[m] * (d_gates[m] - mean_gate), 0.0)
        for m in range(2)
    )
    high = wide(low(d_logits))
    d_stack[2 * half + 2 * head :, :] = low(jnp.concatenate([high, d_logits - high], axis=0))

    def d_probs_of(at):
        return dot_nn(value_n[...], spread[:, at : at + ROWS])

    d_probs = d_probs_of(0)
    for at in range(0, 2 * tok, ROWS):
        later = d_probs_of(at + ROWS) if at + ROWS < 2 * tok else None
        here = slice(at, at + ROWS)
        d_score = low(wide(exps[:, here]) * d_probs)
        d_scores[:, here] = d_score
        d_queries[:, here] = dot_nn(key_t[...], d_score) * scale
        d_probs = later
    d_values = dot_nt(exps[...], spread[:head, :])
    d_keys = dot_nt(d_scores[...], q_sel[...]) * scale
    d_stack[2 * half : 2 * half + head, :] = low(d_keys.T)
    d_stack[2 * half + head : 2 * half + 2 * head, :] = low(d_values.T)
    first, second = d_queries[:, halves[0]], d_queries[:, halves[1]]
    for e in range(experts):
        d_stack[e * head : (e + 1) * head, :] = low(
            jnp.where(hits[0][e], first, jnp.where(hits[1][e], second, 0.0))
        )
    grad_o[...] = dot_nn(placed[...], d_low[...])


def close_kernel(
    units_of, d_stack, grad_o, q_own, q_other, normed, vecs, return_bias_grad, second_gain_grad,
    second_bias_grad, key_w, value_w, router_w, *rest,
):
    bias_parts, (own_grads, other_grads, common) = rest[:PARTS], rest[PARTS:]
    half, head, experts = q_own.shape[0], key_w.shape[0], router_w.shape[0]
    owned = at_kv = 2 * half
    rows_in = normed[...]
    parts = ((0, half, q_own[...]), (half, at_kv, q_other[...]))
    tail_w = jnp.concatenate([key_w[...], value_w[...], router_w[...], router_w[...]], axis=0)
    parts = parts + ((at_kv, d_stack.shape[0], tail_w),)
    bias_sum, product_sum, grads = 0.0, 0.0, []
    for start, stop, weights in parts:
        stack = d_stack[start:stop, :]
        grad = dot_nn(stack, rows_in)
        grads.append(grad)
        row_sums = jnp.sum(wide(stack), axis=1, keepdims=True)
        bias_sum = bias_sum + jnp.sum(row_sums * wide(weights), axis=0, keepdims=True)
        product_sum = product_sum + jnp.sum(grad * wide(weights), axis=0, keepdims=True)
    gain = vecs[FIRST_GAIN : FIRST_GAIN + 1, :]
    gain_sum = (product_sum - vecs[FIRST_BIAS : FIRST_BIAS + 1, :] * bias_sum) / gain
    own_grads[:half, :] = low(grads[0])
    other_grads[:half, :] = low(grads[1])
    own_grads[half:owned, :] = low(grad_o[:half, :])
    other_grads[half:owned, :] = low(grad_o[half:, :])
    tail = grads[2]
    common[...] = jnp.zeros_like(common)
    common[: 2 * head, :] = tail[: 2 * head, :]
    row = 2 * head
    common[row : row + experts, :] = (
        tail[2 * head : 2 * head + experts, :] + tail[2 * head + experts :, :]
    )
    row = row + experts
    rows = (gain_sum, bias_sum, second_gain_grad[...], second_bias_grad[...], return_bias_grad[...])
    for j, values in enumerate(rows):
        common[row + j : row + j + 1, :] = values
    for unit, part in zip(units_of(), bias_parts):
        cols = part.shape[1]
        at = pl.ds(row + HIDDEN_BIAS + unit // 2, 1)
        there_now = common[at, :]
        doubled = jnp.concatenate([part[...], part[...]], axis=1)
        lanes = lax.broadcasted_iota(jnp.int32, doubled.shape, 1)
        common[at, :] = jnp.where(lanes // cols == unit % 2, doubled, there_now)
    own_grads[owned:, :] = low(common[...])
    other_grads[owned:, :] = low(common[...])


def input_kernel(
    d_stack, q_own, q_other, key_w, value_w, router_w, x, d_middle, vecs,
    token, far, near, sems,
):
    token[...] = jnp.zeros_like(token)
    half = q_own.shape[0]
    at_kv = 2 * half
    tail_w = jnp.concatenate([key_w[...], value_w[...], router_w[...], router_w[...]], axis=0)
    gain = vecs[FIRST_GAIN : FIRST_GAIN + 1, :]

    def compute(here, at):
        d_normed = dot_tn(d_stack[:half, here], q_own[...])
        d_normed = d_normed + dot_tn(d_stack[half:at_kv, here], q_other[...])
        d_normed = d_normed + dot_tn(d_stack[at_kv:, here], tail_w)
        unit, inv = norm_parts(wide(x[here, :]))
        near[here, :] = d_middle[here, :] + norm_back(d_normed, unit, inv, gain)

    rows_out(near, far, sems, compute)


def halvings(n_dp):
    return n_dp.bit_length() - 3


def step_orders(n_dp):
    first = list(range(halvings(n_dp)))
    second = []
    for at in range(0, len(first), 2):
        second += first[at : at + 2][::-1]
    return first, second


def pairs_of(n_dp, step):
    orders = step_orders(n_dp)
    return [
        (chip * 2 + core, (chip ^ (1 << orders[core][step])) * 2 + core)
        for chip in range(n_dp)
        for core in range(2)
    ]


def quad_pairs(n_dp, turn):
    return [
        (chip * 2 + core, (chip ^ (turn << halvings(n_dp))) * 2 + core)
        for chip in range(n_dp)
        for core in range(2)
    ]


def cross_pairs(n_dp, turn):
    low_bit = halvings(n_dp)
    return [
        (chip * 2 + core, (chip ^ (1 << (low_bit + turn))) * 2 + core)
        for chip in range(n_dp)
        for core in range(2)
    ]


def core_swap(values, n_dp):
    return lax.ppermute(values, AXES, [(at, at ^ 1) for at in range(2 * n_dp)])


def bit_here(n_dp, step, core=None):
    first, second = step_orders(n_dp)
    chip = lax.axis_index("dp")
    core = core_here() if core is None else core
    return jnp.where(core == 0, chip >> first[step], chip >> second[step]) & 1


def units_here(n_dp, entries):
    core = core_here()
    mine, theirs = bit_here(n_dp, 0), bit_here(n_dp, 0, 1 - core)
    other = 1 - core
    blocks = [2 * other + 1 - theirs, 2 * core + 1 - mine, 2 * other + theirs, 2 * core + mine]
    return [2 * blocks[entry // 2] + entry % 2 for entry in entries]


def rows_at(index, size):
    return pl.ds(pl.multiple_of(index * size, size), size)


def add_kernel(*refs):
    total = wide(refs[0][...])
    for ref in refs[1:-1]:
        total = total + wide(ref[...])
    refs[-1][...] = low(total)


def rows_of(ref, at, size):
    return wide(ref[pl.ds(pl.multiple_of(at, size), size), :])


def partial_sum(n_dp, terms, step, last_kept):
    start = step - len(terms) + 1
    size = terms[0][0].shape[0] >> (step - start + 1)
    at, total = 0, 0.0
    for j in range(step, start - 1, -1):
        bit = bit_here(n_dp, j)
        bit = bit if last_kept or j < step else 1 - bit
        at = at + bit * (size << (step - j))
        for ref in terms[j - start]:
            total = total + rows_of(ref, at, size)
    return total


def group(refs, counts):
    refs = list(refs)
    return [[refs.pop(0) for _ in range(count)] for count in counts]


def split_terms(terms, joint):
    parts = []
    for part in range(2):
        chosen = []
        for refs, flags in zip(terms, joint):
            chosen.append([])
            for ref, flag in zip(refs, flags):
                half = ref.shape[0] // 2
                if flag == 2:
                    chosen[-1].append(ref.at[pl.ds(part * half, half), :])
                elif flag == part:
                    chosen[-1].append(ref)
        parts.append(chosen)
    return parts


def send_kernel(n_dp, step, counts, joint, *refs):
    out = refs[-1]
    terms = group(refs[:-1], counts)
    if joint is None:
        out[...] = low(partial_sum(n_dp, terms, step, False))
        return
    size = out.shape[0] // 2
    for part, chosen in enumerate(split_terms(terms, joint)):
        out[part * size : (part + 1) * size, :] = low(partial_sum(n_dp, chosen, step, False))


def kept_kernel(n_dp, step, counts, *refs):
    *terms, last = group(refs[:-1], counts)
    refs[-1][...] = low(partial_sum(n_dp, terms, step, True) + wide(last[0][...]))


def spot_here(n_dp, turn):
    return jnp.bitwise_xor(lax.axis_index("dp") >> halvings(n_dp), turn)


def quarters_kernel(n_dp, step, counts, joint, *refs):
    count = sum(counts)
    terms = group(refs[:count], counts)
    outs, total = refs[count:-1], refs[-1]
    size = total.shape[0] // 2
    for part, (*chosen, last) in enumerate(split_terms(terms, joint)):
        total[part * size : (part + 1) * size, :] = partial_sum(
            n_dp, chosen, step, True
        ) + wide(last[0][...])
    cols = outs[0].shape[1]
    for turn, out in enumerate(outs):
        out[...] = low(total[:, rows_at(spot_here(n_dp, turn), cols)])


def row_of_four(n_dp, part, *refs):
    pieces, out = refs[:4], refs[4]
    size, cols = out.shape[0], pieces[0].shape[1]
    for turn, piece in enumerate(pieces):
        at = rows_at(spot_here(n_dp, turn), cols)
        out[:, at] = piece[part * size : (part + 1) * size, :]


def join_kernel(n_dp, step, mine, got, out):
    size = mine.shape[0]
    bit = bit_here(n_dp, step)
    out[rows_at(bit, size), :] = mine[...]
    out[rows_at(1 - bit, size), :] = got[...]


def pass_kernel(source, out):
    out[...] = source[...]


def stack_kernel(first, second, out):
    size = first.shape[0]
    out[:size, :] = first[...]
    out[size:, :] = second[...]


def place_kernel(units_of, count, more, *refs):
    hidden, returned, left, right, sems = refs[-5:]
    copies = []
    width = left.shape[1]
    parts = []
    for ref in refs[:count]:
        parts += [ref.at[pl.ds(row, width), :] for row in range(0, ref.shape[0], width)]
    for j, (unit, part) in enumerate(zip(units_of(), parts)):
        cols = part.shape[1] // 2
        at = rows_at(unit, cols)
        left[j] = wide(part[:, :cols])
        copies.append(pltpu.make_async_copy(left.at[j], hidden.at[:, at], sems.at[2 * j]))
        copies[-1].start()
        right[j] = wide(part[:, cols:]).T
        copies.append(pltpu.make_async_copy(right.at[j], returned.at[at, :], sems.at[2 * j + 1]))
        copies[-1].start()
    if more:
        refs[-6][...] = jnp.zeros_like(refs[-6])
    for copy in copies:
        copy.wait()


def finish_kernel(n_dp, mine, got, token, query_g, output_g, key_g, value_g, router_g, *refs):
    vectors, whole = refs[:-1], refs[-1]
    token[...] = jnp.zeros_like(token)
    size, width = mine.shape
    bit = bit_here(n_dp, 0)
    whole[rows_at(bit, size), :] = wide(mine[...])
    whole[rows_at(1 - bit, size), :] = wide(got[...])
    row = 0
    for out in (query_g, output_g, key_g, value_g, router_g):
        out[...] = whole[row : row + out.shape[0], :]
        row = row + out.shape[0]
    for j, vector in enumerate(vectors[:-1]):
        vector[...] = whole[row + j, :]
    row = row + len(vectors) - 1
    for j in range(vectors[-1].shape[0] // width):
        vectors[-1][j * width : (j + 1) * width] = whole[row + j, :]


def local(
    inputs, cotangent, lengths, routes, first_gain, first_bias, router_weight, key_weight,
    value_weight, query_weight, output_weight, second_gain, second_bias, hidden_weight,
    hidden_bias, return_weight, return_bias,
):
    tok, width = inputs.shape
    ff = hidden_weight.shape[1]
    n_dp = lax.axis_size("dp")
    own, _, head = query_weight.shape
    experts = 2 * own
    half = own * head
    blocks = tok // ROWS

    q_own = jnp.transpose(query_weight, (0, 2, 1)).reshape(half, width)
    o_own = output_weight.reshape(half, width)
    q_other, o_other = core_swap(q_own, n_dp), core_swap(o_own, n_dp)
    vec_rows = 5 + ff // width
    program = Program()
    call = program.call
    (
        normed, vecs, keys_ext, key_t, value_n, values_ext, logits, x, q_own, o_own, key_w, value_w,
        router_w, routes, ends,
    ) = call(
        open_kernel, "first_norm", [],
        [
            held((tok, width), LOW), held((vec_rows + -vec_rows % 8, width), WIDE),
            held((tok, 2 * head), LOW), held((head, tok), LOW), held((tok, 2 * head), LOW),
            held((head + 16, tok), LOW), held((experts, tok), WIDE), held((tok, width), LOW),
            held((half, width), LOW), held((half, width), LOW), held((head, width), LOW),
            held((head, width), LOW), held((experts, width), LOW), held((2, tok), jnp.int32),
            held((8, 128), jnp.int32),
        ],
        scratch=[pltpu.SMEM(lengths.shape[1:], jnp.int32)]
        + [pltpu.VMEM((width,), LOW)] * 5
        + [pltpu.VMEM((ff,), LOW), pltpu.SemaphoreType.DMA((blocks + 13,))],
        far=[
            inputs, lengths[0], first_gain, first_bias, key_weight.T, value_weight.T,
            router_weight.T, q_own, o_own, second_gain, second_bias, return_bias, hidden_bias,
            jnp.transpose(routes[0], (0, 2, 1)),
        ],
    )
    (
        exps, q_sel, attended, row_facts, placed, middle, hidden_in, hidden_in_t, d_feed, d_feed_t,
        return_bias_grad, cot, hidden_w, return_w,
    ) = call(
        forward_kernel, "attention_forward",
        [
            normed, x, vecs, q_own, q_other, o_own, o_other, keys_ext, values_ext, logits, routes,
            ends, key_t,
        ],
        [
            held((tok, 2 * tok), LOW), held((head, 2 * tok), LOW), held((head, 2 * tok), WIDE),
            held((8, 2 * tok), WIDE), held((2 * half, tok), LOW), held((tok, width), WIDE),
            held((tok, width), LOW), held((width, tok), LOW), held((tok, width), LOW),
            held((width, tok), LOW), held((1, width), WIDE), held((tok, width), LOW),
            held(hidden_weight.shape, LOW), held(return_weight.shape, LOW),
        ],
        scratch=[pltpu.VMEM((2 * head, 2 * tok), LOW), pltpu.SemaphoreType.DMA((3,))],
        far=[cotangent, hidden_weight, return_weight],
    )

    cols = ff // PARTS
    units = lambda *entries: functools.partial(units_here, n_dp, entries)
    steps = halvings(n_dp)

    def feed(*entries):
        outs = call(
            functools.partial(feed_kernel, units(*entries), True), f"feed_{entries[0]}",
            [hidden_in, hidden_in_t, d_feed, d_feed_t, vecs, hidden_w, return_w],
            [held((tok, cols), LOW), held((tok, cols), LOW), held((1, cols), WIDE)] * len(entries)
            + [there((len(entries) * width, 2 * cols), LOW)],
        )
        return list(zip(*[iter(outs[:-1])] * 3)), outs[-1]

    def add(name, *terms):
        return call(add_kernel, name, terms, there(terms[0].shape, LOW))

    parts_a, theirs = feed(0)
    swapped = core_swap(theirs, n_dp)
    parts_c, mine = feed(2)
    sent_a = lax.ppermute(add("feed_add_0", mine, swapped), AXES, pairs_of(n_dp, 0))
    parts_b, theirs = feed(1)
    swapped = core_swap(theirs, n_dp)
    parts_d, mine = feed(3)
    sent_b = lax.ppermute(add("feed_add_1", mine, swapped), AXES, pairs_of(n_dp, 0))
    parts_e, theirs = feed(4, 5)
    swapped = core_swap(theirs, n_dp)
    parts_f, mine = feed(6, 7)
    parts = parts_a + parts_b + parts_c + parts_d + parts_e + parts_f

    every = units(*range(PARTS))
    d_middle, d_low, second_gain_grad, second_bias_grad = call(
        functools.partial(middle_kernel, every), "second_norm_back",
        [p[1] for p in parts] + [hidden_w, vecs, middle, cot, ends],
        [
            held((tok, width), WIDE), held((tok, width), LOW), held((1, width), WIDE),
            held((1, width), WIDE),
        ],
    )

    feed_terms, feed_joint = [[sent_a, sent_b, swapped, mine]], [[0, 1, 2, 2]]

    def feed_send(step):
        counts = [len(t) for t in feed_terms]
        part = call(
            functools.partial(send_kernel, n_dp, step, counts, list(feed_joint)),
            f"feed_send_{step}", sum(feed_terms, []), there((2 * width >> step, 2 * cols), LOW),
        )
        feed_terms.append([lax.ppermute(part, AXES, pairs_of(n_dp, step))])
        feed_joint.append([2])

    for step in range(1, steps):
        feed_send(step)
    d_stack, grad_o = call(
        attention_back_kernel, "attention_backward",
        [d_low, exps, q_sel, attended, row_facts, placed, key_t, value_n, o_own, o_other, routes],
        [held((2 * half + 2 * head + 2 * experts, tok), LOW), held((2 * half, width), WIDE)],
        scratch=[
            pltpu.VMEM((2 * head, 2 * tok), LOW), pltpu.VMEM((tok, 2 * tok), LOW),
            pltpu.VMEM((head, 2 * tok), WIDE),
        ],
    )
    shared = 2 * head + experts + 5 + ff // width
    shared = shared + -(2 * half + shared) % (16 << steps)
    rows = 2 * half + shared
    own_grads, other_grads = call(
        functools.partial(close_kernel, every), "projection_grads",
        [
            d_stack, grad_o, q_own, q_other, normed, vecs, return_bias_grad, second_gain_grad,
            second_bias_grad, key_w, value_w, router_w, *[p[2] for p in parts],
        ],
        [there((rows, width), LOW), there((rows, width), LOW)],
        scratch=[pltpu.VMEM((shared, width), WIDE)],
    )

    def output(kernel, name, operands):
        _, out = call(
            kernel, name, operands, [held((8, 128), WIDE), there((tok, width), WIDE)],
            scratch=[pltpu.VMEM((tok, width), WIDE), pltpu.SemaphoreType.DMA((blocks,))],
            far_out=1,
        )
        return out

    rest_terms = [[own_grads, core_swap(other_grads, n_dp)]]
    counts = [len(t) for t in feed_terms]
    own_piece, *pieces = call(
        functools.partial(quarters_kernel, n_dp, steps - 1, counts, feed_joint), "feed_cut",
        sum(feed_terms, []), [there((2 * width >> (steps - 1), cols // 2), LOW)] * 4,
        scratch=[pltpu.VMEM((2 * width >> (steps - 1), 2 * cols), WIDE)],
    )

    def across(values):
        return [
            lax.ppermute(v, AXES, quad_pairs(n_dp, t + 1)) for t, v in enumerate(values)
        ]

    pieces = across(pieces)


    def rest_send(step):
        counts = [len(t) for t in rest_terms]
        part = call(
            functools.partial(send_kernel, n_dp, step, counts, None), f"rest_send_{step}",
            sum(rest_terms, []), there((rows >> (step + 1), width), LOW),
        )
        rest_terms.append([lax.ppermute(part, AXES, pairs_of(n_dp, step))])

    def join(name, step, mine, got):
        size, wide_cols = mine.shape
        kernel = functools.partial(join_kernel, n_dp, step)
        joined = call(kernel, name, [mine, got], there((2 * size, wide_cols), LOW))
        return joined, lax.ppermute(joined, AXES, pairs_of(n_dp, step - 1))

    written = None

    def place(name, entries, values, more=True):
        nonlocal written
        count = len(values)
        *_, one, two = call(
            functools.partial(place_kernel, units(*entries), count, more), name, values,
            [held((8, 128), WIDE)] * more + [there((width, ff), WIDE), there((ff, width), WIDE)],
            scratch=[
                pltpu.VMEM((len(entries), width, cols), WIDE),
                pltpu.VMEM((len(entries), cols, width), WIDE),
                pltpu.SemaphoreType.DMA((2 * len(entries),)),
            ],
            far=[] if written is None else written,
            far_out=2,
            aliases=[] if written is None else [(0, 0), (1, 1)],
        )
        written = [one, two]

    rest_send(0)
    layer_out = output(
        functools.partial(layer_kernel, every), "layer_out",
        [p[0] for p in parts] + [return_w, vecs, middle, ends],
    )
    for step in range(1, steps):
        rest_send(step)
    own_piece = add("feed_sum", own_piece, *pieces)
    pieces = across([own_piece] * 3)
    counts = [len(t) for t in rest_terms]
    rest = call(
        functools.partial(kept_kernel, n_dp, steps - 1, counts), "rest_sum", sum(rest_terms, []),
        there((rows >> steps, width), LOW),
    )
    rest_got = lax.ppermute(rest, AXES, cross_pairs(n_dp, 0))
    input_grad = output(
        input_kernel, "first_norm_back",
        [d_stack, q_own, q_other, key_w, value_w, router_w, x, d_middle, vecs],
    )
    size = own_piece.shape[0] // 2
    joined, got = [None] * 2, [None] * 2
    for part in range(2):
        joined[part] = call(
            functools.partial(row_of_four, n_dp, part), f"feed_row_{part}", [own_piece] + pieces,
            there((size, 2 * cols), LOW),
        )
        got[part] = lax.ppermute(joined[part], AXES, pairs_of(n_dp, steps - 1))
    rest = add("rest_add_0", rest, rest_got)
    rest_got = lax.ppermute(rest, AXES, cross_pairs(n_dp, 1))
    for step in reversed(range(1, steps)):
        for part in range(2):
            name = f"feed_join_{step}_{part}"
            joined[part], got[part] = join(name, step, joined[part], got[part])
            if step == 1:
                place(f"place_own_{part}", (6 + part,), [joined[part]])
    both = call(stack_kernel, "feed_own", joined, there((2 * width, 2 * cols), LOW))
    other = core_swap(both, n_dp)
    rest = add("rest_add_1", rest, rest_got)
    rest_got = lax.ppermute(rest, AXES, pairs_of(n_dp, steps - 1))
    place("place_other", (4, 5), [other])
    far = []

    def place_got(part):
        row = call(pass_kernel, f"feed_got_{part}", [got[part]], there((width, 2 * cols), LOW))
        far.append(core_swap(row, n_dp))
        place(f"place_got_{part}", (2 + part,), [row])

    place_got(0)
    for step in reversed(range(1, steps)):
        rest, rest_got = join(f"rest_join_{step}", step, rest, rest_got)
    place_got(1)
    place("place_far", (0, 1), far)
    vectors = [there((width,), WIDE)] * 5 + [there((ff,), WIDE)]
    _, query_grad, output_grad, key_g, value_g, router_g, fg, fb, sg, sb, rb, hb = call(
        functools.partial(finish_kernel, n_dp), "finish", [rest, rest_got],
        [held((8, 128), WIDE)] + [there((half, width), WIDE)] * 2 + [there((head, width), WIDE)] * 2
        + [there((experts, width), WIDE)] + vectors,
        scratch=[pltpu.VMEM((rows, width), WIDE)],
    )
    hidden_grad, return_grad = written
    return (
        layer_out,
        input_grad,
        fg,
        fb,
        router_g.T,
        key_g.T,
        value_g.T,
        jnp.transpose(query_grad.reshape(-1, head, width), (0, 2, 1)),
        output_grad.reshape(-1, head, width),
        sg,
        sb,
        hidden_grad,
        hb,
        return_grad,
        rb,
    )


def solution(mesh):
    rows = P(AXES, None)
    cut = P("expert", None, None)
    in_specs = (
        (rows, rows, P("dp", None, None), P("dp", None, None, None))
        + (P(),) * 5
        + (cut, cut)
        + (P(),) * 6
    )
    out_specs = (rows, rows) + (P(),) * 5 + (cut, cut) + (P(),) * 6
    return jax.shard_map(local, mesh=mesh, in_specs=in_specs, out_specs=out_specs, check_vma=False)
```

```python
import functools

import jax
import jax.numpy as jnp
from jax import lax
from jax.experimental import pallas as pl
from jax.experimental.pallas import tpu as pltpu
from jax.sharding import PartitionSpec as P

AXES = ("dp", "expert")
WIDE = jnp.float32
LOW = jnp.bfloat16
EPS = 1e-05
MASKED = -1e30
REACH = 40.0
ROWS = 256
SPAN = 512
CURVE = 0.7978845608028654
CUBIC = 0.044715
VMEM_LIMIT = 16 * 1024 * 1024


def low(values):
    return values.astype(LOW)


def wide(values):
    return values.astype(WIDE)


def dot_nn(left_op, right_op):
    return lax.dot_general(
        left_op, right_op, (((1,), (0,)), ((), ())), preferred_element_type=WIDE
    )


def dot_tn(left_op, right_op):
    return lax.dot_general(
        left_op, right_op, (((0,), (0,)), ((), ())), preferred_element_type=WIDE
    )


def dot_nt(left_op, right_op):
    return lax.dot_general(
        left_op, right_op, (((1,), (1,)), ((), ())), preferred_element_type=WIDE
    )


def norm_parts(values):
    row_mean = jnp.mean(values, axis=-1, keepdims=True)
    centred = values - row_mean
    inv_dev = lax.rsqrt(jnp.mean(centred * centred, axis=-1, keepdims=True) + EPS)
    return centred * inv_dev, inv_dev


def norm_back(d_out, unit, inv_dev, gain_vec):
    weighted = d_out * gain_vec
    mean_w = jnp.mean(weighted, axis=-1, keepdims=True)
    mean_wn = jnp.mean(weighted * unit, axis=-1, keepdims=True)
    return inv_dev * (weighted - mean_w - unit * mean_wn)


def core_here():
    return lax.axis_index("expert")


def segment_of(places, ends):
    return sum((places >= end).astype(jnp.int32) for end in ends)


def held(shape, dtype):
    return pltpu.VMEM(shape, dtype)


def there(shape, dtype):
    return jax.ShapeDtypeStruct(shape, dtype)


ANYWHERE = pl.BlockSpec(memory_space=pl.ANY)
INSIDE = pl.BlockSpec(memory_space=pltpu.VMEM)


class Program:
    def __init__(self):
        self.before = []

    def call(self, kernel, name, operands, out_shape, scratch=(), far=(), far_out=0, aliases=()):
        operands = [pltpu.with_memory_space_constraint(v, pltpu.VMEM) for v in operands]
        if not aliases:
            far = [pltpu.with_memory_space_constraint(v, pltpu.HBM) for v in far]
        count, waits = len(operands) + len(far), len(self.before)

        def run(*refs):
            kernel(*refs[:count], *refs[count + waits :])

        single = not isinstance(out_shape, (list, tuple))
        outs = [out_shape] if single else list(out_shape)
        near = len(outs) - far_out
        result = pl.pallas_call(
            run,
            in_specs=[INSIDE] * len(operands) + [ANYWHERE] * (len(far) + waits),
            out_specs=[INSIDE] * near + [ANYWHERE] * far_out,
            out_shape=outs,
            scratch_shapes=list(scratch),
            input_output_aliases={len(operands) + a: near + b for a, b in aliases},
            compiler_params=pltpu.CompilerParams(vmem_limit_bytes=VMEM_LIMIT),
            cost_estimate=pl.CostEstimate(flops=3 * 10**10 if name == "place_got_0" else 10**10, bytes_accessed=1, transcendentals=0),
            name=name,
        )(*operands, *far, *self.before)
        self.before = [result[0]]
        return result[0] if single else result


FIRST_GAIN, FIRST_BIAS, SECOND_GAIN, SECOND_BIAS, RETURN_BIAS, HIDDEN_BIAS = range(6)
SLOTS = 4
PARTS = 8


def bias_row(vecs, unit, cols):
    row = vecs[pl.ds(HIDDEN_BIAS + unit // 2, 1), :]
    return jnp.where(unit % 2 == 0, row[:, :cols], row[:, cols:])


def open_kernel(
    x_far, lengths_far, first_gain_far, first_bias_far, key_far, value_far, router_far, q_far,
    o_far, second_gain_far, second_bias_far, return_bias_far, hidden_bias_far, routes_far,
    normed, vecs, keys_ext, key_t, value_n, values_ext, logits, x, q_own, o_own, key_w, value_w,
    router_w, routes, ends_out,
    lengths, first_gain, first_bias, second_gain, second_bias, return_bias, hidden_bias, sems,
):
    spans = [slice(at, at + ROWS) for at in range(0, x.shape[0], ROWS)]
    moves = [(x_far.at[here, :], x.at[here, :]) for here in spans]
    needed = [
        (lengths_far, lengths), (first_gain_far, first_gain), (first_bias_far, first_bias),
        (key_far, key_w), (value_far, value_w), (router_far, router_w),
    ]
    later = [
        (q_far, q_own), (o_far, o_own), (second_gain_far, second_gain),
        (second_bias_far, second_bias), (return_bias_far, return_bias),
        (hidden_bias_far, hidden_bias), (routes_far.at[core_here()], routes),
    ]
    moves = moves[:1] + needed + moves[1:] + later
    copies = [pltpu.make_async_copy(*move, sems.at[j]) for j, move in enumerate(moves)]
    for copy in copies:
        copy.start()
    for copy in copies[: len(needed) + len(spans)]:
        copy.wait()
    head = key_w.shape[0]
    width = x.shape[1]
    ends, end = [], 0
    for slot in range(lengths.shape[1]):
        end = end + lengths[core_here(), slot]
        ends.append(end)
        ends_out[slot : slot + 1, :] = jnp.full((1, ends_out.shape[1]), end, jnp.int32)
    vecs[...] = jnp.zeros_like(vecs)
    for j, vec in enumerate((first_gain, first_bias)):
        vecs[j : j + 1, :] = wide(vec[...]).reshape(1, width)
    pair_w = jnp.concatenate([key_w[...], value_w[...]], axis=0)
    all_w = jnp.concatenate([key_w[...], value_w[...], router_w[...]], axis=0)
    for j, here in enumerate(spans):
        at = j * ROWS
        unit, _ = norm_parts(wide(x[here, :]))
        rows = low(
            unit * vecs[FIRST_GAIN : FIRST_GAIN + 1, :] + vecs[FIRST_BIAS : FIRST_BIAS + 1, :]
        )
        normed[here, :] = rows
        across = dot_nt(all_w, rows)
        key_t[:, here] = low(across[:head, :])
        values_ext[:head, here] = low(across[head : 2 * head, :])
        values_ext[head:, here] = jnp.ones((values_ext.shape[0] - head, ROWS), LOW)
        logits[:, here] = across[2 * head :, :]
        along = low(dot_nt(rows, pair_w))
        places = at + lax.broadcasted_iota(jnp.int32, (ROWS, head), 0)
        lanes = lax.broadcasted_iota(jnp.int32, (ROWS, head), 1)
        marks = low(jnp.where(segment_of(places, ends) == lanes, 1.0, 0.0))
        keys_ext[here, :] = jnp.concatenate([along[:, :head], marks], axis=1)
        value_n[here, :] = jnp.concatenate(
            [along[:, head:], jnp.ones((ROWS, head), LOW)], axis=1
        )
    for copy in copies[len(needed) + len(spans) :]:
        copy.wait()
    for j, vec in enumerate((second_gain, second_bias, return_bias)):
        vecs[SECOND_GAIN + j : SECOND_GAIN + j + 1, :] = wide(vec[...]).reshape(1, width)
    for j in range(hidden_bias.shape[0] // width):
        part = hidden_bias[j * width : (j + 1) * width]
        vecs[HIDDEN_BIAS + j : HIDDEN_BIAS + j + 1, :] = wide(part).reshape(1, width)


def expert_hits(route, experts):
    own = experts // 2
    relative = lax.rem(route - core_here() * own + experts, experts)
    return [relative == e for e in range(experts)]


def forward_kernel(
    normed, x, vecs, q_own, q_other, o_own, o_other, keys_ext, values_ext, logits, routes, ends_in,
    key_t, cot_far, hidden_w_far, return_w_far,
    exps, q_sel, attended, row_facts, placed, middle, hidden_in, hidden_in_t, d_feed, d_feed_t,
    bias_grad, cot, hidden_w, return_w, spread, sems,
):
    moves = ((cot_far, cot), (hidden_w_far, hidden_w), (return_w_far, return_w))
    copies = [pltpu.make_async_copy(*move, sems.at[j]) for j, move in enumerate(moves)]
    for copy in copies:
        copy.start()
    ends = [ends_in[slot, 0] for slot in range(SLOTS)]
    head = q_sel.shape[0]
    tok, half = x.shape[0], q_own.shape[0]
    experts = 2 * half // head
    own = experts // 2
    q_all = [low(dot_nt(q_own[...], normed[...])), low(dot_nt(q_other[...], normed[...]))]
    hits = [expert_hits(routes[m : m + 1, :], experts) for m in range(2)]
    places = lax.broadcasted_iota(jnp.int32, (head, tok), 1)
    subs = lax.broadcasted_iota(jnp.int32, (head, tok), 0)
    fence = low(jnp.where(segment_of(places, ends) == subs, 0.0, MASKED))
    for m in range(2):
        query = jnp.zeros((head, tok), LOW)
        for e in range(experts):
            from_e = q_all[e // own][(e % own) * head : (e % own + 1) * head, :]
            query = jnp.where(hits[m][e], from_e, query)
        lanes = slice(m * tok, (m + 1) * tok)
        q_sel[:, lanes] = query
        spread[:head, lanes] = low(wide(query) * head**-0.5)
        spread[head:, lanes] = fence

    def scores_of(here):
        return dot_nn(keys_ext[...], spread[:, here])

    def attend(here, powers):
        exps[:, here] = powers
        summed = dot_nn(values_ext[...], powers)
        inv = 1.0 / summed[head : head + 1, :]
        attended[:, here] = summed[:head, :] * inv
        row_facts[1:2, here] = inv

    longest_query = jnp.max(jnp.sum(jnp.square(wide(spread[:head, :])), axis=0, keepdims=True))
    longest_key = jnp.max(jnp.sum(jnp.square(wide(key_t[...])), axis=0, keepdims=True))
    within = longest_query * longest_key < REACH * REACH

    @pl.when(within)
    def _():
        for at in range(0, 2 * tok, SPAN):
            here = slice(at, at + SPAN)
            attend(here, low(jnp.exp(scores_of(here))))

    @pl.when(jnp.logical_not(within))
    def _():
        @pl.loop(0, 2 * tok // SPAN)
        def _(turn):
            here = rows_at(turn, SPAN)
            scores = scores_of(here)
            attend(here, low(jnp.exp(scores - jnp.max(scores, axis=0, keepdims=True))))

    ids = lax.broadcasted_iota(jnp.int32, (experts, tok), 0)
    chosen = [
        jnp.sum(jnp.where(ids == routes[m : m + 1, :], logits[...], 0.0), axis=0, keepdims=True)
        for m in range(2)
    ]
    top = jnp.maximum(chosen[0], chosen[1])
    lifts = [jnp.exp(c - top) for c in chosen]
    inv_sum = 1.0 / (lifts[0] + lifts[1])
    gated = []
    for m in range(2):
        lanes = slice(m * tok, (m + 1) * tok)
        gate = lifts[m] * inv_sum
        row_facts[0:1, lanes] = gate
        gated.append(attended[:, lanes] * gate)
    for e in range(experts):
        placed[e * head : (e + 1) * head, :] = low(
            jnp.where(hits[0][e], gated[0], jnp.where(hits[1][e], gated[1], 0.0))
        )
    copies[0].wait()
    total = jnp.zeros(bias_grad.shape, WIDE)
    for at in range(0, tok, SPAN):
        here = slice(at, at + SPAN)
        branch = dot_tn(placed[:half, here], o_own[...]) + dot_tn(placed[half:, here], o_other[...])
        spots = at + lax.broadcasted_iota(jnp.int32, (SPAN, 1), 0)
        mid = wide(x[here, :]) + jnp.where(spots < ends[-1], branch, 0.0)
        middle[here, :] = mid
        unit, _ = norm_parts(mid)
        hidden = (
            unit * vecs[SECOND_GAIN : SECOND_GAIN + 1, :] + vecs[SECOND_BIAS : SECOND_BIAS + 1, :]
        )
        hidden_in[here, :] = low(hidden)
        hidden_in_t[:, here] = low(hidden.T)
        masked = jnp.where(spots < ends[-1], wide(cot[here, :]), 0.0)
        d_feed[here, :] = low(masked)
        d_feed_t[:, here] = low(masked.T)
        total = total + jnp.sum(masked, axis=0, keepdims=True)
    bias_grad[...] = total
    for copy in copies[1:]:
        copy.wait()


def feed_kernel(
    units_of, joint, hidden_in, hidden_in_t, d_feed, d_feed_t, vecs, hidden_w, return_w, *outs
):
    units = units_of()
    grads_all = outs[-1] if joint else None
    for j, unit in enumerate(units):
        act, d_before, bias_grad = outs[3 * j : 3 * j + 3]
        cols = act.shape[1]
        at = rows_at(unit, cols)
        weight_in, weight_out = hidden_w[:, at], return_w[at, :]
        bias = bias_row(vecs, unit, cols)
        bias_sum = jnp.zeros(bias_grad.shape, WIDE)
        for row in range(0, act.shape[0], ROWS):
            here = slice(row, row + ROWS)
            x = dot_nn(hidden_in[here, :], weight_in) + bias
            d_act = dot_nt(d_feed[here, :], weight_out)
            squared = x * x
            rise = 0.5 + 0.5 * jnp.tanh(x * (CURVE + CURVE * CUBIC * squared))
            out = x * rise
            slope = rise + out * (1.0 - rise) * (2 * CURVE + 6 * CURVE * CUBIC * squared)
            act[here, :] = low(out)
            d_x = d_act * slope
            d_before[here, :] = low(d_x)
            bias_sum = bias_sum + jnp.sum(d_x, axis=0, keepdims=True)
        bias_grad[...] = bias_sum
        width = hidden_in.shape[1]
        rows = slice(j * width, (j + 1) * width)
        grads_all[rows, :cols] = low(dot_nn(hidden_in_t[...], d_before[...]))
        grads_all[rows, cols:] = low(dot_nn(d_feed_t[...], act[...]))


def spans_of(units, cols):
    return [rows_at(unit, cols) for unit in units]


def middle_kernel(units_of, *refs):
    d_befores, (hidden_w, vecs, middle, cot, ends_in) = refs[:PARTS], refs[PARTS : PARTS + 5]
    d_middle, d_low, gain_grad, bias_grad = refs[PARTS + 5 :]
    end = ends_in[SLOTS - 1, 0]
    spans = spans_of(units_of(), d_befores[0].shape[1])
    gain = vecs[SECOND_GAIN : SECOND_GAIN + 1, :]
    gain_sum = jnp.zeros(gain_grad.shape, WIDE)
    bias_sum = jnp.zeros(bias_grad.shape, WIDE)
    for at in range(0, middle.shape[0], ROWS):
        here = slice(at, at + ROWS)
        d_hidden = 0.0
        for part, span in zip(d_befores, spans):
            d_hidden = d_hidden + dot_nt(part[here, :], hidden_w[:, span])
        valid = at + lax.broadcasted_iota(jnp.int32, (ROWS, 1), 0) < end
        unit, inv = norm_parts(middle[here, :])
        d_mid = wide(cot[here, :]) + norm_back(d_hidden, unit, inv, gain)
        d_middle[here, :] = d_mid
        d_low[here, :] = low(jnp.where(valid, d_mid, 0.0))
        gain_sum = gain_sum + jnp.sum(d_hidden * unit, axis=0, keepdims=True)
        bias_sum = bias_sum + jnp.sum(d_hidden, axis=0, keepdims=True)
    gain_grad[...] = gain_sum
    bias_grad[...] = bias_sum


def rows_out(near, far, sems, compute):
    blocks = near.shape[0] // ROWS

    def leaving(turn):
        here = rows_at(turn, ROWS)
        return pltpu.make_async_copy(near.at[here, :], far.at[here, :], sems.at[turn])

    @pl.loop(0, blocks)
    def _(turn):
        compute(rows_at(turn, ROWS), turn * ROWS)
        leaving(turn).start()

    for turn in range(blocks):
        leaving(turn).wait()


def layer_kernel(units_of, *refs):
    acts, (return_w, vecs, middle, ends_in) = refs[:PARTS], refs[PARTS : PARTS + 4]
    token, far, near, sems = refs[PARTS + 4 :]
    token[...] = jnp.zeros_like(token)
    end = ends_in[SLOTS - 1, 0]
    spans = spans_of(units_of(), acts[0].shape[1])

    def compute(here, at):
        feed = vecs[RETURN_BIAS : RETURN_BIAS + 1, :]
        for part, span in zip(acts, spans):
            feed = feed + dot_nn(part[here, :], return_w[span, :])
        valid = at + lax.broadcasted_iota(jnp.int32, (ROWS, 1), 0) < end
        near[here, :] = middle[here, :] + jnp.where(valid, feed, 0.0)

    rows_out(near, far, sems, compute)


def attention_back_kernel(
    d_low, exps, q_sel, attended, row_facts, placed, key_t, value_n, o_own, o_other, routes,
    d_stack, grad_o, spread, d_scores, d_queries,
):
    head = key_t.shape[0]
    tok, half = d_low.shape[0], o_own.shape[0]
    experts = 2 * half // head
    own = experts // 2
    scale = head**-0.5
    d_all = [dot_nt(o_own[...], d_low[...]), dot_nt(o_other[...], d_low[...])]
    hits = [expert_hits(routes[m : m + 1, :], experts) for m in range(2)]
    halves = [slice(m * tok, (m + 1) * tok) for m in range(2)]
    gates = [row_facts[0:1, lanes] for lanes in halves]
    subs = lax.broadcasted_iota(jnp.int32, (head, tok), 0)
    d_gates = []
    for m, lanes in enumerate(halves):
        d_raw = jnp.zeros((head, tok), WIDE)
        for e in range(experts):
            from_e = d_all[e // own][(e % own) * head : (e % own + 1) * head, :]
            d_raw = jnp.where(hits[m][e], from_e, d_raw)
        att = attended[:, lanes]
        d_gates.append(jnp.sum(d_raw * att, axis=0, keepdims=True))
        d_att = low(d_raw * (gates[m] * row_facts[1:2, lanes]))
        inner = jnp.sum(wide(d_att) * att, axis=0, keepdims=True)
        inner_high = wide(low(inner))
        tail = jnp.where(subs == 0, -inner_high, jnp.where(subs == 1, inner_high - inner, 0.0))
        spread[:head, lanes] = d_att
        spread[head:, lanes] = low(tail)
    mean_gate = gates[0] * d_gates[0] + gates[1] * d_gates[1]
    ids = lax.broadcasted_iota(jnp.int32, (experts, tok), 0)
    d_logits = sum(
        jnp.where(ids == routes[m : m + 1, :], gates[m] * (d_gates[m] - mean_gate), 0.0)
        for m in range(2)
    )
    high = wide(low(d_logits))
    d_stack[2 * half + 2 * head :, :] = low(jnp.concatenate([high, d_logits - high], axis=0))

    def d_probs_of(at):
        return dot_nn(value_n[...], spread[:, at : at + ROWS])

    d_probs = d_probs_of(0)
    for at in range(0, 2 * tok, ROWS):
        later = d_probs_of(at + ROWS) if at + ROWS < 2 * tok else None
        here = slice(at, at + ROWS)
        d_score = low(wide(exps[:, here]) * d_probs)
        d_scores[:, here] = d_score
        d_queries[:, here] = dot_nn(key_t[...], d_score) * scale
        d_probs = later
    d_values = dot_nt(exps[...], spread[:head, :])
    d_keys = dot_nt(d_scores[...], q_sel[...]) * scale
    d_stack[2 * half : 2 * half + head, :] = low(d_keys.T)
    d_stack[2 * half + head : 2 * half + 2 * head, :] = low(d_values.T)
    first, second = d_queries[:, halves[0]], d_queries[:, halves[1]]
    for e in range(experts):
        d_stack[e * head : (e + 1) * head, :] = low(
            jnp.where(hits[0][e], first, jnp.where(hits[1][e], second, 0.0))
        )
    grad_o[...] = dot_nn(placed[...], d_low[...])


def close_kernel(
    units_of, d_stack, grad_o, q_own, q_other, normed, vecs, return_bias_grad, second_gain_grad,
    second_bias_grad, key_w, value_w, router_w, *rest,
):
    bias_parts, (own_grads, other_grads, common) = rest[:PARTS], rest[PARTS:]
    half, head, experts = q_own.shape[0], key_w.shape[0], router_w.shape[0]
    owned = at_kv = 2 * half
    rows_in = normed[...]
    parts = ((0, half, q_own[...]), (half, at_kv, q_other[...]))
    tail_w = jnp.concatenate([key_w[...], value_w[...], router_w[...], router_w[...]], axis=0)
    parts = parts + ((at_kv, d_stack.shape[0], tail_w),)
    bias_sum, product_sum, grads = 0.0, 0.0, []
    for start, stop, weights in parts:
        stack = d_stack[start:stop, :]
        grad = dot_nn(stack, rows_in)
        grads.append(grad)
        row_sums = jnp.sum(wide(stack), axis=1, keepdims=True)
        bias_sum = bias_sum + jnp.sum(row_sums * wide(weights), axis=0, keepdims=True)
        product_sum = product_sum + jnp.sum(grad * wide(weights), axis=0, keepdims=True)
    gain = vecs[FIRST_GAIN : FIRST_GAIN + 1, :]
    gain_sum = (product_sum - vecs[FIRST_BIAS : FIRST_BIAS + 1, :] * bias_sum) / gain
    own_grads[:half, :] = low(grads[0])
    other_grads[:half, :] = low(grads[1])
    own_grads[half:owned, :] = low(grad_o[:half, :])
    other_grads[half:owned, :] = low(grad_o[half:, :])
    tail = grads[2]
    common[...] = jnp.zeros_like(common)
    common[: 2 * head, :] = tail[: 2 * head, :]
    row = 2 * head
    common[row : row + experts, :] = (
        tail[2 * head : 2 * head + experts, :] + tail[2 * head + experts :, :]
    )
    row = row + experts
    rows = (gain_sum, bias_sum, second_gain_grad[...], second_bias_grad[...], return_bias_grad[...])
    for j, values in enumerate(rows):
        common[row + j : row + j + 1, :] = values
    for unit, part in zip(units_of(), bias_parts):
        cols = part.shape[1]
        at = pl.ds(row + HIDDEN_BIAS + unit // 2, 1)
        there_now = common[at, :]
        doubled = jnp.concatenate([part[...], part[...]], axis=1)
        lanes = lax.broadcasted_iota(jnp.int32, doubled.shape, 1)
        common[at, :] = jnp.where(lanes // cols == unit % 2, doubled, there_now)
    own_grads[owned:, :] = low(common[...])
    other_grads[owned:, :] = low(common[...])


def input_kernel(
    d_stack, q_own, q_other, key_w, value_w, router_w, x, d_middle, vecs,
    token, far, near, sems,
):
    token[...] = jnp.zeros_like(token)
    half = q_own.shape[0]
    at_kv = 2 * half
    tail_w = jnp.concatenate([key_w[...], value_w[...], router_w[...], router_w[...]], axis=0)
    gain = vecs[FIRST_GAIN : FIRST_GAIN + 1, :]

    def compute(here, at):
        d_normed = dot_tn(d_stack[:half, here], q_own[...])
        d_normed = d_normed + dot_tn(d_stack[half:at_kv, here], q_other[...])
        d_normed = d_normed + dot_tn(d_stack[at_kv:, here], tail_w)
        unit, inv = norm_parts(wide(x[here, :]))
        near[here, :] = d_middle[here, :] + norm_back(d_normed, unit, inv, gain)

    rows_out(near, far, sems, compute)


def halvings(n_dp):
    return n_dp.bit_length() - 3


def step_orders(n_dp):
    first = list(range(halvings(n_dp)))
    second = []
    for at in range(0, len(first), 2):
        second += first[at : at + 2][::-1]
    return first, second


def pairs_of(n_dp, step):
    orders = step_orders(n_dp)
    return [
        (chip * 2 + core, (chip ^ (1 << orders[core][step])) * 2 + core)
        for chip in range(n_dp)
        for core in range(2)
    ]


def quad_pairs(n_dp, turn):
    return [
        (chip * 2 + core, (chip ^ (turn << halvings(n_dp))) * 2 + core)
        for chip in range(n_dp)
        for core in range(2)
    ]


def cross_pairs(n_dp, turn):
    low_bit = halvings(n_dp)
    return [
        (chip * 2 + core, (chip ^ (1 << (low_bit + turn))) * 2 + core)
        for chip in range(n_dp)
        for core in range(2)
    ]


def core_swap(values, n_dp):
    return lax.ppermute(values, AXES, [(at, at ^ 1) for at in range(2 * n_dp)])


def bit_here(n_dp, step, core=None):
    first, second = step_orders(n_dp)
    chip = lax.axis_index("dp")
    core = core_here() if core is None else core
    return jnp.where(core == 0, chip >> first[step], chip >> second[step]) & 1


def units_here(n_dp, entries):
    core = core_here()
    mine, theirs = bit_here(n_dp, 0), bit_here(n_dp, 0, 1 - core)
    other = 1 - core
    blocks = [2 * other + 1 - theirs, 2 * core + 1 - mine, 2 * other + theirs, 2 * core + mine]
    return [2 * blocks[entry // 2] + entry % 2 for entry in entries]


def rows_at(index, size):
    return pl.ds(pl.multiple_of(index * size, size), size)


def add_kernel(*refs):
    total = wide(refs[0][...])
    for ref in refs[1:-1]:
        total = total + wide(ref[...])
    refs[-1][...] = low(total)


def rows_of(ref, at, size):
    return wide(ref[pl.ds(pl.multiple_of(at, size), size), :])


def partial_sum(n_dp, terms, step, last_kept):
    start = step - len(terms) + 1
    size = terms[0][0].shape[0] >> (step - start + 1)
    at, total = 0, 0.0
    for j in range(step, start - 1, -1):
        bit = bit_here(n_dp, j)
        bit = bit if last_kept or j < step else 1 - bit
        at = at + bit * (size << (step - j))
        for ref in terms[j - start]:
            total = total + rows_of(ref, at, size)
    return total


def group(refs, counts):
    refs = list(refs)
    return [[refs.pop(0) for _ in range(count)] for count in counts]


def split_terms(terms, joint):
    parts = []
    for part in range(2):
        chosen = []
        for refs, flags in zip(terms, joint):
            chosen.append([])
            for ref, flag in zip(refs, flags):
                half = ref.shape[0] // 2
                if flag == 2:
                    chosen[-1].append(ref.at[pl.ds(part * half, half), :])
                elif flag == part:
                    chosen[-1].append(ref)
        parts.append(chosen)
    return parts


def send_kernel(n_dp, step, counts, joint, *refs):
    out = refs[-1]
    terms = group(refs[:-1], counts)
    if joint is None:
        out[...] = low(partial_sum(n_dp, terms, step, False))
        return
    size = out.shape[0] // 2
    for part, chosen in enumerate(split_terms(terms, joint)):
        out[part * size : (part + 1) * size, :] = low(partial_sum(n_dp, chosen, step, False))


def kept_kernel(n_dp, step, counts, *refs):
    *terms, last = group(refs[:-1], counts)
    refs[-1][...] = low(partial_sum(n_dp, terms, step, True) + wide(last[0][...]))


def spot_here(n_dp, turn):
    return jnp.bitwise_xor(lax.axis_index("dp") >> halvings(n_dp), turn)


def quarters_kernel(n_dp, step, counts, joint, *refs):
    count = sum(counts)
    terms = group(refs[:count], counts)
    outs, total = refs[count:-1], refs[-1]
    size = total.shape[0] // 2
    for part, (*chosen, last) in enumerate(split_terms(terms, joint)):
        total[part * size : (part + 1) * size, :] = partial_sum(
            n_dp, chosen, step, True
        ) + wide(last[0][...])
    cols = outs[0].shape[1]
    for turn, out in enumerate(outs):
        out[...] = low(total[:, rows_at(spot_here(n_dp, turn), cols)])


def row_of_four(n_dp, part, *refs):
    pieces, out = refs[:4], refs[4]
    size, cols = out.shape[0], pieces[0].shape[1]
    for turn, piece in enumerate(pieces):
        at = rows_at(spot_here(n_dp, turn), cols)
        out[:, at] = piece[part * size : (part + 1) * size, :]


def join_kernel(n_dp, step, mine, got, out):
    size = mine.shape[0]
    bit = bit_here(n_dp, step)
    out[rows_at(bit, size), :] = mine[...]
    out[rows_at(1 - bit, size), :] = got[...]


def pass_kernel(source, out):
    out[...] = source[...]


def stack_kernel(first, second, out):
    size = first.shape[0]
    out[:size, :] = first[...]
    out[size:, :] = second[...]


def place_kernel(units_of, count, more, *refs):
    hidden, returned, left, right, sems = refs[-5:]
    copies = []
    width = left.shape[1]
    parts = []
    for ref in refs[:count]:
        parts += [ref.at[pl.ds(row, width), :] for row in range(0, ref.shape[0], width)]
    for j, (unit, part) in enumerate(zip(units_of(), parts)):
        cols = part.shape[1] // 2
        at = rows_at(unit, cols)
        left[j] = wide(part[:, :cols])
        copies.append(pltpu.make_async_copy(left.at[j], hidden.at[:, at], sems.at[2 * j]))
        copies[-1].start()
        right[j] = wide(part[:, cols:]).T
        copies.append(pltpu.make_async_copy(right.at[j], returned.at[at, :], sems.at[2 * j + 1]))
        copies[-1].start()
    if more:
        refs[-6][...] = jnp.zeros_like(refs[-6])
    for copy in copies:
        copy.wait()


def finish_kernel(n_dp, mine, got, token, query_g, output_g, key_g, value_g, router_g, *refs):
    vectors, whole = refs[:-1], refs[-1]
    token[...] = jnp.zeros_like(token)
    size, width = mine.shape
    bit = bit_here(n_dp, 0)
    whole[rows_at(bit, size), :] = wide(mine[...])
    whole[rows_at(1 - bit, size), :] = wide(got[...])
    row = 0
    for out in (query_g, output_g, key_g, value_g, router_g):
        out[...] = whole[row : row + out.shape[0], :]
        row = row + out.shape[0]
    for j, vector in enumerate(vectors[:-1]):
        vector[...] = whole[row + j, :]
    row = row + len(vectors) - 1
    for j in range(vectors[-1].shape[0] // width):
        vectors[-1][j * width : (j + 1) * width] = whole[row + j, :]


def local(
    inputs, cotangent, lengths, routes, first_gain, first_bias, router_weight, key_weight,
    value_weight, query_weight, output_weight, second_gain, second_bias, hidden_weight,
    hidden_bias, return_weight, return_bias,
):
    tok, width = inputs.shape
    ff = hidden_weight.shape[1]
    n_dp = lax.axis_size("dp")
    own, _, head = query_weight.shape
    experts = 2 * own
    half = own * head
    blocks = tok // ROWS

    q_own = jnp.transpose(query_weight, (0, 2, 1)).reshape(half, width)
    o_own = output_weight.reshape(half, width)
    q_other, o_other = core_swap(q_own, n_dp), core_swap(o_own, n_dp)
    vec_rows = 5 + ff // width
    program = Program()
    call = program.call
    (
        normed, vecs, keys_ext, key_t, value_n, values_ext, logits, x, q_own, o_own, key_w, value_w,
        router_w, routes, ends,
    ) = call(
        open_kernel, "first_norm", [],
        [
            held((tok, width), LOW), held((vec_rows + -vec_rows % 8, width), WIDE),
            held((tok, 2 * head), LOW), held((head, tok), LOW), held((tok, 2 * head), LOW),
            held((head + 16, tok), LOW), held((experts, tok), WIDE), held((tok, width), LOW),
            held((half, width), LOW), held((half, width), LOW), held((head, width), LOW),
            held((head, width), LOW), held((experts, width), LOW), held((2, tok), jnp.int32),
            held((8, 128), jnp.int32),
        ],
        scratch=[pltpu.SMEM(lengths.shape[1:], jnp.int32)]
        + [pltpu.VMEM((width,), LOW)] * 5
        + [pltpu.VMEM((ff,), LOW), pltpu.SemaphoreType.DMA((blocks + 13,))],
        far=[
            inputs, lengths[0], first_gain, first_bias, key_weight.T, value_weight.T,
            router_weight.T, q_own, o_own, second_gain, second_bias, return_bias, hidden_bias,
            jnp.transpose(routes[0], (0, 2, 1)),
        ],
    )
    (
        exps, q_sel, attended, row_facts, placed, middle, hidden_in, hidden_in_t, d_feed, d_feed_t,
        return_bias_grad, cot, hidden_w, return_w,
    ) = call(
        forward_kernel, "attention_forward",
        [
            normed, x, vecs, q_own, q_other, o_own, o_other, keys_ext, values_ext, logits, routes,
            ends, key_t,
        ],
        [
            held((tok, 2 * tok), LOW), held((head, 2 * tok), LOW), held((head, 2 * tok), WIDE),
            held((8, 2 * tok), WIDE), held((2 * half, tok), LOW), held((tok, width), WIDE),
            held((tok, width), LOW), held((width, tok), LOW), held((tok, width), LOW),
            held((width, tok), LOW), held((1, width), WIDE), held((tok, width), LOW),
            held(hidden_weight.shape, LOW), held(return_weight.shape, LOW),
        ],
        scratch=[pltpu.VMEM((2 * head, 2 * tok), LOW), pltpu.SemaphoreType.DMA((3,))],
        far=[cotangent, hidden_weight, return_weight],
    )

    cols = ff // PARTS
    units = lambda *entries: functools.partial(units_here, n_dp, entries)
    steps = halvings(n_dp)

    def feed(*entries):
        outs = call(
            functools.partial(feed_kernel, units(*entries), True), f"feed_{entries[0]}",
            [hidden_in, hidden_in_t, d_feed, d_feed_t, vecs, hidden_w, return_w],
            [held((tok, cols), LOW), held((tok, cols), LOW), held((1, cols), WIDE)] * len(entries)
            + [there((len(entries) * width, 2 * cols), LOW)],
        )
        return list(zip(*[iter(outs[:-1])] * 3)), outs[-1]

    def add(name, *terms):
        return call(add_kernel, name, terms, there(terms[0].shape, LOW))

    parts_a, theirs = feed(0)
    swapped = core_swap(theirs, n_dp)
    parts_c, mine = feed(2)
    sent_a = lax.ppermute(add("feed_add_0", mine, swapped), AXES, pairs_of(n_dp, 0))
    parts_b, theirs = feed(1)
    swapped = core_swap(theirs, n_dp)
    parts_d, mine = feed(3)
    sent_b = lax.ppermute(add("feed_add_1", mine, swapped), AXES, pairs_of(n_dp, 0))
    parts_e, theirs = feed(4, 5)
    swapped = core_swap(theirs, n_dp)
    parts_f, mine = feed(6, 7)
    parts = parts_a + parts_b + parts_c + parts_d + parts_e + parts_f

    every = units(*range(PARTS))
    d_middle, d_low, second_gain_grad, second_bias_grad = call(
        functools.partial(middle_kernel, every), "second_norm_back",
        [p[1] for p in parts] + [hidden_w, vecs, middle, cot, ends],
        [
            held((tok, width), WIDE), held((tok, width), LOW), held((1, width), WIDE),
            held((1, width), WIDE),
        ],
    )

    feed_terms, feed_joint = [[sent_a, sent_b, swapped, mine]], [[0, 1, 2, 2]]

    def feed_send(step):
        counts = [len(t) for t in feed_terms]
        part = call(
            functools.partial(send_kernel, n_dp, step, counts, list(feed_joint)),
            f"feed_send_{step}", sum(feed_terms, []), there((2 * width >> step, 2 * cols), LOW),
        )
        feed_terms.append([lax.ppermute(part, AXES, pairs_of(n_dp, step))])
        feed_joint.append([2])

    for step in range(1, steps):
        feed_send(step)
    d_stack, grad_o = call(
        attention_back_kernel, "attention_backward",
        [d_low, exps, q_sel, attended, row_facts, placed, key_t, value_n, o_own, o_other, routes],
        [held((2 * half + 2 * head + 2 * experts, tok), LOW), held((2 * half, width), WIDE)],
        scratch=[
            pltpu.VMEM((2 * head, 2 * tok), LOW), pltpu.VMEM((tok, 2 * tok), LOW),
            pltpu.VMEM((head, 2 * tok), WIDE),
        ],
    )
    shared = 2 * head + experts + 5 + ff // width
    shared = shared + -(2 * half + shared) % (16 << steps)
    rows = 2 * half + shared
    own_grads, other_grads = call(
        functools.partial(close_kernel, every), "projection_grads",
        [
            d_stack, grad_o, q_own, q_other, normed, vecs, return_bias_grad, second_gain_grad,
            second_bias_grad, key_w, value_w, router_w, *[p[2] for p in parts],
        ],
        [there((rows, width), LOW), there((rows, width), LOW)],
        scratch=[pltpu.VMEM((shared, width), WIDE)],
    )

    def output(kernel, name, operands):
        _, out = call(
            kernel, name, operands, [held((8, 128), WIDE), there((tok, width), WIDE)],
            scratch=[pltpu.VMEM((tok, width), WIDE), pltpu.SemaphoreType.DMA((blocks,))],
            far_out=1,
        )
        return out

    rest_terms = [[own_grads, core_swap(other_grads, n_dp)]]
    counts = [len(t) for t in feed_terms]
    own_piece, *pieces = call(
        functools.partial(quarters_kernel, n_dp, steps - 1, counts, feed_joint), "feed_cut",
        sum(feed_terms, []), [there((2 * width >> (steps - 1), cols // 2), LOW)] * 4,
        scratch=[pltpu.VMEM((2 * width >> (steps - 1), 2 * cols), WIDE)],
    )

    def across(values):
        return [
            lax.ppermute(v, AXES, quad_pairs(n_dp, t + 1)) for t, v in enumerate(values)
        ]

    pieces = across(pieces)


    def rest_send(step):
        counts = [len(t) for t in rest_terms]
        part = call(
            functools.partial(send_kernel, n_dp, step, counts, None), f"rest_send_{step}",
            sum(rest_terms, []), there((rows >> (step + 1), width), LOW),
        )
        rest_terms.append([lax.ppermute(part, AXES, pairs_of(n_dp, step))])

    def join(name, step, mine, got):
        size, wide_cols = mine.shape
        kernel = functools.partial(join_kernel, n_dp, step)
        joined = call(kernel, name, [mine, got], there((2 * size, wide_cols), LOW))
        return joined, lax.ppermute(joined, AXES, pairs_of(n_dp, step - 1))

    written = None

    def place(name, entries, values, more=True):
        nonlocal written
        count = len(values)
        *_, one, two = call(
            functools.partial(place_kernel, units(*entries), count, more), name, values,
            [held((8, 128), WIDE)] * more + [there((width, ff), WIDE), there((ff, width), WIDE)],
            scratch=[
                pltpu.VMEM((len(entries), width, cols), WIDE),
                pltpu.VMEM((len(entries), cols, width), WIDE),
                pltpu.SemaphoreType.DMA((2 * len(entries),)),
            ],
            far=[] if written is None else written,
            far_out=2,
            aliases=[] if written is None else [(0, 0), (1, 1)],
        )
        written = [one, two]

    rest_send(0)
    layer_out = output(
        functools.partial(layer_kernel, every), "layer_out",
        [p[0] for p in parts] + [return_w, vecs, middle, ends],
    )
    for step in range(1, steps):
        rest_send(step)
    own_piece = add("feed_sum", own_piece, *pieces)
    pieces = across([own_piece] * 3)
    counts = [len(t) for t in rest_terms]
    rest = call(
        functools.partial(kept_kernel, n_dp, steps - 1, counts), "rest_sum", sum(rest_terms, []),
        there((rows >> steps, width), LOW),
    )
    rest_got = lax.ppermute(rest, AXES, cross_pairs(n_dp, 0))
    input_grad = output(
        input_kernel, "first_norm_back",
        [d_stack, q_own, q_other, key_w, value_w, router_w, x, d_middle, vecs],
    )
    size = own_piece.shape[0] // 2
    joined, got = [None] * 2, [None] * 2
    for part in range(2):
        joined[part] = call(
            functools.partial(row_of_four, n_dp, part), f"feed_row_{part}", [own_piece] + pieces,
            there((size, 2 * cols), LOW),
        )
        got[part] = lax.ppermute(joined[part], AXES, pairs_of(n_dp, steps - 1))
    rest = add("rest_add_0", rest, rest_got)
    rest_got = lax.ppermute(rest, AXES, cross_pairs(n_dp, 1))
    for step in reversed(range(1, steps)):
        for part in range(2):
            name = f"feed_join_{step}_{part}"
            joined[part], got[part] = join(name, step, joined[part], got[part])
            if step == 1:
                place(f"place_own_{part}", (6 + part,), [joined[part]])
                if part == 0:
                    rest = add("rest_add_1", rest, rest_got)
                    rest_got = lax.ppermute(rest, AXES, pairs_of(n_dp, steps - 1))
    both = call(stack_kernel, "feed_own", joined, there((2 * width, 2 * cols), LOW))
    other = core_swap(both, n_dp)
    far = []

    def place_got(part):
        row = call(pass_kernel, f"feed_got_{part}", [got[part]], there((width, 2 * cols), LOW))
        far.append(core_swap(row, n_dp))
        place(f"place_got_{part}", (2 + part,), [row])

    place_got(0)
    for step in reversed(range(1, steps)):
        rest, rest_got = join(f"rest_join_{step}", step, rest, rest_got)
    place("place_other", (4, 5), [other])
    place_got(1)
    place("place_far", (0, 1), far)
    vectors = [there((width,), WIDE)] * 5 + [there((ff,), WIDE)]
    _, query_grad, output_grad, key_g, value_g, router_g, fg, fb, sg, sb, rb, hb = call(
        functools.partial(finish_kernel, n_dp), "finish", [rest, rest_got],
        [held((8, 128), WIDE)] + [there((half, width), WIDE)] * 2 + [there((head, width), WIDE)] * 2
        + [there((experts, width), WIDE)] + vectors,
        scratch=[pltpu.VMEM((rows, width), WIDE)],
    )
    hidden_grad, return_grad = written
    return (
        layer_out,
        input_grad,
        fg,
        fb,
        router_g.T,
        key_g.T,
        value_g.T,
        jnp.transpose(query_grad.reshape(-1, head, width), (0, 2, 1)),
        output_grad.reshape(-1, head, width),
        sg,
        sb,
        hidden_grad,
        hb,
        return_grad,
        rb,
    )


def solution(mesh):
    rows = P(AXES, None)
    cut = P("expert", None, None)
    in_specs = (
        (rows, rows, P("dp", None, None), P("dp", None, None, None))
        + (P(),) * 5
        + (cut, cut)
        + (P(),) * 6
    )
    out_specs = (rows, rows) + (P(),) * 5 + (cut, cut) + (P(),) * 6
    return jax.shard_map(local, mesh=mesh, in_specs=in_specs, out_specs=out_specs, check_vma=False)
```

```python
import functools

import jax
import jax.numpy as jnp
from jax import lax
from jax.experimental import pallas as pl
from jax.experimental.pallas import tpu as pltpu
from jax.sharding import PartitionSpec as P

AXES = ("dp", "expert")
WIDE = jnp.float32
LOW = jnp.bfloat16
EPS = 1e-05
MASKED = -1e30
REACH = 40.0
ROWS = 256
SPAN = 512
CURVE = 0.7978845608028654
CUBIC = 0.044715
VMEM_LIMIT = 16 * 1024 * 1024


def low(values):
    return values.astype(LOW)


def wide(values):
    return values.astype(WIDE)


def dot_nn(left_op, right_op):
    return lax.dot_general(
        left_op, right_op, (((1,), (0,)), ((), ())), preferred_element_type=WIDE
    )


def dot_tn(left_op, right_op):
    return lax.dot_general(
        left_op, right_op, (((0,), (0,)), ((), ())), preferred_element_type=WIDE
    )


def dot_nt(left_op, right_op):
    return lax.dot_general(
        left_op, right_op, (((1,), (1,)), ((), ())), preferred_element_type=WIDE
    )


def norm_parts(values):
    row_mean = jnp.mean(values, axis=-1, keepdims=True)
    centred = values - row_mean
    inv_dev = lax.rsqrt(jnp.mean(centred * centred, axis=-1, keepdims=True) + EPS)
    return centred * inv_dev, inv_dev


def norm_back(d_out, unit, inv_dev, gain_vec):
    weighted = d_out * gain_vec
    mean_w = jnp.mean(weighted, axis=-1, keepdims=True)
    mean_wn = jnp.mean(weighted * unit, axis=-1, keepdims=True)
    return inv_dev * (weighted - mean_w - unit * mean_wn)


def core_here():
    return lax.axis_index("expert")


def segment_of(places, ends):
    return sum((places >= end).astype(jnp.int32) for end in ends)


def held(shape, dtype):
    return pltpu.VMEM(shape, dtype)


def there(shape, dtype):
    return jax.ShapeDtypeStruct(shape, dtype)


ANYWHERE = pl.BlockSpec(memory_space=pl.ANY)
INSIDE = pl.BlockSpec(memory_space=pltpu.VMEM)


class Program:
    def __init__(self):
        self.before = []

    def call(self, kernel, name, operands, out_shape, scratch=(), far=(), far_out=0, aliases=()):
        operands = [pltpu.with_memory_space_constraint(v, pltpu.VMEM) for v in operands]
        if not aliases:
            far = [pltpu.with_memory_space_constraint(v, pltpu.HBM) for v in far]
        count, waits = len(operands) + len(far), len(self.before)

        def run(*refs):
            kernel(*refs[:count], *refs[count + waits :])

        single = not isinstance(out_shape, (list, tuple))
        outs = [out_shape] if single else list(out_shape)
        near = len(outs) - far_out
        result = pl.pallas_call(
            run,
            in_specs=[INSIDE] * len(operands) + [ANYWHERE] * (len(far) + waits),
            out_specs=[INSIDE] * near + [ANYWHERE] * far_out,
            out_shape=outs,
            scratch_shapes=list(scratch),
            input_output_aliases={len(operands) + a: near + b for a, b in aliases},
            compiler_params=pltpu.CompilerParams(vmem_limit_bytes=VMEM_LIMIT),
            cost_estimate=pl.CostEstimate(flops=3 * 10**10 if name == "place_got_0" else 10**10, bytes_accessed=1, transcendentals=0),
            name=name,
        )(*operands, *far, *self.before)
        self.before = [result[0]]
        return result[0] if single else result


FIRST_GAIN, FIRST_BIAS, SECOND_GAIN, SECOND_BIAS, RETURN_BIAS, HIDDEN_BIAS = range(6)
SLOTS = 4
PARTS = 8


def bias_row(vecs, unit, cols):
    row = vecs[pl.ds(HIDDEN_BIAS + unit // 2, 1), :]
    return jnp.where(unit % 2 == 0, row[:, :cols], row[:, cols:])


def open_kernel(
    x_far, lengths_far, first_gain_far, first_bias_far, key_far, value_far, router_far, q_far,
    o_far, second_gain_far, second_bias_far, return_bias_far, hidden_bias_far, routes_far,
    normed, vecs, keys_ext, key_t, value_n, values_ext, logits, x, q_own, o_own, key_w, value_w,
    router_w, routes, ends_out,
    lengths, first_gain, first_bias, second_gain, second_bias, return_bias, hidden_bias, sems,
):
    spans = [slice(at, at + ROWS) for at in range(0, x.shape[0], ROWS)]
    moves = [(x_far.at[here, :], x.at[here, :]) for here in spans]
    needed = [
        (lengths_far, lengths), (first_gain_far, first_gain), (first_bias_far, first_bias),
        (key_far, key_w), (value_far, value_w), (router_far, router_w),
    ]
    later = [
        (q_far, q_own), (o_far, o_own), (second_gain_far, second_gain),
        (second_bias_far, second_bias), (return_bias_far, return_bias),
        (hidden_bias_far, hidden_bias), (routes_far.at[core_here()], routes),
    ]
    moves = moves[:1] + needed + moves[1:] + later
    copies = [pltpu.make_async_copy(*move, sems.at[j]) for j, move in enumerate(moves)]
    for copy in copies:
        copy.start()
    for copy in copies[: len(needed) + len(spans)]:
        copy.wait()
    head = key_w.shape[0]
    width = x.shape[1]
    ends, end = [], 0
    for slot in range(lengths.shape[1]):
        end = end + lengths[core_here(), slot]
        ends.append(end)
        ends_out[slot : slot + 1, :] = jnp.full((1, ends_out.shape[1]), end, jnp.int32)
    vecs[...] = jnp.zeros_like(vecs)
    for j, vec in enumerate((first_gain, first_bias)):
        vecs[j : j + 1, :] = wide(vec[...]).reshape(1, width)
    pair_w = jnp.concatenate([key_w[...], value_w[...]], axis=0)
    all_w = jnp.concatenate([key_w[...], value_w[...], router_w[...]], axis=0)
    for j, here in enumerate(spans):
        at = j * ROWS
        unit, _ = norm_parts(wide(x[here, :]))
        rows = low(
            unit * vecs[FIRST_GAIN : FIRST_GAIN + 1, :] + vecs[FIRST_BIAS : FIRST_BIAS + 1, :]
        )
        normed[here, :] = rows
        across = dot_nt(all_w, rows)
        key_t[:, here] = low(across[:head, :])
        values_ext[:head, here] = low(across[head : 2 * head, :])
        values_ext[head:, here] = jnp.ones((values_ext.shape[0] - head, ROWS), LOW)
        logits[:, here] = across[2 * head :, :]
        along = low(dot_nt(rows, pair_w))
        places = at + lax.broadcasted_iota(jnp.int32, (ROWS, head), 0)
        lanes = lax.broadcasted_iota(jnp.int32, (ROWS, head), 1)
        marks = low(jnp.where(segment_of(places, ends) == lanes, 1.0, 0.0))
        keys_ext[here, :] = jnp.concatenate([along[:, :head], marks], axis=1)
        value_n[here, :] = jnp.concatenate(
            [along[:, head:], jnp.ones((ROWS, head), LOW)], axis=1
        )
    for copy in copies[len(needed) + len(spans) :]:
        copy.wait()
    for j, vec in enumerate((second_gain, second_bias, return_bias)):
        vecs[SECOND_GAIN + j : SECOND_GAIN + j + 1, :] = wide(vec[...]).reshape(1, width)
    for j in range(hidden_bias.shape[0] // width):
        part = hidden_bias[j * width : (j + 1) * width]
        vecs[HIDDEN_BIAS + j : HIDDEN_BIAS + j + 1, :] = wide(part).reshape(1, width)


def expert_hits(route, experts):
    own = experts // 2
    relative = lax.rem(route - core_here() * own + experts, experts)
    return [relative == e for e in range(experts)]


def forward_kernel(
    normed, x, vecs, q_own, q_other, o_own, o_other, keys_ext, values_ext, logits, routes, ends_in,
    key_t, cot_far, hidden_w_far, return_w_far,
    exps, q_sel, attended, row_facts, placed, middle, hidden_in, hidden_in_t, d_feed, d_feed_t,
    bias_grad, cot, hidden_w, return_w, spread, sems,
):
    moves = ((cot_far, cot), (hidden_w_far, hidden_w), (return_w_far, return_w))
    copies = [pltpu.make_async_copy(*move, sems.at[j]) for j, move in enumerate(moves)]
    for copy in copies:
        copy.start()
    ends = [ends_in[slot, 0] for slot in range(SLOTS)]
    head = q_sel.shape[0]
    tok, half = x.shape[0], q_own.shape[0]
    experts = 2 * half // head
    own = experts // 2
    q_all = [low(dot_nt(q_own[...], normed[...])), low(dot_nt(q_other[...], normed[...]))]
    hits = [expert_hits(routes[m : m + 1, :], experts) for m in range(2)]
    places = lax.broadcasted_iota(jnp.int32, (head, tok), 1)
    subs = lax.broadcasted_iota(jnp.int32, (head, tok), 0)
    fence = low(jnp.where(segment_of(places, ends) == subs, 0.0, MASKED))
    for m in range(2):
        query = jnp.zeros((head, tok), LOW)
        for e in range(experts):
            from_e = q_all[e // own][(e % own) * head : (e % own + 1) * head, :]
            query = jnp.where(hits[m][e], from_e, query)
        lanes = slice(m * tok, (m + 1) * tok)
        q_sel[:, lanes] = query
        spread[:head, lanes] = low(wide(query) * head**-0.5)
        spread[head:, lanes] = fence

    def scores_of(here):
        return dot_nn(keys_ext[...], spread[:, here])

    def attend(here, powers):
        exps[:, here] = powers
        summed = dot_nn(values_ext[...], powers)
        inv = 1.0 / summed[head : head + 1, :]
        attended[:, here] = summed[:head, :] * inv
        row_facts[1:2, here] = inv

    longest_query = jnp.max(jnp.sum(jnp.square(wide(spread[:head, :])), axis=0, keepdims=True))
    longest_key = jnp.max(jnp.sum(jnp.square(wide(key_t[...])), axis=0, keepdims=True))
    within = longest_query * longest_key < REACH * REACH

    @pl.when(within)
    def _():
        for at in range(0, 2 * tok, SPAN):
            here = slice(at, at + SPAN)
            attend(here, low(jnp.exp(scores_of(here))))

    @pl.when(jnp.logical_not(within))
    def _():
        @pl.loop(0, 2 * tok // SPAN)
        def _(turn):
            here = rows_at(turn, SPAN)
            scores = scores_of(here)
            attend(here, low(jnp.exp(scores - jnp.max(scores, axis=0, keepdims=True))))

    ids = lax.broadcasted_iota(jnp.int32, (experts, tok), 0)
    chosen = [
        jnp.sum(jnp.where(ids == routes[m : m + 1, :], logits[...], 0.0), axis=0, keepdims=True)
        for m in range(2)
    ]
    top = jnp.maximum(chosen[0], chosen[1])
    lifts = [jnp.exp(c - top) for c in chosen]
    inv_sum = 1.0 / (lifts[0] + lifts[1])
    gated = []
    for m in range(2):
        lanes = slice(m * tok, (m + 1) * tok)
        gate = lifts[m] * inv_sum
        row_facts[0:1, lanes] = gate
        gated.append(attended[:, lanes] * gate)
    for e in range(experts):
        placed[e * head : (e + 1) * head, :] = low(
            jnp.where(hits[0][e], gated[0], jnp.where(hits[1][e], gated[1], 0.0))
        )
    copies[0].wait()
    total = jnp.zeros(bias_grad.shape, WIDE)
    for at in range(0, tok, SPAN):
        here = slice(at, at + SPAN)
        branch = dot_tn(placed[:half, here], o_own[...]) + dot_tn(placed[half:, here], o_other[...])
        spots = at + lax.broadcasted_iota(jnp.int32, (SPAN, 1), 0)
        mid = wide(x[here, :]) + jnp.where(spots < ends[-1], branch, 0.0)
        middle[here, :] = mid
        unit, _ = norm_parts(mid)
        hidden = (
            unit * vecs[SECOND_GAIN : SECOND_GAIN + 1, :] + vecs[SECOND_BIAS : SECOND_BIAS + 1, :]
        )
        hidden_in[here, :] = low(hidden)
        hidden_in_t[:, here] = low(hidden.T)
        masked = jnp.where(spots < ends[-1], wide(cot[here, :]), 0.0)
        d_feed[here, :] = low(masked)
        d_feed_t[:, here] = low(masked.T)
        total = total + jnp.sum(masked, axis=0, keepdims=True)
    bias_grad[...] = total
    for copy in copies[1:]:
        copy.wait()


def feed_kernel(
    units_of, joint, hidden_in, hidden_in_t, d_feed, d_feed_t, vecs, hidden_w, return_w, *outs
):
    units = units_of()
    grads_all = outs[-1] if joint else None
    for j, unit in enumerate(units):
        act, d_before, bias_grad = outs[3 * j : 3 * j + 3]
        cols = act.shape[1]
        at = rows_at(unit, cols)
        weight_in, weight_out = hidden_w[:, at], return_w[at, :]
        bias = bias_row(vecs, unit, cols)
        bias_sum = jnp.zeros(bias_grad.shape, WIDE)
        for row in range(0, act.shape[0], ROWS):
            here = slice(row, row + ROWS)
            x = dot_nn(hidden_in[here, :], weight_in) + bias
            d_act = dot_nt(d_feed[here, :], weight_out)
            squared = x * x
            rise = 0.5 + 0.5 * jnp.tanh(x * (CURVE + CURVE * CUBIC * squared))
            out = x * rise
            slope = rise + out * (1.0 - rise) * (2 * CURVE + 6 * CURVE * CUBIC * squared)
            act[here, :] = low(out)
            d_x = d_act * slope
            d_before[here, :] = low(d_x)
            bias_sum = bias_sum + jnp.sum(d_x, axis=0, keepdims=True)
        bias_grad[...] = bias_sum
        width = hidden_in.shape[1]
        rows = slice(j * width, (j + 1) * width)
        grads_all[rows, :cols] = low(dot_nn(hidden_in_t[...], d_before[...]))
        grads_all[rows, cols:] = low(dot_nn(d_feed_t[...], act[...]))


def spans_of(units, cols):
    return [rows_at(unit, cols) for unit in units]


def middle_kernel(units_of, *refs):
    d_befores, (hidden_w, vecs, middle, cot, ends_in) = refs[:PARTS], refs[PARTS : PARTS + 5]
    d_middle, d_low, gain_grad, bias_grad = refs[PARTS + 5 :]
    end = ends_in[SLOTS - 1, 0]
    spans = spans_of(units_of(), d_befores[0].shape[1])
    gain = vecs[SECOND_GAIN : SECOND_GAIN + 1, :]
    gain_sum = jnp.zeros(gain_grad.shape, WIDE)
    bias_sum = jnp.zeros(bias_grad.shape, WIDE)
    for at in range(0, middle.shape[0], ROWS):
        here = slice(at, at + ROWS)
        d_hidden = 0.0
        for part, span in zip(d_befores, spans):
            d_hidden = d_hidden + dot_nt(part[here, :], hidden_w[:, span])
        valid = at + lax.broadcasted_iota(jnp.int32, (ROWS, 1), 0) < end
        unit, inv = norm_parts(middle[here, :])
        d_mid = wide(cot[here, :]) + norm_back(d_hidden, unit, inv, gain)
        d_middle[here, :] = d_mid
        d_low[here, :] = low(jnp.where(valid, d_mid, 0.0))
        gain_sum = gain_sum + jnp.sum(d_hidden * unit, axis=0, keepdims=True)
        bias_sum = bias_sum + jnp.sum(d_hidden, axis=0, keepdims=True)
    gain_grad[...] = gain_sum
    bias_grad[...] = bias_sum


def rows_out(near, far, sems, compute):
    blocks = near.shape[0] // ROWS

    def leaving(turn):
        here = rows_at(turn, ROWS)
        return pltpu.make_async_copy(near.at[here, :], far.at[here, :], sems.at[turn])

    @pl.loop(0, blocks)
    def _(turn):
        compute(rows_at(turn, ROWS), turn * ROWS)
        leaving(turn).start()

    for turn in range(blocks):
        leaving(turn).wait()


def layer_kernel(units_of, *refs):
    acts, (return_w, vecs, middle, ends_in) = refs[:PARTS], refs[PARTS : PARTS + 4]
    token, far, near, sems = refs[PARTS + 4 :]
    token[...] = jnp.zeros_like(token)
    end = ends_in[SLOTS - 1, 0]
    spans = spans_of(units_of(), acts[0].shape[1])

    def compute(here, at):
        feed = vecs[RETURN_BIAS : RETURN_BIAS + 1, :]
        for part, span in zip(acts, spans):
            feed = feed + dot_nn(part[here, :], return_w[span, :])
        valid = at + lax.broadcasted_iota(jnp.int32, (ROWS, 1), 0) < end
        near[here, :] = middle[here, :] + jnp.where(valid, feed, 0.0)

    rows_out(near, far, sems, compute)


def attention_back_kernel(
    d_low, exps, q_sel, attended, row_facts, placed, key_t, value_n, o_own, o_other, routes,
    d_stack, grad_o, spread, d_scores, d_queries,
):
    head = key_t.shape[0]
    tok, half = d_low.shape[0], o_own.shape[0]
    experts = 2 * half // head
    own = experts // 2
    scale = head**-0.5
    d_all = [dot_nt(o_own[...], d_low[...]), dot_nt(o_other[...], d_low[...])]
    hits = [expert_hits(routes[m : m + 1, :], experts) for m in range(2)]
    halves = [slice(m * tok, (m + 1) * tok) for m in range(2)]
    gates = [row_facts[0:1, lanes] for lanes in halves]
    subs = lax.broadcasted_iota(jnp.int32, (head, tok), 0)
    d_gates = []
    for m, lanes in enumerate(halves):
        d_raw = jnp.zeros((head, tok), WIDE)
        for e in range(experts):
            from_e = d_all[e // own][(e % own) * head : (e % own + 1) * head, :]
            d_raw = jnp.where(hits[m][e], from_e, d_raw)
        att = attended[:, lanes]
        d_gates.append(jnp.sum(d_raw * att, axis=0, keepdims=True))
        d_att = low(d_raw * (gates[m] * row_facts[1:2, lanes]))
        inner = jnp.sum(wide(d_att) * att, axis=0, keepdims=True)
        inner_high = wide(low(inner))
        tail = jnp.where(subs == 0, -inner_high, jnp.where(subs == 1, inner_high - inner, 0.0))
        spread[:head, lanes] = d_att
        spread[head:, lanes] = low(tail)
    mean_gate = gates[0] * d_gates[0] + gates[1] * d_gates[1]
    ids = lax.broadcasted_iota(jnp.int32, (experts, tok), 0)
    d_logits = sum(
        jnp.where(ids == routes[m : m + 1, :], gates[m] * (d_gates[m] - mean_gate), 0.0)
        for m in range(2)
    )
    high = wide(low(d_logits))
    d_stack[2 * half + 2 * head :, :] = low(jnp.concatenate([high, d_logits - high], axis=0))

    def d_probs_of(at):
        return dot_nn(value_n[...], spread[:, at : at + ROWS])

    d_probs = d_probs_of(0)
    for at in range(0, 2 * tok, ROWS):
        later = d_probs_of(at + ROWS) if at + ROWS < 2 * tok else None
        here = slice(at, at + ROWS)
        d_score = low(wide(exps[:, here]) * d_probs)
        d_scores[:, here] = d_score
        d_queries[:, here] = dot_nn(key_t[...], d_score) * scale
        d_probs = later
    d_values = dot_nt(exps[...], spread[:head, :])
    d_keys = dot_nt(d_scores[...], q_sel[...]) * scale
    d_stack[2 * half : 2 * half + head, :] = low(d_keys.T)
    d_stack[2 * half + head : 2 * half + 2 * head, :] = low(d_values.T)
    first, second = d_queries[:, halves[0]], d_queries[:, halves[1]]
    for e in range(experts):
        d_stack[e * head : (e + 1) * head, :] = low(
            jnp.where(hits[0][e], first, jnp.where(hits[1][e], second, 0.0))
        )
    grad_o[...] = dot_nn(placed[...], d_low[...])


def close_kernel(
    units_of, d_stack, grad_o, q_own, q_other, normed, vecs, return_bias_grad, second_gain_grad,
    second_bias_grad, key_w, value_w, router_w, *rest,
):
    bias_parts, (own_grads, other_grads, common) = rest[:PARTS], rest[PARTS:]
    half, head, experts = q_own.shape[0], key_w.shape[0], router_w.shape[0]
    owned = at_kv = 2 * half
    rows_in = normed[...]
    parts = ((0, half, q_own[...]), (half, at_kv, q_other[...]))
    tail_w = jnp.concatenate([key_w[...], value_w[...], router_w[...], router_w[...]], axis=0)
    parts = parts + ((at_kv, d_stack.shape[0], tail_w),)
    bias_sum, product_sum, grads = 0.0, 0.0, []
    for start, stop, weights in parts:
        stack = d_stack[start:stop, :]
        grad = dot_nn(stack, rows_in)
        grads.append(grad)
        row_sums = jnp.sum(wide(stack), axis=1, keepdims=True)
        bias_sum = bias_sum + jnp.sum(row_sums * wide(weights), axis=0, keepdims=True)
        product_sum = product_sum + jnp.sum(grad * wide(weights), axis=0, keepdims=True)
    gain = vecs[FIRST_GAIN : FIRST_GAIN + 1, :]
    gain_sum = (product_sum - vecs[FIRST_BIAS : FIRST_BIAS + 1, :] * bias_sum) / gain
    own_grads[:half, :] = low(grads[0])
    other_grads[:half, :] = low(grads[1])
    own_grads[half:owned, :] = low(grad_o[:half, :])
    other_grads[half:owned, :] = low(grad_o[half:, :])
    tail = grads[2]
    common[...] = jnp.zeros_like(common)
    common[: 2 * head, :] = tail[: 2 * head, :]
    row = 2 * head
    common[row : row + experts, :] = (
        tail[2 * head : 2 * head + experts, :] + tail[2 * head + experts :, :]
    )
    row = row + experts
    rows = (gain_sum, bias_sum, second_gain_grad[...], second_bias_grad[...], return_bias_grad[...])
    for j, values in enumerate(rows):
        common[row + j : row + j + 1, :] = values
    for unit, part in zip(units_of(), bias_parts):
        cols = part.shape[1]
        at = pl.ds(row + HIDDEN_BIAS + unit // 2, 1)
        there_now = common[at, :]
        doubled = jnp.concatenate([part[...], part[...]], axis=1)
        lanes = lax.broadcasted_iota(jnp.int32, doubled.shape, 1)
        common[at, :] = jnp.where(lanes // cols == unit % 2, doubled, there_now)
    own_grads[owned:, :] = low(common[...])
    other_grads[owned:, :] = low(common[...])


def input_kernel(
    d_stack, q_own, q_other, key_w, value_w, router_w, x, d_middle, vecs,
    token, far, near, sems,
):
    token[...] = jnp.zeros_like(token)
    half = q_own.shape[0]
    at_kv = 2 * half
    tail_w = jnp.concatenate([key_w[...], value_w[...], router_w[...], router_w[...]], axis=0)
    gain = vecs[FIRST_GAIN : FIRST_GAIN + 1, :]

    def compute(here, at):
        d_normed = dot_tn(d_stack[:half, here], q_own[...])
        d_normed = d_normed + dot_tn(d_stack[half:at_kv, here], q_other[...])
        d_normed = d_normed + dot_tn(d_stack[at_kv:, here], tail_w)
        unit, inv = norm_parts(wide(x[here, :]))
        near[here, :] = d_middle[here, :] + norm_back(d_normed, unit, inv, gain)

    rows_out(near, far, sems, compute)


def halvings(n_dp):
    return n_dp.bit_length() - 3


def step_orders(n_dp):
    first = list(range(halvings(n_dp)))
    second = []
    for at in range(0, len(first), 2):
        second += first[at : at + 2][::-1]
    return first, second


def pairs_of(n_dp, step):
    orders = step_orders(n_dp)
    return [
        (chip * 2 + core, (chip ^ (1 << orders[core][step])) * 2 + core)
        for chip in range(n_dp)
        for core in range(2)
    ]


def quad_pairs(n_dp, turn):
    return [
        (chip * 2 + core, (chip ^ (turn << halvings(n_dp))) * 2 + core)
        for chip in range(n_dp)
        for core in range(2)
    ]


def cross_pairs(n_dp, turn):
    low_bit = halvings(n_dp)
    return [
        (chip * 2 + core, (chip ^ (1 << (low_bit + turn))) * 2 + core)
        for chip in range(n_dp)
        for core in range(2)
    ]


def core_swap(values, n_dp):
    return lax.ppermute(values, AXES, [(at, at ^ 1) for at in range(2 * n_dp)])


def bit_here(n_dp, step, core=None):
    first, second = step_orders(n_dp)
    chip = lax.axis_index("dp")
    core = core_here() if core is None else core
    return jnp.where(core == 0, chip >> first[step], chip >> second[step]) & 1


def units_here(n_dp, entries):
    core = core_here()
    mine, theirs = bit_here(n_dp, 0), bit_here(n_dp, 0, 1 - core)
    other = 1 - core
    blocks = [2 * other + 1 - theirs, 2 * core + 1 - mine, 2 * other + theirs, 2 * core + mine]
    return [2 * blocks[entry // 2] + entry % 2 for entry in entries]


def rows_at(index, size):
    return pl.ds(pl.multiple_of(index * size, size), size)


def add_kernel(*refs):
    total = wide(refs[0][...])
    for ref in refs[1:-1]:
        total = total + wide(ref[...])
    refs[-1][...] = low(total)


def rows_of(ref, at, size):
    return wide(ref[pl.ds(pl.multiple_of(at, size), size), :])


def partial_sum(n_dp, terms, step, last_kept):
    start = step - len(terms) + 1
    size = terms[0][0].shape[0] >> (step - start + 1)
    at, total = 0, 0.0
    for j in range(step, start - 1, -1):
        bit = bit_here(n_dp, j)
        bit = bit if last_kept or j < step else 1 - bit
        at = at + bit * (size << (step - j))
        for ref in terms[j - start]:
            total = total + rows_of(ref, at, size)
    return total


def group(refs, counts):
    refs = list(refs)
    return [[refs.pop(0) for _ in range(count)] for count in counts]


def split_terms(terms, joint):
    parts = []
    for part in range(2):
        chosen = []
        for refs, flags in zip(terms, joint):
            chosen.append([])
            for ref, flag in zip(refs, flags):
                half = ref.shape[0] // 2
                if flag == 2:
                    chosen[-1].append(ref.at[pl.ds(part * half, half), :])
                elif flag == part:
                    chosen[-1].append(ref)
        parts.append(chosen)
    return parts


def send_kernel(n_dp, step, counts, joint, *refs):
    out = refs[-1]
    terms = group(refs[:-1], counts)
    if joint is None:
        out[...] = low(partial_sum(n_dp, terms, step, False))
        return
    size = out.shape[0] // 2
    for part, chosen in enumerate(split_terms(terms, joint)):
        out[part * size : (part + 1) * size, :] = low(partial_sum(n_dp, chosen, step, False))


def kept_kernel(n_dp, step, counts, *refs):
    *terms, last = group(refs[:-1], counts)
    refs[-1][...] = low(partial_sum(n_dp, terms, step, True) + wide(last[0][...]))


def spot_here(n_dp, turn):
    return jnp.bitwise_xor(lax.axis_index("dp") >> halvings(n_dp), turn)


def quarters_kernel(n_dp, step, counts, joint, *refs):
    count = sum(counts)
    terms = group(refs[:count], counts)
    outs, total = refs[count:-1], refs[-1]
    size = total.shape[0] // 2
    for part, (*chosen, last) in enumerate(split_terms(terms, joint)):
        total[part * size : (part + 1) * size, :] = partial_sum(
            n_dp, chosen, step, True
        ) + wide(last[0][...])
    cols = outs[0].shape[1]
    for turn, out in enumerate(outs):
        out[...] = low(total[:, rows_at(spot_here(n_dp, turn), cols)])


def row_of_four(n_dp, part, *refs):
    pieces, out = refs[:4], refs[4]
    size, cols = out.shape[0], pieces[0].shape[1]
    for turn, piece in enumerate(pieces):
        at = rows_at(spot_here(n_dp, turn), cols)
        out[:, at] = piece[part * size : (part + 1) * size, :]


def join_kernel(n_dp, step, mine, got, out):
    size = mine.shape[0]
    bit = bit_here(n_dp, step)
    out[rows_at(bit, size), :] = mine[...]
    out[rows_at(1 - bit, size), :] = got[...]


def pass_kernel(source, out):
    out[...] = source[...]


def stack_kernel(first, second, out):
    size = first.shape[0]
    out[:size, :] = first[...]
    out[size:, :] = second[...]


def place_kernel(units_of, count, more, *refs):
    hidden, returned, left, right, sems = refs[-5:]
    copies = []
    width = left.shape[1]
    parts = []
    for ref in refs[:count]:
        parts += [ref.at[pl.ds(row, width), :] for row in range(0, ref.shape[0], width)]
    for j, (unit, part) in enumerate(zip(units_of(), parts)):
        cols = part.shape[1] // 2
        at = rows_at(unit, cols)
        left[j] = wide(part[:, :cols])
        copies.append(pltpu.make_async_copy(left.at[j], hidden.at[:, at], sems.at[2 * j]))
        copies[-1].start()
        right[j] = wide(part[:, cols:]).T
        copies.append(pltpu.make_async_copy(right.at[j], returned.at[at, :], sems.at[2 * j + 1]))
        copies[-1].start()
    if more:
        refs[-6][...] = jnp.zeros_like(refs[-6])
    for copy in copies:
        copy.wait()


def finish_kernel(n_dp, mine, got, token, query_g, output_g, key_g, value_g, router_g, *refs):
    vectors, whole = refs[:-1], refs[-1]
    token[...] = jnp.zeros_like(token)
    size, width = mine.shape
    bit = bit_here(n_dp, 0)
    whole[rows_at(bit, size), :] = wide(mine[...])
    whole[rows_at(1 - bit, size), :] = wide(got[...])
    row = 0
    for out in (query_g, output_g, key_g, value_g, router_g):
        out[...] = whole[row : row + out.shape[0], :]
        row = row + out.shape[0]
    for j, vector in enumerate(vectors[:-1]):
        vector[...] = whole[row + j, :]
    row = row + len(vectors) - 1
    for j in range(vectors[-1].shape[0] // width):
        vectors[-1][j * width : (j + 1) * width] = whole[row + j, :]


def local(
    inputs, cotangent, lengths, routes, first_gain, first_bias, router_weight, key_weight,
    value_weight, query_weight, output_weight, second_gain, second_bias, hidden_weight,
    hidden_bias, return_weight, return_bias,
):
    tok, width = inputs.shape
    ff = hidden_weight.shape[1]
    n_dp = lax.axis_size("dp")
    own, _, head = query_weight.shape
    experts = 2 * own
    half = own * head
    blocks = tok // ROWS

    q_own = jnp.transpose(query_weight, (0, 2, 1)).reshape(half, width)
    o_own = output_weight.reshape(half, width)
    q_other, o_other = core_swap(q_own, n_dp), core_swap(o_own, n_dp)
    vec_rows = 5 + ff // width
    program = Program()
    call = program.call
    (
        normed, vecs, keys_ext, key_t, value_n, values_ext, logits, x, q_own, o_own, key_w, value_w,
        router_w, routes, ends,
    ) = call(
        open_kernel, "first_norm", [],
        [
            held((tok, width), LOW), held((vec_rows + -vec_rows % 8, width), WIDE),
            held((tok, 2 * head), LOW), held((head, tok), LOW), held((tok, 2 * head), LOW),
            held((head + 16, tok), LOW), held((experts, tok), WIDE), held((tok, width), LOW),
            held((half, width), LOW), held((half, width), LOW), held((head, width), LOW),
            held((head, width), LOW), held((experts, width), LOW), held((2, tok), jnp.int32),
            held((8, 128), jnp.int32),
        ],
        scratch=[pltpu.SMEM(lengths.shape[1:], jnp.int32)]
        + [pltpu.VMEM((width,), LOW)] * 5
        + [pltpu.VMEM((ff,), LOW), pltpu.SemaphoreType.DMA((blocks + 13,))],
        far=[
            inputs, lengths[0], first_gain, first_bias, key_weight.T, value_weight.T,
            router_weight.T, q_own, o_own, second_gain, second_bias, return_bias, hidden_bias,
            jnp.transpose(routes[0], (0, 2, 1)),
        ],
    )
    (
        exps, q_sel, attended, row_facts, placed, middle, hidden_in, hidden_in_t, d_feed, d_feed_t,
        return_bias_grad, cot, hidden_w, return_w,
    ) = call(
        forward_kernel, "attention_forward",
        [
            normed, x, vecs, q_own, q_other, o_own, o_other, keys_ext, values_ext, logits, routes,
            ends, key_t,
        ],
        [
            held((tok, 2 * tok), LOW), held((head, 2 * tok), LOW), held((head, 2 * tok), WIDE),
            held((8, 2 * tok), WIDE), held((2 * half, tok), LOW), held((tok, width), WIDE),
            held((tok, width), LOW), held((width, tok), LOW), held((tok, width), LOW),
            held((width, tok), LOW), held((1, width), WIDE), held((tok, width), LOW),
            held(hidden_weight.shape, LOW), held(return_weight.shape, LOW),
        ],
        scratch=[pltpu.VMEM((2 * head, 2 * tok), LOW), pltpu.SemaphoreType.DMA((3,))],
        far=[cotangent, hidden_weight, return_weight],
    )

    cols = ff // PARTS
    units = lambda *entries: functools.partial(units_here, n_dp, entries)
    steps = halvings(n_dp)

    def feed(*entries):
        outs = call(
            functools.partial(feed_kernel, units(*entries), True), f"feed_{entries[0]}",
            [hidden_in, hidden_in_t, d_feed, d_feed_t, vecs, hidden_w, return_w],
            [held((tok, cols), LOW), held((tok, cols), LOW), held((1, cols), WIDE)] * len(entries)
            + [there((len(entries) * width, 2 * cols), LOW)],
        )
        return list(zip(*[iter(outs[:-1])] * 3)), outs[-1]

    def add(name, *terms):
        return call(add_kernel, name, terms, there(terms[0].shape, LOW))

    parts_a, theirs = feed(0)
    swapped = core_swap(theirs, n_dp)
    parts_c, mine = feed(2)
    sent_a = lax.ppermute(add("feed_add_0", mine, swapped), AXES, pairs_of(n_dp, 0))
    parts_b, theirs = feed(1)
    swapped = core_swap(theirs, n_dp)
    parts_d, mine = feed(3)
    sent_b = lax.ppermute(add("feed_add_1", mine, swapped), AXES, pairs_of(n_dp, 0))
    parts_e, theirs = feed(4, 5)
    swapped = core_swap(theirs, n_dp)
    parts_f, mine = feed(6, 7)
    parts = parts_a + parts_b + parts_c + parts_d + parts_e + parts_f

    every = units(*range(PARTS))
    d_middle, d_low, second_gain_grad, second_bias_grad = call(
        functools.partial(middle_kernel, every), "second_norm_back",
        [p[1] for p in parts] + [hidden_w, vecs, middle, cot, ends],
        [
            held((tok, width), WIDE), held((tok, width), LOW), held((1, width), WIDE),
            held((1, width), WIDE),
        ],
    )

    feed_terms, feed_joint = [[sent_a, sent_b, swapped, mine]], [[0, 1, 2, 2]]

    def feed_send(step):
        counts = [len(t) for t in feed_terms]
        part = call(
            functools.partial(send_kernel, n_dp, step, counts, list(feed_joint)),
            f"feed_send_{step}", sum(feed_terms, []), there((2 * width >> step, 2 * cols), LOW),
        )
        feed_terms.append([lax.ppermute(part, AXES, pairs_of(n_dp, step))])
        feed_joint.append([2])

    for step in range(1, steps):
        feed_send(step)
    d_stack, grad_o = call(
        attention_back_kernel, "attention_backward",
        [d_low, exps, q_sel, attended, row_facts, placed, key_t, value_n, o_own, o_other, routes],
        [held((2 * half + 2 * head + 2 * experts, tok), LOW), held((2 * half, width), WIDE)],
        scratch=[
            pltpu.VMEM((2 * head, 2 * tok), LOW), pltpu.VMEM((tok, 2 * tok), LOW),
            pltpu.VMEM((head, 2 * tok), WIDE),
        ],
    )
    shared = 2 * head + experts + 5 + ff // width
    shared = shared + -(2 * half + shared) % (16 << steps)
    rows = 2 * half + shared
    own_grads, other_grads = call(
        functools.partial(close_kernel, every), "projection_grads",
        [
            d_stack, grad_o, q_own, q_other, normed, vecs, return_bias_grad, second_gain_grad,
            second_bias_grad, key_w, value_w, router_w, *[p[2] for p in parts],
        ],
        [there((rows, width), LOW), there((rows, width), LOW)],
        scratch=[pltpu.VMEM((shared, width), WIDE)],
    )

    def output(kernel, name, operands):
        _, out = call(
            kernel, name, operands, [held((8, 128), WIDE), there((tok, width), WIDE)],
            scratch=[pltpu.VMEM((tok, width), WIDE), pltpu.SemaphoreType.DMA((blocks,))],
            far_out=1,
        )
        return out

    rest_terms = [[own_grads, core_swap(other_grads, n_dp)]]
    counts = [len(t) for t in feed_terms]
    own_piece, *pieces = call(
        functools.partial(quarters_kernel, n_dp, steps - 1, counts, feed_joint), "feed_cut",
        sum(feed_terms, []), [there((2 * width >> (steps - 1), cols // 2), LOW)] * 4,
        scratch=[pltpu.VMEM((2 * width >> (steps - 1), 2 * cols), WIDE)],
    )

    def across(values):
        return [
            lax.ppermute(v, AXES, quad_pairs(n_dp, t + 1)) for t, v in enumerate(values)
        ]

    pieces = across(pieces)


    def rest_send(step):
        counts = [len(t) for t in rest_terms]
        part = call(
            functools.partial(send_kernel, n_dp, step, counts, None), f"rest_send_{step}",
            sum(rest_terms, []), there((rows >> (step + 1), width), LOW),
        )
        rest_terms.append([lax.ppermute(part, AXES, pairs_of(n_dp, step))])

    def join(name, step, mine, got):
        size, wide_cols = mine.shape
        kernel = functools.partial(join_kernel, n_dp, step)
        joined = call(kernel, name, [mine, got], there((2 * size, wide_cols), LOW))
        return joined, lax.ppermute(joined, AXES, pairs_of(n_dp, step - 1))

    written = None

    def place(name, entries, values, more=True):
        nonlocal written
        count = len(values)
        *_, one, two = call(
            functools.partial(place_kernel, units(*entries), count, more), name, values,
            [held((8, 128), WIDE)] * more + [there((width, ff), WIDE), there((ff, width), WIDE)],
            scratch=[
                pltpu.VMEM((len(entries), width, cols), WIDE),
                pltpu.VMEM((len(entries), cols, width), WIDE),
                pltpu.SemaphoreType.DMA((2 * len(entries),)),
            ],
            far=[] if written is None else written,
            far_out=2,
            aliases=[] if written is None else [(0, 0), (1, 1)],
        )
        written = [one, two]

    rest_send(0)
    layer_out = output(
        functools.partial(layer_kernel, every), "layer_out",
        [p[0] for p in parts] + [return_w, vecs, middle, ends],
    )
    for step in range(1, steps):
        rest_send(step)
    own_piece = add("feed_sum", own_piece, *pieces)
    pieces = across([own_piece] * 3)
    counts = [len(t) for t in rest_terms]
    rest = call(
        functools.partial(kept_kernel, n_dp, steps - 1, counts), "rest_sum", sum(rest_terms, []),
        there((rows >> steps, width), LOW),
    )
    rest_got = lax.ppermute(rest, AXES, cross_pairs(n_dp, 0))
    input_grad = output(
        input_kernel, "first_norm_back",
        [d_stack, q_own, q_other, key_w, value_w, router_w, x, d_middle, vecs],
    )
    size = own_piece.shape[0] // 2
    joined, got = [None] * 2, [None] * 2
    for part in range(2):
        joined[part] = call(
            functools.partial(row_of_four, n_dp, part), f"feed_row_{part}", [own_piece] + pieces,
            there((size, 2 * cols), LOW),
        )
        got[part] = lax.ppermute(joined[part], AXES, pairs_of(n_dp, steps - 1))
        if part == 0:
            rest = add("rest_add_0", rest, rest_got)
            rest_got = lax.ppermute(rest, AXES, cross_pairs(n_dp, 1))
    for step in reversed(range(1, steps)):
        for part in range(2):
            name = f"feed_join_{step}_{part}"
            joined[part], got[part] = join(name, step, joined[part], got[part])
            if step == 1:
                place(f"place_own_{part}", (6 + part,), [joined[part]])
                if part == 0:
                    rest = add("rest_add_1", rest, rest_got)
                    rest_got = lax.ppermute(rest, AXES, pairs_of(n_dp, steps - 1))
    both = call(stack_kernel, "feed_own", joined, there((2 * width, 2 * cols), LOW))
    other = core_swap(both, n_dp)
    far = []

    def place_got(part):
        row = call(pass_kernel, f"feed_got_{part}", [got[part]], there((width, 2 * cols), LOW))
        far.append(core_swap(row, n_dp))
        place(f"place_got_{part}", (2 + part,), [row])

    place_got(0)
    for step in reversed(range(1, steps)):
        rest, rest_got = join(f"rest_join_{step}", step, rest, rest_got)
    place("place_other", (4, 5), [other])
    place_got(1)
    place("place_far", (0, 1), far)
    vectors = [there((width,), WIDE)] * 5 + [there((ff,), WIDE)]
    _, query_grad, output_grad, key_g, value_g, router_g, fg, fb, sg, sb, rb, hb = call(
        functools.partial(finish_kernel, n_dp), "finish", [rest, rest_got],
        [held((8, 128), WIDE)] + [there((half, width), WIDE)] * 2 + [there((head, width), WIDE)] * 2
        + [there((experts, width), WIDE)] + vectors,
        scratch=[pltpu.VMEM((rows, width), WIDE)],
    )
    hidden_grad, return_grad = written
    return (
        layer_out,
        input_grad,
        fg,
        fb,
        router_g.T,
        key_g.T,
        value_g.T,
        jnp.transpose(query_grad.reshape(-1, head, width), (0, 2, 1)),
        output_grad.reshape(-1, head, width),
        sg,
        sb,
        hidden_grad,
        hb,
        return_grad,
        rb,
    )


def solution(mesh):
    rows = P(AXES, None)
    cut = P("expert", None, None)
    in_specs = (
        (rows, rows, P("dp", None, None), P("dp", None, None, None))
        + (P(),) * 5
        + (cut, cut)
        + (P(),) * 6
    )
    out_specs = (rows, rows) + (P(),) * 5 + (cut, cut) + (P(),) * 6
    return jax.shard_map(local, mesh=mesh, in_specs=in_specs, out_specs=out_specs, check_vma=False)
```
